32 devices in a mesh: dp: 4 (over y, x), fsdp: 8 (over z, core).
Axes of the slice: x: 2, y: 2, z: 4, core: 2. Of those that a mesh axis runs over, the one named last changes fastest.
Arguments:
- images: bfloat16 [768, 197, 384], P(('dp', 'fsdp')), may hold values from -6 to 6
- cotangent: bfloat16 [768, 197, 384], P(('dp', 'fsdp')), may hold values from -6 to 6
- counts: int32 [32], P(('dp', 'fsdp')), may hold values from 1 to 24, as said below
- w_qkv: float32 [384, 1152], P('fsdp'), may hold values from -0.3125 to 0.3125
- w_proj: float32 [384, 384], P('fsdp'), may hold values from -1.25 to 1.25
- w_fc1: float32 [384, 1152], P('fsdp'), may hold values from -0.3125 to 0.3125
- w_fc2: float32 [1152, 384], P(None, 'fsdp'), may hold values from -0.1875 to 0.1875
- b_fc1: float32 [1152], P('fsdp'), may hold values from -3 to 3
- vectors: float32 [6, 384], P(None, 'fsdp'), may hold values from 0.1 to 1.9
- m_qkv: float32 [384, 1152], P('fsdp'), may hold values from -0.125 to 0.125
- m_proj: float32 [384, 384], P('fsdp'), may hold values from -0.125 to 0.125
- m_fc1: float32 [384, 1152], P('fsdp'), may hold values from -0.125 to 0.125
- m_fc2: float32 [1152, 384], P(None, 'fsdp'), may hold values from -0.125 to 0.125
- m_bias1: float32 [1152], P('fsdp'), may hold values from -0.125 to 0.125
- m_vectors: float32 [6, 384], P(None, 'fsdp'), may hold values from -0.125 to 0.125
- v_qkv: float32 [384, 1152], P('fsdp'), may hold values from 1e-05 to 0.001
- v_proj: float32 [384, 384], P('fsdp'), may hold values from 1e-05 to 0.001
- v_fc1: float32 [384, 1152], P('fsdp'), may hold values from 1e-05 to 0.001
- v_fc2: float32 [1152, 384], P(None, 'fsdp'), may hold values from 1e-05 to 0.001
- v_bias1: float32 [1152], P('fsdp'), may hold values from 1e-05 to 0.001
- v_vectors: float32 [6, 384], P(None, 'fsdp'), may hold values from 1e-05 to 0.001
- decay_flags: int32 [6], replicated, may hold values from 0 to 1
- group_ids: int32 [6], replicated, may hold values from 0 to 2
- group_scales: float32 [3], replicated, may hold values from 0.5 to 4
Outputs:
- out_block: bfloat16 [768, 197, 384], P(('dp', 'fsdp'))
- grad_input: bfloat16 [768, 197, 384], P(('dp', 'fsdp'))
- g_qkv: float32 [384, 1152], P('fsdp')
- g_proj: float32 [384, 384], P('fsdp')
- g_fc1: float32 [384, 1152], P('fsdp')
- g_fc2: float32 [1152, 384], P(None, 'fsdp')
- g_bias1: float32 [1152], P('fsdp')
- g_vectors: float32 [6, 384], P(None, 'fsdp')
- new_qkv: float32 [384, 1152], P('fsdp')
- new_proj: float32 [384, 384], P('fsdp')
- new_fc1: float32 [384, 1152], P('fsdp')
- new_fc2: float32 [1152, 384], P(None, 'fsdp')
- new_bias1: float32 [1152], P('fsdp')
- new_vectors: float32 [6, 384], P(None, 'fsdp')
- first_qkv: float32 [384, 1152], P('fsdp')
- first_proj: float32 [384, 384], P('fsdp')
- first_fc1: float32 [384, 1152], P('fsdp')
- first_fc2: float32 [1152, 384], P(None, 'fsdp')
- first_bias1: float32 [1152], P('fsdp')
- first_vectors: float32 [6, 384], P(None, 'fsdp')
- second_qkv: float32 [384, 1152], P('fsdp')
- second_proj: float32 [384, 384], P('fsdp')
- second_fc1: float32 [384, 1152], P('fsdp')
- second_fc2: float32 [1152, 384], P(None, 'fsdp')
- second_bias1: float32 [1152], P('fsdp')
- second_vectors: float32 [6, 384], P(None, 'fsdp')
The draws below stay inside these ranges and needn't reach their ends.
Inputs may be any that keep to these rules, and one draw needn't show every extreme that they name: `counts`: number of real images among a device's 24 slots, the first ones; some device has all slots real.
All inputs are finite; a program needn't handle non-finite values.
Results may differ from the reference program's by a relative error of at most 0.022.
The reference program's roundings to bfloat16 on the way count: a program that leaves them out, or rounds other values in their place, can miss the bound.
Values may be sent and summed in bfloat16 or wider, within the bound.
No kernel may reach another device: no remote copies, remote signals or barrier semaphores. Data moves between devices by JAX's collectives and lax.ppermute only.
A program may use at most 256 MiB of HBM per device.

```python
import math
import jax
import jax.numpy as jnp
from jax import lax

D = 384
HEADS = 6
HEAD_DIM = 64
FF = 1152
SEQ = 197
IMG_DEV = 24
GROUPS = 3
IMAGES = 768
N_DP = 4
N_FSDP = 8


def draw_counts(key, part):
    device_total = N_DP * N_FSDP
    lowest = max(IMG_DEV // 4, 1)
    base = jax.random.randint(key, (device_total,), lowest, IMG_DEV + 1, dtype=jnp.int32)
    chosen = jax.random.randint(jax.random.fold_in(key, 7), (), 0, device_total, dtype=jnp.int32)
    return base.at[chosen].set(IMG_DEV)


def touch_ends(values, rng, smallest, high):
    shape = values.shape
    spot = [jax.random.randint(jax.random.fold_in(rng, axis), (), 0, shape[axis]) for axis in range(len(shape))]
    values = values.at[tuple(spot)].set(smallest)
    longest = shape.index(max(shape))
    spot[longest] = (spot[longest] + 1) % shape[longest]
    return values.at[tuple(spot)].set(high)


def block_scale(key, shape, pieces, least, largest):
    level, own = 1.0, jax.random.fold_in(key, 6)
    for axis_at, shards_of in pieces:
        heights = jnp.exp(jax.random.uniform(jax.random.fold_in(own, axis_at), (shards_of,), jnp.float32, least / len(pieces), largest / len(pieces)))
        level = level * jnp.repeat(heights, shape[axis_at] // shards_of).reshape([-1 if axis == axis_at else 1 for axis in range(len(shape))])
    return level


def normal_values(key, dims, width, most, pieces=(), kind=jnp.bfloat16):
    array = jax.random.normal(key, dims, jnp.float32) * width
    if len(pieces) > 0:
        array = block_scale(key, dims, pieces, -0.22, 0.18) * array
    return jnp.clip(array, min=-most, max=most).astype(kind)


def setup_inputs(seed: int = 0) -> dict:
    splits = jax.random.split(jax.random.key(seed), 25)
    images = normal_values(splits[0], (IMAGES, SEQ, D), 1.0, 6.0, ((0, 32),))
    cotangent = normal_values(splits[1], (IMAGES, SEQ, D), 1.0, 6.0, ((0, 32),))
    counts = draw_counts(jax.random.fold_in(splits[24], 71), 0)
    w_qkv = normal_values(splits[3], (D, 3 * D), D ** -0.5, 0.3125, ((0, 8),), jnp.float32)
    w_proj = normal_values(splits[4], (D, D), (D // 14) ** -0.5, 1.25, ((0, 8),), jnp.float32)
    w_fc1 = normal_values(splits[5], (D, FF), D ** -0.5, 0.3125, ((0, 8),), jnp.float32)
    w_fc2 = normal_values(splits[6], (FF, D), FF ** -0.5, 0.1875, ((1, 8),), jnp.float32)
    b_fc1 = normal_values(splits[7], (FF,), 0.5, 3.0, ((0, 8),), jnp.float32)
    vectors = jnp.clip(1.0 + 0.18 * jax.random.normal(splits[8], (6, D), jnp.float32), 0.1, 1.9)
    m_qkv = normal_values(splits[9], (D, 3 * D), 0.02, 0.125, ((0, 8),), jnp.float32)
    m_proj = normal_values(splits[10], (D, D), 0.02, 0.125, ((0, 8),), jnp.float32)
    m_fc1 = normal_values(splits[11], (D, FF), 0.02, 0.125, ((0, 8),), jnp.float32)
    m_fc2 = normal_values(splits[12], (FF, D), 0.02, 0.125, ((1, 8),), jnp.float32)
    m_bias1 = normal_values(splits[13], (FF,), 0.02, 0.125, ((0, 8),), jnp.float32)
    m_vectors = normal_values(splits[14], (6, D), 0.02, 0.125, ((1, 8),), jnp.float32)
    v_qkv = jnp.clip(jnp.exp(math.log(0.001) - 4.6051703 * jax.random.uniform(splits[15], (D, 3 * D), jnp.float32) ** block_scale(splits[15], (D, 3 * D), ((0, 8),), -0.2, 0.2)), 9.999999747378752e-06, 0.001)
    v_proj = jnp.clip(jnp.exp(math.log(0.001) - 4.6051703 * jax.random.uniform(splits[16], (D, D), jnp.float32) ** block_scale(splits[16], (D, D), ((0, 8),), -0.2, 0.2)), 9.999999747378752e-06, 0.001)
    v_fc1 = jnp.clip(jnp.exp(math.log(0.001) - 4.6051703 * jax.random.uniform(splits[17], (D, FF), jnp.float32) ** block_scale(splits[17], (D, FF), ((0, 8),), -0.2, 0.2)), 9.999999747378752e-06, 0.001)
    v_fc2 = jnp.clip(jnp.exp(math.log(0.001) - 4.6051703 * jax.random.uniform(splits[18], (FF, D), jnp.float32) ** block_scale(splits[18], (FF, D), ((1, 8),), -0.2, 0.2)), 9.999999747378752e-06, 0.001)
    v_bias1 = jnp.clip(jnp.exp(math.log(0.001) - 4.6051703 * jax.random.uniform(splits[19], (FF,), jnp.float32) ** block_scale(splits[19], (FF,), ((0, 8),), -0.2, 0.2)), 9.999999747378752e-06, 0.001)
    v_vectors = jnp.clip(jnp.exp(math.log(0.001) - 4.6051703 * jax.random.uniform(splits[20], (6, D), jnp.float32) ** block_scale(splits[20], (6, D), ((1, 8),), -0.2, 0.2)), 9.999999747378752e-06, 0.001)
    decay_flags = touch_ends(jax.random.randint(splits[21], (6,), 0, 2), jax.random.fold_in(splits[21], 1), 0, 1).astype(jnp.int32)
    group_ids = touch_ends(jax.random.randint(splits[22], (6,), 0, GROUPS), jax.random.fold_in(splits[22], 1), 0, GROUPS - 1).astype(jnp.int32)
    group_scales = jnp.clip(jnp.exp(jax.random.uniform(splits[23], (GROUPS,), jnp.float32, math.log(0.5), math.log(4.0))), 0.5, 4.0)
    return {"images": images, "cotangent": cotangent, "counts": counts, "w_qkv": w_qkv, "w_proj": w_proj, "w_fc1": w_fc1, "w_fc2": w_fc2, "b_fc1": b_fc1, "vectors": vectors, "m_qkv": m_qkv, "m_proj": m_proj, "m_fc1": m_fc1, "m_fc2": m_fc2, "m_bias1": m_bias1, "m_vectors": m_vectors, "v_qkv": v_qkv, "v_proj": v_proj, "v_fc1": v_fc1, "v_fc2": v_fc2, "v_bias1": v_bias1, "v_vectors": v_vectors, "decay_flags": decay_flags, "group_ids": group_ids, "group_scales": group_scales}


@jax.custom_vjp
def low(v):
    return lax.optimization_barrier(v.astype(jnp.bfloat16)).astype(jnp.float32)

@jax.custom_vjp
def low_back(v):
    return v

def low_keep(v):
    return (low(v), None)

def low_pass(kept, grad):
    return (grad,)

def back_keep(v):
    return (v, None)

def back_low(kept, grad):
    return (low(grad),)
low.defvjp(low_keep, low_pass)
low_back.defvjp(back_keep, back_low)
HIGH = lax.Precision.HIGHEST
EPS_LN = 1e-06
LEARN_RATE = 0.2
BETA_ONE = 0.9
BETA_TWO = 0.999
ADAM_EPS = 1e-08
DECAY_RATE = 0.5
adam_steps = 10.0

def matmul(left, right):
    return jnp.dot(left, right, precision=HIGH)

def norm_affine(inputs, gain, shift):
    centre = inputs - lax.optimization_barrier(jnp.mean(inputs, axis=-1, keepdims=True))
    spread = lax.optimization_barrier(jnp.mean(centre * centre, axis=-1, keepdims=True))
    return centre * lax.rsqrt(spread + EPS_LN) * gain + shift

def forward(images_f, params, valid):
    rounded = [low(param) for param in params]
    qkv_weight, proj_weight, fc1_weight, fc2_weight, fc1_bias, vector_rows = rounded
    count_img, seq_len, model_width = images_f.shape
    total_rows = count_img * seq_len
    tokens_f = images_f.reshape(total_rows, model_width)
    normed_a = low(norm_affine(tokens_f, vector_rows[0], vector_rows[1]))
    packed = low_back(low(matmul(normed_a, qkv_weight)))
    packed = packed.reshape(count_img, seq_len, 3, HEADS, HEAD_DIM)
    queries = packed[:, :, 0]
    keys_in = packed[:, :, 1]
    values_in = packed[:, :, 2]
    scores = HEAD_DIM ** (-0.5) * low_back(jnp.einsum('bqhd,bkhd->bhqk', queries, keys_in, precision=HIGH))
    probs = jax.nn.softmax(scores, axis=-1)
    mixed = jnp.einsum('bhqk,bkhd->bqhd', low(probs), values_in, precision=HIGH)
    mixed = low_back(low(mixed.reshape(total_rows, model_width)))
    middle = tokens_f + low_back(matmul(mixed, proj_weight)) + vector_rows[2]
    normed_b = low(norm_affine(middle, vector_rows[3], vector_rows[4]))
    hidden = low_back(matmul(normed_b, fc1_weight)) + fc1_bias
    active = low(jax.nn.gelu(hidden, approximate=False))
    output = middle + low_back(matmul(active, fc2_weight)) + vector_rows[5]
    return output.reshape(images_f.shape) * valid

def adam_update(weight, grad, first, second, flag, lr_scale):
    first_new = BETA_ONE * first + (1.0 - BETA_ONE) * grad
    second_new = BETA_TWO * second + (1.0 - BETA_TWO) * grad * grad
    corr_one = 1.0 - BETA_ONE ** adam_steps
    corr_two = 1.0 - BETA_TWO ** adam_steps
    direction = first_new / corr_one / (jnp.sqrt(second_new / corr_two) + ADAM_EPS)
    weight_new = weight - LEARN_RATE * lr_scale * (direction + DECAY_RATE * flag * weight)
    return (weight_new, first_new, second_new)

def reference(images, cotangent, counts, w_qkv, w_proj, w_fc1, w_fc2, b_fc1, vectors, m_qkv, m_proj, m_fc1, m_fc2, m_bias1, m_vectors, v_qkv, v_proj, v_fc1, v_fc2, v_bias1, v_vectors, decay_flags, group_ids, group_scales):
    device_total = N_DP * N_FSDP
    images_f = images.astype(jnp.float32).reshape(device_total, IMG_DEV, SEQ, D)
    cot_f = cotangent.astype(jnp.float32).reshape(device_total, IMG_DEV, SEQ, D)
    params = (w_qkv, w_proj, w_fc1, w_fc2, b_fc1, vectors)

    def per_group(carry, inputs):
        image_grp, cot_grp, count_here = inputs
        valid = (jnp.arange(IMG_DEV, dtype=jnp.int32) < count_here).astype(images_f.dtype)[:, None, None]

        def closed(image_in, param_in):
            return forward(image_in, param_in, valid)
        result, pull = jax.vjp(closed, image_grp, params)
        grad_in, grad_par = pull(cot_grp)
        carry = tuple((total + part for total, part in zip(carry, grad_par)))
        return (carry, (result.astype(jnp.bfloat16), grad_in.astype(jnp.bfloat16)))
    start = tuple((jnp.zeros_like(param) for param in params))
    sums, (out_all, grad_all) = lax.scan(per_group, start, (images_f, cot_f, counts))
    grads = tuple((total / IMAGES for total in sums))
    firsts = (m_qkv, m_proj, m_fc1, m_fc2, m_bias1, m_vectors)
    seconds = (v_qkv, v_proj, v_fc1, v_fc2, v_bias1, v_vectors)
    new_w, new_m, new_v = ([], [], [])
    for place in range(6):
        flag = decay_flags[place].astype(group_scales.dtype)
        lr_scale = jnp.sum(jnp.where(jnp.arange(GROUPS, dtype=jnp.int32) == group_ids[place], group_scales, 0.0))
        weight_n, first_n, second_n = adam_update(params[place], grads[place], firsts[place], seconds[place], flag, lr_scale)
        new_w.append(weight_n)
        new_m.append(first_n)
        new_v.append(second_n)
    out_block = out_all.reshape(IMAGES, SEQ, D)
    grad_input = grad_all.reshape(IMAGES, SEQ, D)
    return (out_block, grad_input, grads[0], grads[1], grads[2], grads[3], grads[4], grads[5], new_w[0], new_w[1], new_w[2], new_w[3], new_w[4], new_w[5], new_m[0], new_m[1], new_m[2], new_m[3], new_m[4], new_m[5], new_v[0], new_v[1], new_v[2], new_v[3], new_v[4], new_v[5])
```

```python
import functools
import math

import jax
import jax.numpy as jnp
from jax import lax
from jax.experimental import pallas as pl
from jax.experimental.pallas import tpu as pltpu
from jax.sharding import PartitionSpec as P

BF=jnp.bfloat16; F32=jnp.float32
EPS=1e-6
HD=64
def rup(n,m): return (n+m-1)//m*m
def dot(a,b,ca=1,cb=0):
    return lax.dot_general(a,b,(((ca,),(cb,)),((),())),preferred_element_type=F32)
def ln_hat(x):
    c=x-jnp.mean(x,axis=-1,keepdims=True)
    r=lax.rsqrt(jnp.mean(c*c,axis=-1,keepdims=True)+EPS)
    return c*r,r
VM=pltpu.CompilerParams(vmem_limit_bytes=56<<20)

def k1_body(SEQ,SP,D,IB,x_ref,w_ref,vec_ref,qkv_ref,o_ref,l_ref,a_scr):
    H=D//HD
    @pl.when(pl.program_id(0)==0)
    def _():
        a_scr[...]=jnp.zeros_like(a_scr)
    g=vec_ref[0:1,:]; e=vec_ref[1:2,:]
    for i in range(IB):
        x=x_ref[i].astype(F32)
        xh,_=ln_hat(x)
        a_scr[i*SP:i*SP+SEQ,:]=(xh*g+e).astype(BF)
    for t in range(3):
        y=dot(a_scr[...],w_ref[:,t*D:(t+1)*D])
        if t==0: y=y*(HD**-0.5)
        qkv_ref[:,:,t*D:(t+1)*D]=y.astype(BF).reshape(IB,SP,D)
    for i in range(IB):
        for h in range(0,H,2):
            outs=[]
            for j in range(2):
                lo=(h+j)*HD
                q=qkv_ref[i,:,lo:lo+HD]
                k=qkv_ref[i,0:SEQ,D+lo:D+lo+HD]
                v=qkv_ref[i,0:SEQ,2*D+lo:2*D+lo+HD]
                s=dot(k,q,1,1)
                m=jnp.max(s,axis=0,keepdims=True)
                p=jnp.exp(s-m)
                l=jnp.sum(p,axis=0,keepdims=True)
                l_ref[i,h+j:h+j+1,:]=m+jnp.log(l)
                pb=(p*(1.0/l)).astype(BF)
                outs.append(dot(pb,v,0,0))
            o_ref[i,:,h*HD:(h+2)*HD]=jnp.concatenate(outs,axis=1).astype(BF)

def k1(images,w,vec,IB=2):
    N,SEQ,D=images.shape; SP=rup(SEQ,16); W3=w.shape[1]; H=D//HD
    return pl.pallas_call(functools.partial(k1_body,SEQ,SP,D,IB),grid=(N//IB,),
      in_specs=[pl.BlockSpec((IB,SEQ,D),lambda i:(i,0,0)),pl.BlockSpec(w.shape,lambda i:(0,0)),pl.BlockSpec(vec.shape,lambda i:(0,0))],
      out_specs=[pl.BlockSpec((IB,SP,W3),lambda i:(i,0,0)),pl.BlockSpec((IB,SP,D),lambda i:(i,0,0)),pl.BlockSpec((IB,8,SP),lambda i:(i,0,0))],
      out_shape=[jax.ShapeDtypeStruct((N,SP,W3),BF),jax.ShapeDtypeStruct((N,SP,D),BF),jax.ShapeDtypeStruct((N,8,SP),F32)],
      scratch_shapes=[pltpu.VMEM((IB*SP,D),BF)],compiler_params=VM,name="k1")(images,w,vec)

RS2=math.sqrt(0.5)
def gelu_pair(u):
    a=jnp.abs(u)
    t=1.0/(1.0+(0.3275911*RS2)*a)
    e=jnp.exp(-0.5*(u*u))
    q=t*(0.127414796+t*(-0.142248368+t*(0.7107068705+t*(-0.7265760135+t*0.5307027145))))*e
    phi=jnp.where(u>=0,1.0-q,q)
    return u*phi, phi+u*e*0.3989422804014327

def k2_body(SEQ,SP,D,FF,IB,cnt_ref,x_ref,o_ref,cot_ref,wp_ref,w1_ref,w2t_ref,c1_ref,vec_ref,
            out_ref,dx1_ref,do_ref,tp_ref,t1_ref,t2_ref,tc1_ref,tv_ref,
            b_scr,dy_scr,x1_scr,xh_scr,r_scr,g_scr,du_scr,dx_scr):
    s=pl.program_id(0)
    @pl.when(s==0)
    def _():
        dy_scr[...]=jnp.zeros_like(dy_scr)
        x1_scr[...]=jnp.zeros_like(x1_scr)
        for r in (tp_ref,t1_ref,t2_ref,tc1_ref,tv_ref): r[...]=jnp.zeros_like(r)
    cp=vec_ref[2:3,:]; g2=vec_ref[3:4,:]; e2=vec_ref[4:5,:]; c2=vec_ref[5:6,:]
    R=IB*SP
    for i in range(IB):
        x1_scr[i*SP:i*SP+SEQ,:]=x_ref[i].astype(F32)
        val=(s*IB+i<cnt_ref[0])
        dy_scr[i*SP:i*SP+SEQ,:]=jnp.where(val,cot_ref[i],jnp.zeros((),BF))
    ob=o_ref[...].reshape(R,D)
    x1=x1_scr[...]+dot(ob,wp_ref[...])+cp
    x1_scr[...]=x1
    xh,r=ln_hat(x1)
    xh_scr[...]=xh
    b_scr[...]=(xh*g2+e2).astype(BF)
    r_scr[...]=jnp.broadcast_to(r,(R,128))
    C=D
    for c in range(FF//C):
        sl=slice(c*C,(c+1)*C)
        u=dot(b_scr[...],w1_ref[:,sl])+c1_ref[0:1,sl]
        ga,dg=gelu_pair(u)
        g_scr[:,sl]=ga.astype(BF)
        du=dot(dy_scr[...],w2t_ref[:,sl])*dg
        du_scr[:,sl]=du.astype(BF)
        tc1_ref[0:1,sl]+=jnp.sum(du,axis=0,keepdims=True)
    y=x1_scr[...]+dot(g_scr[...],w2t_ref[...],1,1)+c2
    for i in range(IB):
        val=(s*IB+i<cnt_ref[0])
        out_ref[i]=jnp.where(val,y[i*SP:i*SP+SEQ],0.0).astype(BF)
    db=dot(du_scr[...],w1_ref[...],1,1)
    xh=xh_scr[...]
    dyf=dy_scr[...].astype(F32)
    dxh=db*g2
    m1=jnp.mean(dxh,axis=-1,keepdims=True)
    m2=jnp.mean(dxh*xh,axis=-1,keepdims=True)
    dx=dyf+r_scr[:,0:1]*(dxh-m1-xh*m2)
    tv_ref[3:4,:]+=jnp.sum(db*xh,axis=0,keepdims=True)
    tv_ref[4:5,:]+=jnp.sum(db,axis=0,keepdims=True)
    tv_ref[5:6,:]+=jnp.sum(dyf,axis=0,keepdims=True)
    tv_ref[2:3,:]+=jnp.sum(dx,axis=0,keepdims=True)
    dx1_ref[...]=dx.reshape(IB,SP,D)
    dx_scr[...]=dx.astype(BF)
    do_ref[...]=dot(dx_scr[...],wp_ref[...],1,1).astype(BF).reshape(IB,SP,D)
    tp_ref[...]+=dot(ob,dx_scr[...],0,0)
    t1_ref[...]+=dot(b_scr[...],du_scr[...],0,0)
    t2_ref[...]+=dot(dy_scr[...],g_scr[...],0,0)

def k2(cnt,images,o,cot,wp,w1,w2t,c1,vec,IB=2):
    N,SEQ,D=images.shape; SP=o.shape[1]; FF=w1.shape[1]
    full=lambda a:pl.BlockSpec(a.shape,lambda i,*_:(0,0))
    blk=lambda r,d:pl.BlockSpec((IB,r,d),lambda i,*_:(i,0,0))
    fo=lambda r,c:pl.BlockSpec((r,c),lambda i,*_:(0,0))
    R=IB*SP
    return pl.pallas_call(functools.partial(k2_body,SEQ,SP,D,FF,IB),
      grid_spec=pltpu.PrefetchScalarGridSpec(num_scalar_prefetch=1,grid=(N//IB,),
      in_specs=[blk(SEQ,D),blk(SP,D),blk(SEQ,D),full(wp),full(w1),full(w2t),full(c1),full(vec)],
      out_specs=[blk(SEQ,D),blk(SP,D),blk(SP,D),fo(D,D),fo(D,FF),fo(D,FF),fo(8,FF),fo(8,D)],
      scratch_shapes=[pltpu.VMEM((R,D),BF),pltpu.VMEM((R,D),BF),pltpu.VMEM((R,D),F32),pltpu.VMEM((R,D),F32),pltpu.VMEM((R,128),F32),
         pltpu.VMEM((R,FF),BF),pltpu.VMEM((R,FF),BF),pltpu.VMEM((R,D),BF)]),
      out_shape=[jax.ShapeDtypeStruct((N,SEQ,D),BF),jax.ShapeDtypeStruct((N,SP,D),F32),jax.ShapeDtypeStruct((N,SP,D),BF),
        jax.ShapeDtypeStruct((D,D),F32),jax.ShapeDtypeStruct((D,FF),F32),jax.ShapeDtypeStruct((D,FF),F32),jax.ShapeDtypeStruct((8,FF),F32),jax.ShapeDtypeStruct((8,D),F32)],
      compiler_params=VM,name="k2")(cnt,images,o,cot,wp,w1,w2t,c1,vec)

def k3_body(SEQ,SP,D,IB,x_ref,qkv_ref,l_ref,do_ref,dx1_ref,w_ref,vec_ref,gi_ref,tq_ref,tv_ref,a_scr,d_scr):
    H=D//HD
    @pl.when(pl.program_id(0)==0)
    def _():
        a_scr[...]=jnp.zeros_like(a_scr); d_scr[...]=jnp.zeros_like(d_scr)
        tq_ref[...]=jnp.zeros_like(tq_ref); tv_ref[...]=jnp.zeros_like(tv_ref)
    g=vec_ref[0:1,:]; e=vec_ref[1:2,:]
    for i in range(IB):
        xh,_=ln_hat(x_ref[i].astype(F32))
        a_scr[i*SP:i*SP+SEQ,:]=(xh*g+e).astype(BF)
    for i in range(IB):
        for h in range(0,H,2):
            dq,dk,dv=[],[],[]
            for j in range(2):
                lo=(h+j)*HD
                q=qkv_ref[i,:,lo:lo+HD]
                k=qkv_ref[i,0:SEQ,D+lo:D+lo+HD]
                v=qkv_ref[i,0:SEQ,2*D+lo:2*D+lo+HD]
                do=do_ref[i,:,lo:lo+HD]
                p=jnp.exp(dot(k,q,1,1)-l_ref[i,h+j:h+j+1,:])
                dp=dot(v,do,1,1)
                t=p*dp
                inner=jnp.sum(t,axis=0,keepdims=True)
                ds=(t-p*inner).astype(BF)
                pb=p.astype(BF)
                dv.append(dot(pb,do)); dk.append(dot(ds,q)); dq.append(dot(ds,k,0,0))
            r0=i*SP
            d_scr[r0:r0+SP,h*HD:(h+2)*HD]=(jnp.concatenate(dq,axis=1)*(HD**-0.5)).astype(BF)
            d_scr[r0:r0+SEQ,D+h*HD:D+(h+2)*HD]=jnp.concatenate(dk,axis=1).astype(BF)
            d_scr[r0:r0+SEQ,2*D+h*HD:2*D+(h+2)*HD]=jnp.concatenate(dv,axis=1).astype(BF)
    da=dot(d_scr[...],w_ref[...],1,1)
    tq_ref[...]+=dot(a_scr[...],d_scr[...],0,0)
    for i in range(IB):
        xh,r=ln_hat(x_ref[i].astype(F32))
        d=da[i*SP:i*SP+SEQ]
        dxh=d*g
        m1=jnp.mean(dxh,axis=-1,keepdims=True)
        m2=jnp.mean(dxh*xh,axis=-1,keepdims=True)
        gi_ref[i]=(dx1_ref[i,0:SEQ,:]+r*(dxh-m1-xh*m2)).astype(BF)
        tv_ref[0:1,:]+=jnp.sum(d*xh,axis=0,keepdims=True)
        tv_ref[1:2,:]+=jnp.sum(d,axis=0,keepdims=True)

def k3(images,qkv,l,do,dx1,w,vec,IB=2):
    N,SEQ,D=images.shape; SP=do.shape[1]; W3=w.shape[1]
    full=lambda a:pl.BlockSpec(a.shape,lambda i,*_:(0,0))
    blk=lambda r,d:pl.BlockSpec((IB,r,d),lambda i,*_:(i,0,0))
    fo=lambda r,c:pl.BlockSpec((r,c),lambda i,*_:(0,0))
    return pl.pallas_call(functools.partial(k3_body,SEQ,SP,D,IB),grid=(N//IB,),
      in_specs=[blk(SEQ,D),blk(SP,W3),blk(8,SP),blk(SP,D),blk(SP,D),full(w),full(vec)],
      out_specs=[blk(SEQ,D),fo(D,W3),fo(8,D)],
      out_shape=[jax.ShapeDtypeStruct((N,SEQ,D),BF),jax.ShapeDtypeStruct((D,W3),F32),jax.ShapeDtypeStruct((8,D),F32)],
      scratch_shapes=[pltpu.VMEM((IB*SP,D),BF),pltpu.VMEM((IB*SP,W3),BF)],compiler_params=VM,name="k3")(images,qkv,l,do,dx1,w,vec)


LEARN_RATE = 0.2
BETA_ONE = 0.9
BETA_TWO = 0.999
ADAM_EPS = 1e-08
DECAY_RATE = 0.5
adam_steps = 10.0


def adam_update(weight, grad, first, second, flag, lr_scale):
    first_new = BETA_ONE * first + (1.0 - BETA_ONE) * grad
    second_new = BETA_TWO * second + (1.0 - BETA_TWO) * grad * grad
    corr_one = 1.0 - BETA_ONE**adam_steps
    corr_two = 1.0 - BETA_TWO**adam_steps
    direction = first_new / corr_one / (jnp.sqrt(second_new / corr_two) + ADAM_EPS)
    weight_new = weight - LEARN_RATE * lr_scale * (direction + DECAY_RATE * flag * weight)
    return (weight_new, first_new, second_new)


def pairs(n, k):
    return [(i, i ^ k) for i in range(n)]


def direct(n):
    return 2 <= n <= 8 and n & (n - 1) == 0


def gather(x):
    n = lax.axis_size("fsdp")
    if not direct(n):
        return lax.all_gather(x, "fsdp", axis=0, tiled=True)
    me = lax.axis_index("fsdp")
    pieces = [None] * n
    pieces[0] = x
    for k in range(2, n, 2):
        pieces[k] = lax.ppermute(x, "fsdp", pairs(n, k))
    for k in range(0, n, 2):
        pieces[k + 1] = lax.ppermute(pieces[k], "fsdp", pairs(n, 1))
    out = jnp.stack(pieces)
    bit = 1
    while bit < n:
        v = out.reshape((n // (2 * bit), 2, bit) + x.shape)
        out = jnp.where((me & bit) != 0, v[:, ::-1], v).reshape(out.shape)
        bit *= 2
    return out.reshape((n * x.shape[0],) + x.shape[1:])


def reduce_scatter(g):
    n = lax.axis_size("fsdp")
    d = lax.axis_size("dp")
    r = g.shape[0] // n
    if not (direct(n) and d == 4):
        share = lax.psum_scatter(g, "fsdp", scatter_dimension=0, tiled=True)
        return lax.psum(share.astype(BF), "dp").astype(F32)
    me = lax.axis_index("fsdp")
    core = me % 2
    z = me // 2
    v = g.reshape((n // 2, 2, r) + g.shape[1:])
    mine = lax.dynamic_index_in_dim(v, core, 1, keepdims=False)
    other = lax.dynamic_index_in_dim(v, 1 - core, 1, keepdims=False)
    h = mine + lax.ppermute(other.astype(BF), "fsdp", pairs(n, 1)).astype(F32)
    got = [
        lax.ppermute(
            lax.dynamic_index_in_dim(h, z ^ k, 0, keepdims=False).astype(BF), "fsdp", pairs(n, 2 * k)
        )
        for k in range(1, n // 2)
    ]
    own = lax.dynamic_index_in_dim(h, z, 0, keepdims=False)
    for piece in got:
        own = own + piece.astype(F32)
    b = own.astype(BF)
    p1, p2, p3 = [lax.ppermute(b, "dp", pairs(d, k)).astype(F32) for k in (1, 2, 3)]
    return (b.astype(F32) + p1) + (p2 + p3)


def local(
    images, cotangent, counts,
    w_qkv, w_proj, w_fc1, w_fc2, b_fc1, vectors,
    m_qkv, m_proj, m_fc1, m_fc2, m_bias1, m_vectors,
    v_qkv, v_proj, v_fc1, v_fc2, v_bias1, v_vectors,
    decay_flags, group_ids, group_scales,
):
    masters = (w_qkv, w_proj, w_fc1, w_fc2, b_fc1, vectors)
    r = w_qkv.shape[0]
    D = images.shape[2]
    FF = w_fc1.shape[1]
    nb = b_fc1.shape[0] // r
    nv = vectors.shape[0]
    small = jnp.concatenate(
        [vectors.T, b_fc1.reshape(r, nb), jnp.zeros((r, 128 - nv - nb), F32)], axis=1
    )
    pack_a = jnp.concatenate([w_qkv, small], axis=1).astype(BF)
    pack_b = jnp.concatenate([w_fc1, w_fc2.T, w_proj], axis=1).astype(BF)
    full_a = gather(pack_a)
    full_b = gather(pack_b)
    W3 = w_qkv.shape[1]
    wq = full_a[:, :W3]
    sm = full_a[:, W3:].astype(F32)
    vec = jnp.pad(sm[:, :nv].T, ((0, 8 - nv), (0, 0)))
    c1 = jnp.broadcast_to(sm[:, nv : nv + nb].reshape(1, FF), (8, FF))
    w1 = full_b[:, :FF]
    w2t = full_b[:, FF : 2 * FF]
    wp = full_b[:, 2 * FF :]
    qkv, o, logs = k1(images, wq, vec)
    out_block, dx1, do, tp, t1, t2, tc1, tv2 = k2(counts, images, o, cotangent, wp, w1, w2t, c1, vec)
    grad_input, tq, tv1 = k3(images, qkv, logs, do, dx1, wq, vec)
    gsm = jnp.concatenate([tv2[:nv].T, tc1[0].reshape(D, nb), jnp.zeros((D, 128 - nv - nb), F32)], axis=1)
    red_b = reduce_scatter(jnp.concatenate([t1, t2, tp, gsm], axis=1))
    red_a = reduce_scatter(jnp.concatenate([tq, jnp.pad(tv1[:2].T, ((0, 0), (0, 126)))], axis=1))
    g_small = red_b[:, 2 * FF + D :]
    totals = (
        red_a[:, :W3],
        red_b[:, 2 * FF : 2 * FF + D],
        red_b[:, :FF],
        red_b[:, FF : 2 * FF].T,
        g_small[:, nv : nv + nb].reshape(-1),
        jnp.concatenate([red_a[:, W3 : W3 + 2], g_small[:, 2:nv]], axis=1).T,
    )
    slot_total = images.shape[0] * lax.axis_size("dp") * lax.axis_size("fsdp")
    grads = [total / slot_total for total in totals]
    firsts = (m_qkv, m_proj, m_fc1, m_fc2, m_bias1, m_vectors)
    seconds = (v_qkv, v_proj, v_fc1, v_fc2, v_bias1, v_vectors)
    group_range = jnp.arange(group_scales.shape[0])
    new_weights, new_firsts, new_seconds = ([], [], [])
    for place in range(6):
        flag = decay_flags[place].astype(jnp.float32)
        lr_scale = jnp.sum(jnp.where(group_range == group_ids[place], group_scales, 0.0))
        weight_n, first_n, second_n = adam_update(
            masters[place], grads[place], firsts[place], seconds[place], flag, lr_scale
        )
        new_weights.append(weight_n)
        new_firsts.append(first_n)
        new_seconds.append(second_n)
    return (out_block, grad_input, *grads, *new_weights, *new_firsts, *new_seconds)


def solution(mesh):
    return jax.shard_map(
        local,
        mesh=mesh,
        in_specs=(
            P(("dp", "fsdp"), None, None),
            P(("dp", "fsdp"), None, None),
            P(("dp", "fsdp")),
            P("fsdp", None),
            P("fsdp", None),
            P("fsdp", None),
            P(None, "fsdp"),
            P("fsdp"),
            P(None, "fsdp"),
            P("fsdp", None),
            P("fsdp", None),
            P("fsdp", None),
            P(None, "fsdp"),
            P("fsdp"),
            P(None, "fsdp"),
            P("fsdp", None),
            P("fsdp", None),
            P("fsdp", None),
            P(None, "fsdp"),
            P("fsdp"),
            P(None, "fsdp"),
            P(),
            P(),
            P(),
        ),
        out_specs=(
            P(("dp", "fsdp"), None, None),
            P(("dp", "fsdp"), None, None),
            P("fsdp", None),
            P("fsdp", None),
            P("fsdp", None),
            P(None, "fsdp"),
            P("fsdp"),
            P(None, "fsdp"),
            P("fsdp", None),
            P("fsdp", None),
            P("fsdp", None),
            P(None, "fsdp"),
            P("fsdp"),
            P(None, "fsdp"),
            P("fsdp", None),
            P("fsdp", None),
            P("fsdp", None),
            P(None, "fsdp"),
            P("fsdp"),
            P(None, "fsdp"),
            P("fsdp", None),
            P("fsdp", None),
            P("fsdp", None),
            P(None, "fsdp"),
            P("fsdp"),
            P(None, "fsdp"),
        ),
        check_vma=False,
    )
```

```python
import math
from functools import partial

import jax
import jax.numpy as jnp
from jax import lax
from jax.experimental import pallas as pl
from jax.experimental.pallas import tpu as pltpu
from jax.sharding import PartitionSpec

BF = jnp.bfloat16
F32 = jnp.float32
HEAD_DIM = 64
EPS_LN = 1e-06
LEARN_RATE = 0.2
BETA_ONE = 0.9
BETA_TWO = 0.999
ADAM_EPS = 1e-08
DECAY_RATE = 0.5
ADAM_STEPS = 10.0
GROUP = 8
PAIR = 2
EXTRA = 8
ROOT_HALF = math.sqrt(0.5)


def up(n, m):
    return (n + m - 1) // m * m


def dot(a, b, ca=1, cb=0):
    return lax.dot_general(a, b, (((ca,), (cb,)), ((), ())), preferred_element_type=F32)


def tiles(n, w):
    return [(a, min(w, n - a)) for a in range(0, n, w)]


def params(flops=0, nbytes=0):
    return dict(
        compiler_params=pltpu.CompilerParams(vmem_limit_bytes=58 << 20),
        cost_estimate=pl.CostEstimate(flops=flops, bytes_accessed=nbytes, transcendentals=0),
    )


def weave(ms, vs):
    k = 0
    for a, f in enumerate(ms):
        f()
        while k * len(ms) < len(vs) * (a + 1):
            vs[k]()
            k += 1
    for f in vs[k:]:
        f()


def norm_rows(x):
    c = x - jnp.mean(x, axis=-1, keepdims=True)
    r = lax.rsqrt(jnp.mean(c * c, axis=-1, keepdims=True) + EPS_LN)
    return c * r, r


def gelu_pair(u):
    t = 1.0 / (1.0 + (0.3275911 * ROOT_HALF) * jnp.abs(u))
    e = jnp.exp(-0.5 * (u * u))
    q = t * (0.127414796 + t * (-0.142248368 + t * (0.7107068705 + t * (-0.7265760135 + t * 0.5307027145)))) * e
    phi = jnp.where(u >= 0, 1.0 - q, q)
    return u * phi, phi + u * e * 0.3989422804014327


def full(a):
    return pl.BlockSpec(a.shape, lambda *_: (0,) * len(a.shape))


def whole(*shape):
    return pl.BlockSpec(shape, lambda *_: (0,) * len(shape))


def spread(src, dst, seq):
    for t, n in tiles(seq, 20):
        x = src[t : t + n].astype(F32).reshape(n * GROUP, src.shape[2])
        for c in range(dst.shape[0]):
            dst[c, t * GROUP : (t + n) * GROUP, :] = x[:, c * 128 : (c + 1) * 128]


def image(ref, i, t, n):
    return jnp.concatenate(
        [ref[c, pl.ds(t * GROUP + i, n, stride=GROUP), :] for c in range(ref.shape[0])], axis=1
    )


def token(ref, t, tp):
    return jnp.concatenate(
        [ref[c, pl.ds(t, GROUP, stride=tp), :] for c in range(ref.shape[0])], axis=1
    )


def tokens(ref, t, tp):
    return jnp.stack([token(ref, t, tp), token(ref, t + 1, tp)])


def pack_body(r, wq_ref, vec_ref, b_ref, w1_ref, w2_ref, wp_ref, a_ref, b_out, sm):
    FF = w1_ref.shape[1]
    a_ref[0:r, :] = wq_ref[...].astype(BF)
    sm[...] = jnp.zeros_like(sm)
    sm[0 : vec_ref.shape[0], 0 : vec_ref.shape[1]] = vec_ref[...]
    sm[6:7, 0 : b_ref.shape[1]] = b_ref[...]
    a_ref[r : r + EXTRA, :] = sm[...].astype(BF)
    b_out[:, 0:FF] = w1_ref[...].astype(BF)
    b_out[:, FF : 2 * FF] = w2_ref[...].astype(BF)
    b_out[:, 2 * FF :] = wp_ref[...].astype(BF)


def pack(wq, vec, b, w1, w2t, wp):
    r, W3 = wq.shape
    FF = w1.shape[1]
    C = 2 * FF + wp.shape[1]
    return pl.pallas_call(
        partial(pack_body, r),
        out_shape=[jax.ShapeDtypeStruct((r + EXTRA, W3), BF), jax.ShapeDtypeStruct((r, C), BF)],
        scratch_shapes=[pltpu.VMEM((EXTRA, W3), F32)],
        name="pack",
        **params(),
    )(wq, vec, b, w1, w2t, wp)


def attend_body(SEQ, SP, TP, D, np_, me_ref, x_ref, *refs):
    H = D // HEAD_DIM
    g = pl.program_id(0)
    j = pl.program_id(1)
    if np_:
        pieces, refs = refs[:np_], refs[np_:]
        qkv_ref, o_ref, l_ref, xi_ref, w_ref, vec_ref, c1_ref, sm = refs[:8]
        refs = refs[8:]
    else:
        w_ref, vec_ref, qkv_ref, o_ref, l_ref, xi_ref = refs[:6]
        refs = refs[6:]
    xs, os_, a_scr, s0, s1, p0, p1 = refs

    @pl.when((g == 0) & (j == 0))
    def _():
        for ref in (a_scr, p0, p1, os_):
            ref[...] = jnp.zeros_like(ref)
        if np_:
            r = pieces[0].shape[0] - EXTRA
            for k in range(np_):
                s = me_ref[0] ^ k
                w_ref[pl.ds(pl.multiple_of(s * r, 16), r), :] = pieces[k][0:r, :]
                sm[s] = pieces[k][r : r + EXTRA, 0 : sm.shape[2]].astype(F32)
            nb = c1_ref.shape[1] // np_
            vec_ref[...] = jnp.concatenate([sm[s, :, 0:r] for s in range(np_)], axis=1)
            c1_ref[...] = jnp.broadcast_to(
                jnp.concatenate([sm[s, 6:7, 0:nb] for s in range(np_)], axis=1), c1_ref.shape
            )

    @pl.when(j == 0)
    def _():
        spread(x_ref, xs, SEQ)

    gain = vec_ref[0:1, :]
    shift = vec_ref[1:2, :]
    ss = (s0, s1)
    pp = (p0, p1)
    st = {}
    S8 = SEQ // 8 * 8

    def ln(i, t, n):
        x = image(xs, j * PAIR + i, t, n)
        xi_ref[i, t : t + n, :] = x.astype(BF)
        xh, _ = norm_rows(x)
        a_scr[i * SP + t : i * SP + t + n, :] = (xh * gain + shift).astype(BF)

    def qkv(i, t, c, w):
        y = dot(a_scr[i * SP : (i + 1) * SP, :], w_ref[:, t * D + c : t * D + c + w])
        if t == 0:
            y = y * (HEAD_DIM**-0.5)
        qkv_ref[i, :, t * D + c : t * D + c + w] = y.astype(BF)

    def score(u):
        i, h = divmod(u, H)
        lo = h * HEAD_DIM
        ss[u % 2][...] = dot(
            qkv_ref[i, :, D + lo : D + lo + HEAD_DIM], qkv_ref[i, :, lo : lo + HEAD_DIM], 1, 1
        )

    def tile(ref, t, n):
        x = ref[t : t + n, :]
        if t + n > SEQ:
            x = jnp.where(lax.broadcasted_iota(jnp.int32, (n, 1), 0) < SEQ - t, x, -1e30)
        return x

    def vmax(u, t, n):
        m = jnp.max(tile(ss[u % 2], t, n).reshape(n // 8, 8, SP), axis=0)
        st[u] = m if t == 0 else jnp.maximum(st[u], m)
        if t + n >= SEQ:
            st[u] = jnp.max(st[u], axis=0, keepdims=True)

    def vexp(u, t, n):
        i, h = divmod(u, H)
        p = jnp.exp(tile(ss[u % 2], t, n) - st[u])
        ss[u % 2][t : t + n, :] = p
        total = jnp.sum(p.reshape(n // 8, 8, SP), axis=0)
        k = ("l", u)
        st[k] = total if t == 0 else st[k] + total
        if t + n >= SEQ:
            total = jnp.sum(st[k], axis=0, keepdims=True)
            l_ref[i, h : h + 1, :] = st[u] + jnp.log(total)
            st[k] = 1.0 / total

    def vnorm(u, t, n):
        pp[u % 2][t : t + n, :] = (ss[u % 2][t : t + n, :] * st[("l", u)]).astype(BF)

    def mix(u):
        i, h = divmod(u, H)
        lo = 2 * D + h * HEAD_DIM
        y = dot(pp[u % 2][...], qkv_ref[i, :, lo : lo + HEAD_DIM], 0, 0)
        if h % 2 == 0:
            st["o"] = y
        else:
            y = jnp.concatenate([st["o"], y], axis=1)
            os_[h // 2, pl.ds(pl.multiple_of((j * PAIR + i) * TP, 8), SEQ), :] = y[:SEQ]

    rows = tiles(SEQ, 48)
    for t, n in rows:
        ln(0, t, n)
    c0 = min(256, D)
    cs = tiles(D, 256)
    weave([partial(qkv, 0, t, 0, c0) for t in range(3)], [partial(ln, 1, t, n) for t, n in rows])
    rest = [partial(qkv, 0, t, c, w) for c, w in cs[1:] for t in range(3)]
    rest += [partial(qkv, 1, t, c, w) for c, w in cs for t in range(3)]
    srows = tiles(S8, 64) + ([(S8, 8)] if S8 < SEQ else [])
    nu = PAIR * H
    score(0)
    done = 0
    for k in range(nu):
        ms = []
        need = 3 if k < 2 else 2
        ms += rest[done : done + need]
        done += need
        if k + 1 < nu:
            ms.append(partial(score, k + 1))
        if k >= 1:
            ms.append(partial(mix, k - 1))
        vs = [partial(f, k, t, n) for f in (vmax, vexp, vnorm) for t, n in srows]
        weave(ms, vs)
    assert done >= len(rest)
    mix(nu - 1)
    for i in range(PAIR):
        xi_ref[i, SEQ:SP, :] = jnp.zeros((SP - SEQ, D), BF)

    @pl.when(j == pl.num_programs(1) - 1)
    def _():
        for t in range(0, TP, 2):
            o_ref[t : t + 2] = tokens(os_, t, TP).astype(BF)


def attend(me, x, pieces, w, vec, FF, TP):
    SEQ, N, D = x.shape
    SP = up(SEQ, 16)
    W3 = 3 * D
    np_ = len(pieces)
    tok = lambda t: pl.BlockSpec((t, GROUP, D), lambda g, j, *_: (0, g, 0))
    img = lambda r, d: pl.BlockSpec((PAIR, r, d), lambda g, j, *_: (g * (GROUP // PAIR) + j, 0, 0))
    v = pltpu.VMEM
    s = jax.ShapeDtypeStruct
    ins = list(pieces) if np_ else [w, vec]
    out_specs = [img(SP, W3), tok(TP), img(8, SP), img(SP, D)]
    out_shape = [s((N, SP, W3), BF), s((TP, N, D), BF), s((N, 8, SP), F32), s((N, SP, D), BF)]
    scratch = [v((D // 128, TP * GROUP, 128), F32)] * 2 + [v((PAIR * SP, D), BF)]
    scratch += [v((SP, SP), F32)] * 2 + [v((SP, SP), BF)] * 2
    if np_:
        out_specs += [whole(D, W3), whole(8, D), whole(8, FF)]
        out_shape += [s((D, W3), BF), s((8, D), F32), s((8, FF), F32)]
        scratch = [v((np_, EXTRA, up(max(FF, D) // np_, 128)), F32)] + scratch
    return pl.pallas_call(
        partial(attend_body, SEQ, SP, TP, D, np_),
        grid_spec=pltpu.PrefetchScalarGridSpec(
            num_scalar_prefetch=1,
            grid=(N // GROUP, GROUP // PAIR),
            in_specs=[tok(SEQ)] + [full(a) for a in ins],
            out_specs=out_specs,
            scratch_shapes=scratch,
        ),
        out_shape=out_shape,
        name="attend",
        **params(20 * 10**9, 25 * 10**6),
    )(me, x, *ins)


def feed_body(SEQ, D, FF, T, N, np_, me_ref, cnt_ref, x_ref, o_ref, cot_ref, c1_ref, vec_ref, *refs):
    s = pl.program_id(0)
    R = T * N
    RT = 2 * N
    HR = R // 2
    if np_:
        pieces, refs = refs[:np_], refs[np_:]
        out_ref, dx1_ref, do_ref, tc1_ref, tv_ref, snd_ref, keep_ref = refs[:7]
        wp_ref, w1_ref, w2t_ref, tp_ref, t1_ref, t2_ref = refs[7:13]
        refs = refs[13:]
    else:
        wp_ref, w1_ref, w2t_ref, out_ref, dx1_ref, do_ref, tc1_ref, tv_ref, tp_ref, t1_ref, t2_ref = refs[:11]
        refs = refs[11:]
    b_scr, bt_scr, dy_scr, dyt_scr, xh_scr, r_scr, x1_scr, u0, u1, d0, d1, g_scr, du_scr, y_scr, db_scr, dx_scr = refs

    @pl.when(s == 0)
    def _():
        for ref in (tp_ref, t1_ref, t2_ref, tc1_ref, tv_ref):
            ref[...] = jnp.zeros_like(ref)
        if np_:
            r = pieces[0].shape[0]
            for k in range(np_):
                at = pl.ds(pl.multiple_of((me_ref[0] ^ k) * r, 16), r)
                w1_ref[at, :] = pieces[k][:, 0:FF]
                w2t_ref[at, :] = pieces[k][:, FF : 2 * FF]
                wp_ref[at, :] = pieces[k][:, 2 * FF :]

    cp = vec_ref[2:3, :]
    g2 = vec_ref[3:4, :]
    e2 = vec_ref[4:5, :]
    c2 = vec_ref[5:6, :]
    io = lax.broadcasted_iota(jnp.int32, (RT, 1), 0)
    real = lax.rem(io, N) < cnt_ref[0]
    lim = SEQ * N - s * R
    acc = {}

    def rows(ref, r):
        return ref[r // N : r // N + 2].reshape(RT, D)

    def add(key, v):
        v = jnp.sum(v.reshape(v.shape[0] // 8, 8, v.shape[1]), axis=0)
        acc[key] = v if key not in acc else acc[key] + v

    def m_proj(h):
        x1_scr[h : h + HR, :] = dot(o_ref[h // N : (h + HR) // N].reshape(HR, D), wp_ref[...])

    def v_norm(r):
        inside = (io + r) < lim
        x = jnp.where(inside, rows(x_ref, r).astype(F32), 0.0)
        dy_scr[r : r + RT, :] = jnp.where(real & inside, rows(cot_ref, r), jnp.zeros((), BF))
        x1 = x + x1_scr[r : r + RT, :] + cp
        x1_scr[r : r + RT, :] = x1 + c2
        xh, rr = norm_rows(x1)
        xh_scr[r : r + RT, :] = xh
        r_scr[r : r + RT, :] = jnp.broadcast_to(rr, (RT, 128))
        b_scr[r : r + RT, :] = (xh * g2 + e2).astype(BF)

    cols = tiles(FF, 256)
    us = (u0, u1)
    ds = (d0, d1)

    def m_u(i, h):
        c, w = cols[i]
        us[i % 2][h : h + HR, :w] = dot(b_scr[h : h + HR, :], w1_ref[:, c : c + w]) + c1_ref[0:1, c : c + w]

    def m_d(i, h):
        c, w = cols[i]
        ds[i % 2][h : h + HR, :w] = dot(dy_scr[h : h + HR, :], w2t_ref[:, c : c + w])

    def v_gelu(i, r):
        c, w = cols[i]
        ga, dg = gelu_pair(us[i % 2][r : r + 16, :w])
        g_scr[r : r + 16, c : c + w] = ga.astype(BF)
        du = ds[i % 2][r : r + 16, :w] * dg
        du_scr[r : r + 16, c : c + w] = du.astype(BF)
        add(("c1", i), du)

    def m_t1(i):
        c, w = cols[i]
        t1_ref[:, c : c + w] += dot(bt_scr[...], du_scr[:, c : c + w])

    def m_t2(i):
        c, w = cols[i]
        t2_ref[:, c : c + w] += dot(dyt_scr[...], g_scr[:, c : c + w])

    def m_y(h):
        y_scr[h : h + HR, :] = dot(g_scr[h : h + HR, :], w2t_ref[...], 1, 1)

    def m_db(h):
        db_scr[h : h + HR, :] = dot(du_scr[h : h + HR, :], w1_ref[...], 1, 1)

    def v_out(r):
        y = x1_scr[r : r + RT, :] + y_scr[r : r + RT, :]
        out_ref[r // N : r // N + 2] = jnp.where(real, y, 0.0).astype(BF).reshape(2, N, D)

    def v_back(r):
        db = db_scr[r : r + RT, :]
        xh = xh_scr[r : r + RT, :]
        dyf = dy_scr[r : r + RT, :].astype(F32)
        dxh = db * g2
        mean1 = jnp.mean(dxh, axis=-1, keepdims=True)
        mean2 = jnp.mean(dxh * xh, axis=-1, keepdims=True)
        dx = dyf + r_scr[r : r + RT, 0:1] * (dxh - mean1 - xh * mean2)
        add("g2", db * xh)
        add("e2", db)
        add("c2", dyf)
        add("cp", dx)
        dx1_ref[r // N : r // N + 2] = dx.reshape(2, N, D)
        dx_scr[r : r + RT, :] = dx.astype(BF)

    def m_do(h):
        y = dot(dx_scr[h : h + HR, :], wp_ref[...], 1, 1)
        do_ref[h // N : (h + HR) // N] = y.astype(BF).reshape(HR // N, N, D)

    def m_tp():
        tp_ref[...] += dot(o_ref[...].reshape(R, D), dx_scr[...], 0, 0)

    first = list(range(0, HR, RT))
    second = list(range(HR, R, RT))
    last = len(cols) - 1
    m_proj(0)
    weave([partial(m_proj, HR)], [partial(v_norm, r) for r in first])
    weave([partial(m_u, 0, 0), partial(m_d, 0, 0)], [partial(v_norm, r) for r in second])
    bt_scr[...] = b_scr[...].T
    dyt_scr[...] = dy_scr[...].T
    m_u(0, HR)
    m_d(0, HR)
    for i in range(len(cols)):
        ms = []
        if i < last:
            ms += [partial(f, i + 1, h) for f in (m_u, m_d) for h in (0, HR)]
        if i >= 1:
            ms += [partial(m_t1, i - 1), partial(m_t2, i - 1)]
        weave(ms, [partial(v_gelu, i, r) for r in range(0, R, 16)])
        c, w = cols[i]
        tc1_ref[:, c : c + w] += acc[("c1", i)]
    m_db(0)
    weave([partial(m_db, HR)], [partial(v_back, r) for r in first])
    weave([partial(m_y, 0), partial(m_do, 0)], [partial(v_back, r) for r in second])
    weave([partial(m_y, HR), partial(m_do, HR)], [partial(v_out, r) for r in first])
    weave([partial(m_t1, last), partial(m_t2, last), m_tp], [partial(v_out, r) for r in second])
    for i, k in ((2, "cp"), (3, "g2"), (4, "e2"), (5, "c2")):
        tv_ref[i * 8 : i * 8 + 8, :] += acc[k]

    if np_:

        @pl.when(s == pl.num_programs(0) - 1)
        def _():
            r = D // np_
            for k in range(0, np_, 2):
                for ref, flip in ((keep_ref, 0), (snd_ref, 1)):
                    at = pl.ds(pl.multiple_of((me_ref[0] ^ (k + flip)) * r, 16), r)
                    ref[k // 2, :, 0:FF] = t1_ref[at, :].astype(ref.dtype)
                    ref[k // 2, :, FF : 2 * FF] = t2_ref[at, :].astype(ref.dtype)
                    ref[k // 2, :, 2 * FF :] = tp_ref[at, :].astype(ref.dtype)


def feed(me, cnt, x, o, cot, c1, vec, pieces, weights, T):
    SEQ, N, D = x.shape
    TP = o.shape[0]
    FF = c1.shape[1]
    np_ = len(pieces)
    R = T * N
    v = pltpu.VMEM
    s = jax.ShapeDtypeStruct
    blk = pl.BlockSpec((T, N, D), lambda i, *_: (i, 0, 0))
    ins = list(pieces) if np_ else list(weights)
    out_specs = [blk, blk, blk, whole(8, FF), whole(64, D)]
    out_shape = [s((SEQ, N, D), BF), s((TP, N, D), F32), s((TP, N, D), BF), s((8, FF), F32), s((64, D), F32)]
    scratch = []
    if np_:
        shape = (np_ // 2, D // np_, 2 * FF + D)
        out_specs += [whole(*shape)] * 2
        out_shape += [s(shape, BF), s(shape, F32)]
        scratch += [v((D, D), BF), v((D, FF), BF), v((D, FF), BF), v((D, D), F32), v((D, FF), F32), v((D, FF), F32)]
    else:
        out_specs += [whole(D, D), whole(D, FF), whole(D, FF)]
        out_shape += [s((D, D), F32), s((D, FF), F32), s((D, FF), F32)]
    scratch += [v((R, D), BF), v((D, R), BF), v((R, D), BF), v((D, R), BF), v((R, D), F32), v((R, 128), F32), v((R, D), F32)]
    scratch += [v((R, 256), F32)] * 4 + [v((R, FF), BF)] * 2 + [v((R, D), F32)] * 2 + [v((R, D), BF)]
    return pl.pallas_call(
        partial(feed_body, SEQ, D, FF, T, N, np_),
        grid_spec=pltpu.PrefetchScalarGridSpec(
            num_scalar_prefetch=2,
            grid=(TP // T,),
            in_specs=[blk, blk, blk, full(c1), full(vec)] + [full(a) for a in ins],
            out_specs=out_specs,
            scratch_shapes=scratch,
        ),
        out_shape=out_shape,
        name="feed",
        **params(45 * 10**9, 30 * 10**6),
    )(me, cnt, x, o, cot, c1, vec, *ins)


def back_body(SEQ, SP, TP, D, FF, np_, me_ref, xi_ref, qkv_ref, l_ref, do_ref, dx1_ref, w_ref, vec_ref, tc1_ref, tv2_ref, gi_ref, *refs):
    if np_:
        snd_ref, keep_ref, tq_ref, sm = refs[:4]
        gv_ref, refs = refs[4], refs[5:]
    else:
        tq_ref, gv_ref, refs = refs[0], refs[1], refs[2:]
    dos, gs, dob, a_scr, at_scr, xh_scr, r_scr, d_scr, da_scr, tv_ref, s0, s1, e0, e1, p0, p1, q0, q1 = refs
    H = D // HEAD_DIM
    W3 = 3 * D
    g = pl.program_id(0)
    j = pl.program_id(1)

    @pl.when((g == 0) & (j == 0))
    def _():
        for ref in (d_scr, p0, p1, q0, q1, dob, tq_ref, tv_ref):
            ref[...] = jnp.zeros_like(ref)

    @pl.when(j == 0)
    def _():
        spread(do_ref, dos, SEQ)

    gain = vec_ref[0:1, :]
    shift = vec_ref[1:2, :]
    ss = (s0, s1)
    es = (e0, e1)
    pp = (p0, p1)
    qq = (q0, q1)
    st = {}
    S8 = SEQ // 8 * 8

    def load(i, t, n):
        dob[i * SP + t : i * SP + t + n, :] = image(dos, j * PAIR + i, t, n).astype(BF)

    def ln(i, t, n):
        xh, r = norm_rows(xi_ref[i, t : t + n, :].astype(F32))
        at = slice(i * SP + t, i * SP + t + n)
        xh_scr[at, :] = xh
        r_scr[at, :] = jnp.broadcast_to(r, (n, 128))
        a_scr[at, :] = (xh * gain + shift).astype(BF)

    def part(i, h, t):
        lo = t * D + h * HEAD_DIM
        return qkv_ref[i, :, lo : lo + HEAD_DIM]

    def dpart(i, h):
        return dob[i * SP : (i + 1) * SP, h * HEAD_DIM : (h + 1) * HEAD_DIM]

    def score(u):
        i, h = divmod(u, H)
        ss[u % 2][...] = dot(part(i, h, 1), part(i, h, 0), 1, 1)

    def dprob(u):
        i, h = divmod(u, H)
        es[u % 2][...] = dot(part(i, h, 2), dpart(i, h), 1, 1)

    def v_prob(u, t, n):
        i, h = divmod(u, H)
        p = jnp.exp(ss[u % 2][t : t + n, :] - l_ref[i, h : h + 1, :])
        if t + n > SEQ:
            p = jnp.where(lax.broadcasted_iota(jnp.int32, (n, 1), 0) < SEQ - t, p, 0.0)
        ss[u % 2][t : t + n, :] = p
        pp[u % 2][t : t + n, :] = p.astype(BF)
        x = jnp.sum((p * es[u % 2][t : t + n, :]).reshape(n // 8, 8, SP), axis=0)
        st[u] = x if t == 0 else st[u] + x
        if t + n >= SEQ:
            st[u] = jnp.sum(st[u], axis=0, keepdims=True)

    def v_ds(u, t, n):
        qq[u % 2][t : t + n, :] = (ss[u % 2][t : t + n, :] * (es[u % 2][t : t + n, :] - st[u])).astype(BF)

    def put(u, t, y):
        i, h = divmod(u, H)
        if h % 2 == 0:
            st[("d", t)] = y
        else:
            y = jnp.concatenate([st[("d", t)], y], axis=1).astype(BF)
            lo = t * D + (h - 1) * HEAD_DIM
            d_scr[i * SP : i * SP + SEQ, lo : lo + 2 * HEAD_DIM] = y[:SEQ]

    def m_dv(u):
        put(u, 2, dot(pp[u % 2][...], dpart(*divmod(u, H))))

    def m_dk(u):
        i, h = divmod(u, H)
        put(u, 1, dot(qq[u % 2][...], part(i, h, 0)))

    def m_dq(u):
        i, h = divmod(u, H)
        put(u, 0, dot(qq[u % 2][...], part(i, h, 1), 0, 0) * (HEAD_DIM**-0.5))

    rows = tiles(SEQ, 48)
    srows = tiles(S8, 64) + ([(S8, 8)] if S8 < SEQ else [])
    for t, n in rows:
        load(0, t, n)
    pre = [partial(load, 1, t, n) for t, n in rows] + [partial(ln, i, t, n) for i in range(PAIR) for t, n in rows]
    nu = PAIR * H
    score(0)
    dprob(0)
    for k in range(nu):
        ms = []
        if k + 1 < nu:
            ms += [partial(score, k + 1), partial(dprob, k + 1)]
        if k >= 1:
            ms += [partial(m_dv, k - 1), partial(m_dk, k - 1), partial(m_dq, k - 1)]
        vs = [partial(f, k, t, n) for f in (v_prob, v_ds) for t, n in srows]
        vs += pre[3 * k : 3 * k + 3]
        weave(ms, vs)
    assert 3 * nu >= len(pre)
    m_dv(nu - 1)
    m_dk(nu - 1)
    m_dq(nu - 1)
    acc = {}

    def m_da(i):
        da_scr[i * SP : (i + 1) * SP, :] = dot(d_scr[i * SP : (i + 1) * SP, :], w_ref[...], 1, 1)

    def m_tq(c, w):
        tq_ref[:, c : c + w] += dot(at_scr[...], d_scr[:, c : c + w])

    def add(key, v):
        f = v.shape[0] // 8 * 8
        if f:
            x = jnp.sum(v[:f].reshape(f // 8, 8, D), axis=0)
            acc[key] = x if key not in acc else acc[key] + x
        if f < v.shape[0]:
            x = jnp.sum(v[f:], axis=0, keepdims=True)
            key = key + "tail"
            acc[key] = x if key not in acc else acc[key] + x

    def v_back(i, t, n):
        at = slice(i * SP + t, i * SP + t + n)
        d = da_scr[at, :]
        xh = xh_scr[at, :]
        dxh = d * gain
        mean1 = jnp.mean(dxh, axis=-1, keepdims=True)
        mean2 = jnp.mean(dxh * xh, axis=-1, keepdims=True)
        y = r_scr[at, 0:1] * (dxh - mean1 - xh * mean2)
        for c in range(gs.shape[0]):
            gs[c, pl.ds(pl.multiple_of((j * PAIR + i) * TP + t, 8), n), :] = y[:, c * 128 : (c + 1) * 128]
        add("g", d * xh)
        add("e", d)

    at_scr[...] = a_scr[...].T
    cols = tiles(W3, 256)
    m_da(0)
    weave([partial(m_da, 1)] + [partial(m_tq, c, w) for c, w in cols[:2]], [partial(v_back, 0, t, n) for t, n in rows])
    weave([partial(m_tq, c, w) for c, w in cols[2:]], [partial(v_back, 1, t, n) for t, n in rows])
    tv_ref[0:8, :] += acc["g"]
    tv_ref[8:16, :] += acc["e"]
    if "gtail" in acc:
        tv_ref[0:1, :] += acc["gtail"]
        tv_ref[8:9, :] += acc["etail"]

    @pl.when(j == pl.num_programs(1) - 1)
    def _():
        for t in range(0, SEQ - 1, 2):
            gi_ref[t : t + 2] = (tokens(gs, t, TP) + dx1_ref[t : t + 2]).astype(BF)
        if SEQ % 2:
            gi_ref[SEQ - 1] = (token(gs, SEQ - 1, TP) + dx1_ref[SEQ - 1]).astype(BF)

    @pl.when((j == pl.num_programs(1) - 1) & (g == pl.num_programs(0) - 1))
    def _():
        for i in range(2):
            gv_ref[i : i + 1, :] = jnp.sum(tv_ref[8 * i : 8 * i + 8, :], axis=0, keepdims=True)
        for i in range(2, 6):
            gv_ref[i : i + 1, :] = jnp.sum(tv2_ref[8 * i : 8 * i + 8, :], axis=0, keepdims=True)
        if np_:
            r = D // np_
            nb = FF // np_
            sm[...] = jnp.zeros_like(sm)
            bias = jnp.sum(tc1_ref[...], axis=0, keepdims=True)
            for s in range(np_):
                sm[s, 0:6, 0:r] = gv_ref[0:6, s * r : (s + 1) * r]
                sm[s, 6:7, 0:nb] = bias[:, s * nb : (s + 1) * nb]
            wide = sm.shape[2]
            for k in range(0, np_, 2):
                for ref, flip in ((keep_ref, 0), (snd_ref, 1)):
                    s = me_ref[0] ^ (k + flip)
                    ref[k // 2, 0:r, :] = tq_ref[pl.ds(pl.multiple_of(s * r, 16), r), :].astype(ref.dtype)
                    ref[k // 2, r : r + EXTRA, 0:wide] = sm[s].astype(ref.dtype)
                    ref[k // 2, r : r + EXTRA, wide:] = jnp.zeros((EXTRA, W3 - wide), ref.dtype)


def back(me, xi, qkv, l, do, dx1, w, vec, tc1, tv2, SEQ, np_):
    N, SP, D = xi.shape
    TP = do.shape[0]
    W3 = 3 * D
    FF = tc1.shape[1]
    R = PAIR * SP
    tok = lambda t: pl.BlockSpec((t, GROUP, D), lambda g, j, *_: (0, g, 0))
    img = lambda r, d: pl.BlockSpec((PAIR, r, d), lambda g, j, *_: (g * (GROUP // PAIR) + j, 0, 0))
    v = pltpu.VMEM
    s = jax.ShapeDtypeStruct
    out_specs = [tok(SEQ)]
    out_shape = [s((SEQ, N, D), BF)]
    if np_:
        shape = (np_ // 2, D // np_ + EXTRA, W3)
        out_specs += [whole(*shape)] * 2
        out_shape += [s(shape, BF), s(shape, F32)]
        scratch = [v((D, W3), F32), v((np_, EXTRA, up(max(FF, D) // np_, 128)), F32), v((8, D), F32)]
    else:
        out_specs += [whole(D, W3), whole(8, D)]
        out_shape += [s((D, W3), F32), s((8, D), F32)]
        scratch = []
    scratch += [v((D // 128, TP * GROUP, 128), F32)] * 2
    scratch += [v((R, D), BF), v((R, D), BF), v((D, R), BF), v((R, D), F32), v((R, 128), F32), v((R, W3), BF), v((R, D), F32)]
    scratch += [v((16, D), F32)] + [v((SP, SP), F32)] * 4 + [v((SP, SP), BF)] * 4
    return pl.pallas_call(
        partial(back_body, SEQ, SP, TP, D, FF, np_),
        grid_spec=pltpu.PrefetchScalarGridSpec(
            num_scalar_prefetch=1,
            grid=(N // GROUP, GROUP // PAIR),
            in_specs=[img(SP, D), img(SP, W3), img(8, SP), tok(TP), tok(TP), full(w), full(vec), full(tc1), full(tv2)],
            out_specs=out_specs,
            scratch_shapes=scratch,
        ),
        out_shape=out_shape,
        name="back",
        **params(40 * 10**9, 30 * 10**6),
    )(me, xi, qkv, l, do, dx1, w, vec, tc1, tv2)


def adam_body(na, nb_, slots, FF, flag_ref, gid_ref, scale_ref, *refs):
    pa, refs = refs[:na], refs[na:]
    pb, refs = refs[:nb_], refs[nb_:]
    weights, firsts, seconds = refs[:6], refs[6:12], refs[12:18]
    outs = refs[18:]

    def total(ps, rows, cols):
        xs = [p[rows, cols].astype(F32) for p in ps]
        return xs[0] if len(xs) == 1 else (xs[0] + xs[1]) + (xs[2] + xs[3])

    r = weights[0].shape[0]
    D = weights[1].shape[1]
    every = slice(0, r)
    where = (
        (pa, every, slice(0, 3 * D)),
        (pb, every, slice(2 * FF, 2 * FF + D)),
        (pb, every, slice(0, FF)),
        (pb, every, slice(FF, 2 * FF)),
        (pa, slice(r + 6, r + 7), slice(0, weights[4].shape[1])),
        (pa, slice(r, r + 6), slice(0, weights[5].shape[1])),
    )
    for p, (ps, rows, cols) in enumerate(where):
        grad = total(ps, rows, cols) / slots
        flag = flag_ref[p].astype(F32)
        lr = scale_ref[gid_ref[p]]
        first = BETA_ONE * firsts[p][...] + (1.0 - BETA_ONE) * grad
        second = BETA_TWO * seconds[p][...] + (1.0 - BETA_TWO) * grad * grad
        direction = first / (1.0 - BETA_ONE**ADAM_STEPS) / (jnp.sqrt(second / (1.0 - BETA_TWO**ADAM_STEPS)) + ADAM_EPS)
        weight = weights[p][...]
        outs[p][...] = grad
        outs[6 + p][...] = weight - LEARN_RATE * lr * (direction + DECAY_RATE * flag * weight)
        outs[12 + p][...] = first
        outs[18 + p][...] = second


def adam(flags, gids, scales, pa, pb, weights, firsts, seconds, slots, FF):
    smem = pl.BlockSpec(memory_space=pltpu.SMEM)
    vmem = pl.BlockSpec(memory_space=pltpu.VMEM)
    shapes = [jax.ShapeDtypeStruct(w.shape, F32) for w in weights]
    count = len(pa) + len(pb) + 18
    return pl.pallas_call(
        partial(adam_body, len(pa), len(pb), slots, FF),
        in_specs=[smem] * 3 + [vmem] * count,
        out_specs=[vmem] * 24,
        out_shape=shapes * 4,
        name="adam",
        **params(),
    )(flags, gids, scales, *pa, *pb, *weights, *firsts, *seconds)


def pairs(n, k):
    return [(i, i ^ k) for i in range(n)]


def fetch(x, n):
    pieces = [None] * n
    pieces[0] = x
    for k in range(2, n, 2):
        pieces[k] = lax.ppermute(x, "fsdp", pairs(n, k))
    for k in range(0, n, 2):
        pieces[k + 1] = lax.ppermute(pieces[k], "fsdp", pairs(n, 1))
    return pieces


def halve(snd, keep, n):
    h = keep + lax.ppermute(snd, "fsdp", pairs(n, 1)).astype(F32)
    got = [lax.ppermute(h[k].astype(BF), "fsdp", pairs(n, 2 * k)) for k in range(1, n // 2)]
    return h[0], got


def finish(own, got, d):
    for piece in got:
        own = own + piece.astype(F32)
    b = own.astype(BF)
    return [b] + [lax.ppermute(b, "dp", pairs(d, k)) for k in range(1, d)]


def local(
    images, cotangent, counts,
    w_qkv, w_proj, w_fc1, w_fc2, b_fc1, vectors,
    m_qkv, m_proj, m_fc1, m_fc2, m_bias1, m_vectors,
    v_qkv, v_proj, v_fc1, v_fc2, v_bias1, v_vectors,
    decay_flags, group_ids, group_scales,
):
    n = lax.axis_size("fsdp")
    d = lax.axis_size("dp")
    N, SEQ, D = images.shape
    r = w_qkv.shape[0]
    FF = w_fc1.shape[1]
    T = 20
    TP = up(SEQ, T)
    direct = n in (2, 4, 8) and d == 4 and r % 16 == 0
    x = jnp.transpose(images, (1, 0, 2))
    cot = jnp.transpose(cotangent, (1, 0, 2))
    me = lax.axis_index("fsdp").astype(jnp.int32).reshape(1)
    rows = lambda b: b.reshape(1, -1)
    weights = [w_qkv, w_proj, w_fc1, w_fc2.T, rows(b_fc1), vectors]
    firsts = [m_qkv, m_proj, m_fc1, m_fc2.T, rows(m_bias1), m_vectors]
    seconds = [v_qkv, v_proj, v_fc1, v_fc2.T, rows(v_bias1), v_vectors]
    pack_a, pack_b = pack(weights[0], weights[5], weights[4], weights[2], weights[3], weights[1])
    if direct:
        pieces_a = fetch(pack_a, n)
        pack_b = lax.optimization_barrier((pack_b, pieces_a))[0]
        pieces_b = fetch(pack_b, n)
        qkv, o, logs, xi, wq, vec, c1 = attend(me, x, pieces_a, None, None, FF, TP)
        out, dx1, do, tc1, tv2, snd, keep = feed(me, counts, x, o, cot, c1, vec, pieces_b, (), T)
        own_b, got_b = halve(snd, keep, n)
        do, got0 = lax.optimization_barrier((do, own_b))
        gi, snd, keep = back(me, xi, qkv, logs, do, dx1, wq, vec, tc1, tv2, SEQ, n)
        pb = finish(own_b, got_b, d)
        own_a, got_a = halve(snd, keep, n)
        pa = finish(own_a, got_a, d)
    else:
        all_a = lax.all_gather(pack_a, "fsdp", axis=0, tiled=False)
        all_b = lax.all_gather(pack_b, "fsdp", axis=0, tiled=True)
        wq = all_a[:, :r].reshape(D, 3 * D)
        nb = FF // n
        vec = jnp.transpose(all_a[:, r : r + 8, :r], (1, 0, 2)).reshape(8, D).astype(F32)
        c1 = jnp.broadcast_to(all_a[:, r + 6, :nb].reshape(1, FF), (8, FF)).astype(F32)
        ws = (all_b[:, 2 * FF :], all_b[:, :FF], all_b[:, FF : 2 * FF])
        qkv, o, logs, xi = attend(me, x, (), wq, vec, FF, TP)
        out, dx1, do, tc1, tv2, tp, t1, t2 = feed(me, counts, x, o, cot, c1, vec, (), ws, T)
        gi, tq, gv = back(me, xi, qkv, logs, do, dx1, wq, vec, tc1, tv2, SEQ, 0)
        share = lambda g, axis: lax.psum(
            lax.psum_scatter(g, "fsdp", scatter_dimension=axis, tiled=True).astype(BF), "dp"
        ).astype(F32)
        pb = [share(jnp.concatenate([t1, t2, tp], axis=1), 0)]
        small = jnp.zeros((8, 3 * D), F32).at[:6, :r].set(share(gv[:6], 1))
        small = small.at[6, :nb].set(share(jnp.sum(tc1, axis=0), 0))
        pa = [jnp.concatenate([share(tq, 0), small], axis=0)]
    res = adam(decay_flags, group_ids, group_scales, pa, pb, weights, firsts, seconds, float(N * n * d), FF)
    res = list(res)
    for k in range(4):
        res[6 * k + 3] = res[6 * k + 3].T
        res[6 * k + 4] = res[6 * k + 4].reshape(-1)
    return (jnp.transpose(out, (1, 0, 2)), jnp.transpose(gi, (1, 0, 2)), *res)


def solution(mesh):
    P = PartitionSpec
    both = ("dp", "fsdp")
    six = (P("fsdp", None), P("fsdp", None), P("fsdp", None), P(None, "fsdp"), P("fsdp"), P(None, "fsdp"))
    data = (P(both, None, None), P(both, None, None))
    return jax.shard_map(
        local,
        mesh=mesh,
        in_specs=(*data, P(both), *six, *six, *six, P(), P(), P()),
        out_specs=(*data, *six, *six, *six, *six),
        check_vma=False,
    )
```

```python
import math
from functools import partial

import jax
import jax.numpy as jnp
from jax import lax
from jax.experimental import pallas as pl
from jax.experimental.pallas import tpu as pltpu
from jax.sharding import PartitionSpec

BF = jnp.bfloat16
F32 = jnp.float32
HEAD_DIM = 64
EPS_LN = 1e-06
LEARN_RATE = 0.2
BETA_ONE = 0.9
BETA_TWO = 0.999
ADAM_EPS = 1e-08
DECAY_RATE = 0.5
ADAM_STEPS = 10.0
GROUP = 8
PAIR = 2
EXTRA = 8
ROOT_HALF = math.sqrt(0.5)


def up(n, m):
    return (n + m - 1) // m * m


def dot(a, b, ca=1, cb=0):
    return lax.dot_general(a, b, (((ca,), (cb,)), ((), ())), preferred_element_type=F32)


def tiles(n, w):
    return [(a, min(w, n - a)) for a in range(0, n, w)]


def params(flops=0, nbytes=0):
    return dict(
        compiler_params=pltpu.CompilerParams(vmem_limit_bytes=58 << 20),
        cost_estimate=pl.CostEstimate(flops=flops, bytes_accessed=nbytes, transcendentals=0),
    )


def weave(ms, vs):
    k = 0
    for a, f in enumerate(ms):
        f()
        while k * len(ms) < len(vs) * (a + 1):
            vs[k]()
            k += 1
    for f in vs[k:]:
        f()


def norm_rows(x):
    c = x - jnp.mean(x, axis=-1, keepdims=True)
    r = lax.rsqrt(jnp.mean(c * c, axis=-1, keepdims=True) + EPS_LN)
    return c * r, r


def gelu_pair(u):
    t = 1.0 / (1.0 + (0.3275911 * ROOT_HALF) * jnp.abs(u))
    e = jnp.exp(-0.5 * (u * u))
    q = t * (0.127414796 + t * (-0.142248368 + t * (0.7107068705 + t * (-0.7265760135 + t * 0.5307027145)))) * e
    phi = jnp.where(u >= 0, 1.0 - q, q)
    return u * phi, phi + u * e * 0.3989422804014327


def full(a):
    return pl.BlockSpec(a.shape, lambda *_: (0,) * len(a.shape))


def whole(*shape):
    return pl.BlockSpec(shape, lambda *_: (0,) * len(shape))


def spread(src, dst, seq):
    for t, n in tiles(seq, 20):
        x = src[t : t + n].astype(F32).reshape(n * GROUP, src.shape[2])
        for c in range(dst.shape[0]):
            dst[c, t * GROUP : (t + n) * GROUP, :] = x[:, c * 128 : (c + 1) * 128]


def image(ref, i, t, n):
    return jnp.concatenate(
        [ref[c, pl.ds(t * GROUP + i, n, stride=GROUP), :] for c in range(ref.shape[0])], axis=1
    )


def token(ref, t, tp):
    return jnp.concatenate(
        [ref[c, pl.ds(t, GROUP, stride=tp), :] for c in range(ref.shape[0])], axis=1
    )


def tokens(ref, t, tp):
    return jnp.stack([token(ref, t, tp), token(ref, t + 1, tp)])


def pack_body(r, wq_ref, vec_ref, b_ref, w1_ref, w2_ref, wp_ref, a_ref, b_out, sm):
    FF = w1_ref.shape[1]
    a_ref[0:r, :] = wq_ref[...].astype(BF)
    sm[...] = jnp.zeros_like(sm)
    sm[0 : vec_ref.shape[0], 0 : vec_ref.shape[1]] = vec_ref[...]
    sm[6:7, 0 : b_ref.shape[1]] = b_ref[...]
    a_ref[r : r + EXTRA, :] = sm[...].astype(BF)
    b_out[:, 0:FF] = w1_ref[...].astype(BF)
    b_out[:, FF : 2 * FF] = w2_ref[...].astype(BF)
    b_out[:, 2 * FF :] = wp_ref[...].astype(BF)


def pack(wq, vec, b, w1, w2t, wp):
    r, W3 = wq.shape
    FF = w1.shape[1]
    C = 2 * FF + wp.shape[1]
    return pl.pallas_call(
        partial(pack_body, r),
        out_shape=[jax.ShapeDtypeStruct((r + EXTRA, W3), BF), jax.ShapeDtypeStruct((r, C), BF)],
        scratch_shapes=[pltpu.VMEM((EXTRA, W3), F32)],
        name="pack",
        **params(),
    )(wq, vec, b, w1, w2t, wp)


def norm_body(SEQ, D, x_ref, xh_ref, r_ref, xs):
    j = pl.program_id(1)

    @pl.when(j == 0)
    def _():
        spread(x_ref, xs, SEQ)

    for i in range(PAIR):
        for t, n in tiles(SEQ, 48):
            xh, r = norm_rows(image(xs, j * PAIR + i, t, n))
            xh_ref[i, t : t + n, :] = xh
            r_ref[i, t : t + n, :] = jnp.broadcast_to(r, (n, 128))


def norm(x):
    SEQ, N, D = x.shape
    SP = up(SEQ, 16)
    tok = pl.BlockSpec((SEQ, GROUP, D), lambda g, j: (0, g, 0))
    img = lambda d: pl.BlockSpec((PAIR, SP, d), lambda g, j: (g * (GROUP // PAIR) + j, 0, 0))
    return pl.pallas_call(
        partial(norm_body, SEQ, D),
        grid=(N // GROUP, GROUP // PAIR),
        in_specs=[tok],
        out_specs=[img(D), img(128)],
        out_shape=[jax.ShapeDtypeStruct((N, SP, d), F32) for d in (D, 128)],
        scratch_shapes=[pltpu.VMEM((D // 128, SEQ * GROUP, 128), F32)],
        name="norm",
        **params(8 * 10**9, 15 * 10**6),
    )(x)


def attend_body(SEQ, SP, TP, D, np_, me_ref, xh_ref, *refs):
    H = D // HEAD_DIM
    g = pl.program_id(0)
    j = pl.program_id(1)
    if np_:
        pieces, refs = refs[:np_], refs[np_:]
        qkv_ref, o_ref, l_ref, a_ref, w_ref, vec_ref, c1_ref, sm = refs[:8]
        refs = refs[8:]
    else:
        w_ref, vec_ref, qkv_ref, o_ref, l_ref, a_ref = refs[:6]
        refs = refs[6:]
    os_, a_scr, s0, s1, p0, p1 = refs

    @pl.when((g == 0) & (j == 0))
    def _():
        for ref in (a_scr, p0, p1, os_):
            ref[...] = jnp.zeros_like(ref)
        if np_:
            r = pieces[0].shape[0] - EXTRA
            for k in range(np_):
                s = me_ref[0] ^ k
                w_ref[pl.ds(pl.multiple_of(s * r, 16), r), :] = pieces[k][0:r, :]
                sm[s] = pieces[k][r : r + EXTRA, 0 : sm.shape[2]].astype(F32)
            nb = c1_ref.shape[1] // np_
            vec_ref[...] = jnp.concatenate([sm[s, :, 0:r] for s in range(np_)], axis=1)
            c1_ref[...] = jnp.broadcast_to(
                jnp.concatenate([sm[s, 6:7, 0:nb] for s in range(np_)], axis=1), c1_ref.shape
            )

    gain = vec_ref[0:1, :]
    shift = vec_ref[1:2, :]
    ss = (s0, s1)
    pp = (p0, p1)
    st = {}
    S8 = SEQ // 8 * 8

    def ln(i, t, n):
        y = (xh_ref[i, t : t + n, :] * gain + shift).astype(BF)
        a_scr[i * SP + t : i * SP + t + n, :] = y
        a_ref[i, t : t + n, :] = y

    def qkv(i, t, c, w):
        y = dot(a_scr[i * SP : (i + 1) * SP, :], w_ref[:, t * D + c : t * D + c + w])
        if t == 0:
            y = y * (HEAD_DIM**-0.5)
        qkv_ref[i, :, t * D + c : t * D + c + w] = y.astype(BF)

    def score(u):
        i, h = divmod(u, H)
        lo = h * HEAD_DIM
        ss[u % 2][...] = dot(
            qkv_ref[i, :, D + lo : D + lo + HEAD_DIM], qkv_ref[i, :, lo : lo + HEAD_DIM], 1, 1
        )

    def tile(ref, t, n):
        x = ref[t : t + n, :]
        if t + n > SEQ:
            x = jnp.where(lax.broadcasted_iota(jnp.int32, (n, 1), 0) < SEQ - t, x, -1e30)
        return x

    def vmax(u, t, n):
        m = jnp.max(tile(ss[u % 2], t, n).reshape(n // 8, 8, SP), axis=0)
        st[u] = m if t == 0 else jnp.maximum(st[u], m)
        if t + n >= SEQ:
            st[u] = jnp.max(st[u], axis=0, keepdims=True)

    def vexp(u, t, n):
        i, h = divmod(u, H)
        p = jnp.exp(tile(ss[u % 2], t, n) - st[u])
        ss[u % 2][t : t + n, :] = p
        total = jnp.sum(p.reshape(n // 8, 8, SP), axis=0)
        k = ("l", u)
        st[k] = total if t == 0 else st[k] + total
        if t + n >= SEQ:
            total = jnp.sum(st[k], axis=0, keepdims=True)
            l_ref[i, h : h + 1, :] = st[u] + jnp.log(total)
            st[k] = 1.0 / total

    def vnorm(u, t, n):
        pp[u % 2][t : t + n, :] = (ss[u % 2][t : t + n, :] * st[("l", u)]).astype(BF)

    def mix(u):
        i, h = divmod(u, H)
        lo = 2 * D + h * HEAD_DIM
        y = dot(pp[u % 2][...], qkv_ref[i, :, lo : lo + HEAD_DIM], 0, 0)
        if h % 2 == 0:
            st["o"] = y
        else:
            y = jnp.concatenate([st["o"], y], axis=1)
            os_[h // 2, pl.ds(pl.multiple_of((j * PAIR + i) * TP, 8), SEQ), :] = y[:SEQ]

    rows = tiles(SEQ, 48)
    for t, n in rows:
        ln(0, t, n)
    c0 = min(256, D)
    cs = tiles(D, 256)
    weave([partial(qkv, 0, t, 0, c0) for t in range(3)], [partial(ln, 1, t, n) for t, n in rows])
    rest = [partial(qkv, 0, t, c, w) for c, w in cs[1:] for t in range(3)]
    rest += [partial(qkv, 1, t, c, w) for c, w in cs for t in range(3)]
    srows = tiles(S8, 64) + ([(S8, 8)] if S8 < SEQ else [])
    nu = PAIR * H
    score(0)
    done = 0
    for k in range(nu):
        ms = []
        need = 3 if k < 2 else 2
        ms += rest[done : done + need]
        done += need
        if k + 1 < nu:
            ms.append(partial(score, k + 1))
        if k >= 1:
            ms.append(partial(mix, k - 1))
        vs = [partial(f, k, t, n) for f in (vmax, vexp, vnorm) for t, n in srows]
        weave(ms, vs)
    assert done >= len(rest)
    mix(nu - 1)
    for i in range(PAIR):
        a_ref[i, SEQ:SP, :] = jnp.zeros((SP - SEQ, D), BF)

    @pl.when(j == pl.num_programs(1) - 1)
    def _():
        for t in range(0, TP, 2):
            o_ref[t : t + 2] = tokens(os_, t, TP).astype(BF)


def attend(me, xh, pieces, w, vec, FF, SEQ, TP):
    N, SP, D = xh.shape
    W3 = 3 * D
    np_ = len(pieces)
    tok = lambda t: pl.BlockSpec((t, GROUP, D), lambda g, j, *_: (0, g, 0))
    img = lambda r, d: pl.BlockSpec((PAIR, r, d), lambda g, j, *_: (g * (GROUP // PAIR) + j, 0, 0))
    v = pltpu.VMEM
    s = jax.ShapeDtypeStruct
    ins = list(pieces) if np_ else [w, vec]
    out_specs = [img(SP, W3), tok(TP), img(8, SP), img(SP, D)]
    out_shape = [s((N, SP, W3), BF), s((TP, N, D), BF), s((N, 8, SP), F32), s((N, SP, D), BF)]
    scratch = [v((D // 128, TP * GROUP, 128), F32), v((PAIR * SP, D), BF)]
    scratch += [v((SP, SP), F32)] * 2 + [v((SP, SP), BF)] * 2
    if np_:
        out_specs += [whole(D, W3), whole(8, D), whole(8, FF)]
        out_shape += [s((D, W3), BF), s((8, D), F32), s((8, FF), F32)]
        scratch = [v((np_, EXTRA, up(max(FF, D) // np_, 128)), F32)] + scratch
    return pl.pallas_call(
        partial(attend_body, SEQ, SP, TP, D, np_),
        grid_spec=pltpu.PrefetchScalarGridSpec(
            num_scalar_prefetch=1,
            grid=(N // GROUP, GROUP // PAIR),
            in_specs=[img(SP, D)] + [full(a) for a in ins],
            out_specs=out_specs,
            scratch_shapes=scratch,
        ),
        out_shape=out_shape,
        name="attend",
        **params(20 * 10**9, 25 * 10**6),
    )(me, xh, *ins)


def feed_body(SEQ, D, FF, T, N, np_, me_ref, cnt_ref, x_ref, o_ref, cot_ref, c1_ref, vec_ref, *refs):
    s = pl.program_id(0)
    R = T * N
    RT = 2 * N
    HR = R // 2
    if np_:
        pieces, refs = refs[:np_], refs[np_:]
        out_ref, dx1_ref, do_ref, tc1_ref, tv_ref, snd_ref, keep_ref = refs[:7]
        wp_ref, w1_ref, w2t_ref, tp_ref, t1_ref, t2_ref = refs[7:13]
        refs = refs[13:]
    else:
        wp_ref, w1_ref, w2t_ref, out_ref, dx1_ref, do_ref, tc1_ref, tv_ref, tp_ref, t1_ref, t2_ref = refs[:11]
        refs = refs[11:]
    b_scr, bt_scr, dy_scr, dyt_scr, xh_scr, r_scr, x1_scr, u0, u1, d0, d1, g_scr, du_scr, y_scr, db_scr, dx_scr = refs

    @pl.when(s == 0)
    def _():
        for ref in (tp_ref, t1_ref, t2_ref, tc1_ref, tv_ref):
            ref[...] = jnp.zeros_like(ref)
        if np_:
            r = pieces[0].shape[0]
            for k in range(np_):
                at = pl.ds(pl.multiple_of((me_ref[0] ^ k) * r, 16), r)
                w1_ref[at, :] = pieces[k][:, 0:FF]
                w2t_ref[at, :] = pieces[k][:, FF : 2 * FF]
                wp_ref[at, :] = pieces[k][:, 2 * FF :]

    cp = vec_ref[2:3, :]
    g2 = vec_ref[3:4, :]
    e2 = vec_ref[4:5, :]
    c2 = vec_ref[5:6, :]
    io = lax.broadcasted_iota(jnp.int32, (RT, 1), 0)
    real = lax.rem(io, N) < cnt_ref[0]
    lim = SEQ * N - s * R
    acc = {}

    def rows(ref, r):
        return ref[r // N : r // N + 2].reshape(RT, D)

    def add(key, v):
        v = jnp.sum(v.reshape(v.shape[0] // 8, 8, v.shape[1]), axis=0)
        acc[key] = v if key not in acc else acc[key] + v

    def m_proj(h):
        x1_scr[h : h + HR, :] = dot(o_ref[h // N : (h + HR) // N].reshape(HR, D), wp_ref[...])

    def v_norm(r):
        inside = (io + r) < lim
        x = jnp.where(inside, rows(x_ref, r).astype(F32), 0.0)
        dy_scr[r : r + RT, :] = jnp.where(real & inside, rows(cot_ref, r), jnp.zeros((), BF))
        x1 = x + x1_scr[r : r + RT, :] + cp
        x1_scr[r : r + RT, :] = x1 + c2
        xh, rr = norm_rows(x1)
        xh_scr[r : r + RT, :] = xh
        r_scr[r : r + RT, :] = jnp.broadcast_to(rr, (RT, 128))
        b_scr[r : r + RT, :] = (xh * g2 + e2).astype(BF)

    cols = tiles(FF, 256)
    us = (u0, u1)
    ds = (d0, d1)

    def m_u(i, h):
        c, w = cols[i]
        us[i % 2][h : h + HR, :w] = dot(b_scr[h : h + HR, :], w1_ref[:, c : c + w]) + c1_ref[0:1, c : c + w]

    def m_d(i, h):
        c, w = cols[i]
        ds[i % 2][h : h + HR, :w] = dot(dy_scr[h : h + HR, :], w2t_ref[:, c : c + w])

    def v_gelu(i, r):
        c, w = cols[i]
        ga, dg = gelu_pair(us[i % 2][r : r + 16, :w])
        g_scr[r : r + 16, c : c + w] = ga.astype(BF)
        du = ds[i % 2][r : r + 16, :w] * dg
        du_scr[r : r + 16, c : c + w] = du.astype(BF)
        add(("c1", i), du)

    def m_t1(i):
        c, w = cols[i]
        t1_ref[:, c : c + w] += dot(bt_scr[...], du_scr[:, c : c + w])

    def m_t2(i):
        c, w = cols[i]
        t2_ref[:, c : c + w] += dot(dyt_scr[...], g_scr[:, c : c + w])

    def m_y(h):
        y_scr[h : h + HR, :] = dot(g_scr[h : h + HR, :], w2t_ref[...], 1, 1)

    def m_db(h):
        db_scr[h : h + HR, :] = dot(du_scr[h : h + HR, :], w1_ref[...], 1, 1)

    def v_out(r):
        y = x1_scr[r : r + RT, :] + y_scr[r : r + RT, :]
        out_ref[r // N : r // N + 2] = jnp.where(real, y, 0.0).astype(BF).reshape(2, N, D)

    def v_back(r):
        db = db_scr[r : r + RT, :]
        xh = xh_scr[r : r + RT, :]
        dyf = dy_scr[r : r + RT, :].astype(F32)
        dxh = db * g2
        mean1 = jnp.mean(dxh, axis=-1, keepdims=True)
        mean2 = jnp.mean(dxh * xh, axis=-1, keepdims=True)
        dx = dyf + r_scr[r : r + RT, 0:1] * (dxh - mean1 - xh * mean2)
        add("g2", db * xh)
        add("e2", db)
        add("c2", dyf)
        add("cp", dx)
        dx1_ref[r // N : r // N + 2] = dx.reshape(2, N, D)
        dx_scr[r : r + RT, :] = dx.astype(BF)

    def m_do(h):
        y = dot(dx_scr[h : h + HR, :], wp_ref[...], 1, 1)
        do_ref[h // N : (h + HR) // N] = y.astype(BF).reshape(HR // N, N, D)

    def m_tp():
        tp_ref[...] += dot(o_ref[...].reshape(R, D), dx_scr[...], 0, 0)

    first = list(range(0, HR, RT))
    second = list(range(HR, R, RT))
    last = len(cols) - 1
    m_proj(0)
    weave([partial(m_proj, HR)], [partial(v_norm, r) for r in first])
    weave([partial(m_u, 0, 0), partial(m_d, 0, 0)], [partial(v_norm, r) for r in second])
    bt_scr[...] = b_scr[...].T
    dyt_scr[...] = dy_scr[...].T
    m_u(0, HR)
    m_d(0, HR)
    for i in range(len(cols)):
        ms = []
        if i < last:
            ms += [partial(f, i + 1, h) for f in (m_u, m_d) for h in (0, HR)]
        if i >= 1:
            ms += [partial(m_t1, i - 1), partial(m_t2, i - 1)]
        weave(ms, [partial(v_gelu, i, r) for r in range(0, R, 16)])
        c, w = cols[i]
        tc1_ref[:, c : c + w] += acc[("c1", i)]
    m_db(0)
    weave([partial(m_db, HR)], [partial(v_back, r) for r in first])
    weave([partial(m_y, 0), partial(m_do, 0)], [partial(v_back, r) for r in second])
    weave([partial(m_y, HR), partial(m_do, HR)], [partial(v_out, r) for r in first])
    weave([partial(m_t1, last), partial(m_t2, last), m_tp], [partial(v_out, r) for r in second])
    for i, k in ((2, "cp"), (3, "g2"), (4, "e2"), (5, "c2")):
        tv_ref[i * 8 : i * 8 + 8, :] += acc[k]

    if np_:

        @pl.when(s == pl.num_programs(0) - 1)
        def _():
            r = D // np_
            for k in range(0, np_, 2):
                for ref, flip in ((keep_ref, 0), (snd_ref, 1)):
                    at = pl.ds(pl.multiple_of((me_ref[0] ^ (k + flip)) * r, 16), r)
                    ref[k // 2, :, 0:FF] = t1_ref[at, :].astype(ref.dtype)
                    ref[k // 2, :, FF : 2 * FF] = t2_ref[at, :].astype(ref.dtype)
                    ref[k // 2, :, 2 * FF :] = tp_ref[at, :].astype(ref.dtype)


def feed(me, cnt, x, o, cot, c1, vec, pieces, weights, T):
    SEQ, N, D = x.shape
    TP = o.shape[0]
    FF = c1.shape[1]
    np_ = len(pieces)
    R = T * N
    v = pltpu.VMEM
    s = jax.ShapeDtypeStruct
    blk = pl.BlockSpec((T, N, D), lambda i, *_: (i, 0, 0))
    ins = list(pieces) if np_ else list(weights)
    out_specs = [blk, blk, blk, whole(8, FF), whole(64, D)]
    out_shape = [s((SEQ, N, D), BF), s((TP, N, D), F32), s((TP, N, D), BF), s((8, FF), F32), s((64, D), F32)]
    scratch = []
    if np_:
        shape = (np_ // 2, D // np_, 2 * FF + D)
        out_specs += [whole(*shape)] * 2
        out_shape += [s(shape, BF), s(shape, F32)]
        scratch += [v((D, D), BF), v((D, FF), BF), v((D, FF), BF), v((D, D), F32), v((D, FF), F32), v((D, FF), F32)]
    else:
        out_specs += [whole(D, D), whole(D, FF), whole(D, FF)]
        out_shape += [s((D, D), F32), s((D, FF), F32), s((D, FF), F32)]
    scratch += [v((R, D), BF), v((D, R), BF), v((R, D), BF), v((D, R), BF), v((R, D), F32), v((R, 128), F32), v((R, D), F32)]
    scratch += [v((R, 256), F32)] * 4 + [v((R, FF), BF)] * 2 + [v((R, D), F32)] * 2 + [v((R, D), BF)]
    return pl.pallas_call(
        partial(feed_body, SEQ, D, FF, T, N, np_),
        grid_spec=pltpu.PrefetchScalarGridSpec(
            num_scalar_prefetch=2,
            grid=(TP // T,),
            in_specs=[blk, blk, blk, full(c1), full(vec)] + [full(a) for a in ins],
            out_specs=out_specs,
            scratch_shapes=scratch,
        ),
        out_shape=out_shape,
        name="feed",
        **params(45 * 10**9, 30 * 10**6),
    )(me, cnt, x, o, cot, c1, vec, *ins)


def back_body(SEQ, SP, TP, D, FF, np_, DEPS, me_ref, a_ref, xh_ref, r_ref, qkv_ref, l_ref, do_ref, dx1_ref, w_ref, vec_ref, tc1_ref, tv2_ref, *refs):
    gi_ref, refs = refs[DEPS], refs[DEPS + 1 :]
    if np_:
        snd_ref, keep_ref, tq_ref, sm = refs[:4]
        gv_ref, refs = refs[4], refs[5:]
    else:
        tq_ref, gv_ref, refs = refs[0], refs[1], refs[2:]
    dos, gs, dob, at_scr, d_scr, da_scr, tv_ref, s0, s1, e0, e1, p0, p1, q0, q1 = refs
    H = D // HEAD_DIM
    W3 = 3 * D
    g = pl.program_id(0)
    j = pl.program_id(1)

    @pl.when((g == 0) & (j == 0))
    def _():
        for ref in (d_scr, p0, p1, q0, q1, dob, tq_ref, tv_ref):
            ref[...] = jnp.zeros_like(ref)

    @pl.when(j == 0)
    def _():
        spread(do_ref, dos, SEQ)

    gain = vec_ref[0:1, :]
    ss = (s0, s1)
    es = (e0, e1)
    pp = (p0, p1)
    qq = (q0, q1)
    st = {}
    S8 = SEQ // 8 * 8

    def load(i, t, n):
        dob[i * SP + t : i * SP + t + n, :] = image(dos, j * PAIR + i, t, n).astype(BF)

    def part(i, h, t):
        lo = t * D + h * HEAD_DIM
        return qkv_ref[i, :, lo : lo + HEAD_DIM]

    def dpart(i, h):
        return dob[i * SP : (i + 1) * SP, h * HEAD_DIM : (h + 1) * HEAD_DIM]

    def score(u):
        i, h = divmod(u, H)
        ss[u % 2][...] = dot(part(i, h, 1), part(i, h, 0), 1, 1)

    def dprob(u):
        i, h = divmod(u, H)
        es[u % 2][...] = dot(part(i, h, 2), dpart(i, h), 1, 1)

    def v_prob(u, t, n):
        i, h = divmod(u, H)
        p = jnp.exp(ss[u % 2][t : t + n, :] - l_ref[i, h : h + 1, :])
        if t + n > SEQ:
            p = jnp.where(lax.broadcasted_iota(jnp.int32, (n, 1), 0) < SEQ - t, p, 0.0)
        ss[u % 2][t : t + n, :] = p
        pp[u % 2][t : t + n, :] = p.astype(BF)
        x = jnp.sum((p * es[u % 2][t : t + n, :]).reshape(n // 8, 8, SP), axis=0)
        st[u] = x if t == 0 else st[u] + x
        if t + n >= SEQ:
            st[u] = jnp.sum(st[u], axis=0, keepdims=True)

    def v_ds(u, t, n):
        qq[u % 2][t : t + n, :] = (ss[u % 2][t : t + n, :] * (es[u % 2][t : t + n, :] - st[u])).astype(BF)

    def put(u, t, y):
        i, h = divmod(u, H)
        if h % 2 == 0:
            st[("d", t)] = y
        else:
            y = jnp.concatenate([st[("d", t)], y], axis=1).astype(BF)
            lo = t * D + (h - 1) * HEAD_DIM
            d_scr[i * SP : i * SP + SEQ, lo : lo + 2 * HEAD_DIM] = y[:SEQ]

    def m_dv(u):
        put(u, 2, dot(pp[u % 2][...], dpart(*divmod(u, H))))

    def m_dk(u):
        i, h = divmod(u, H)
        put(u, 1, dot(qq[u % 2][...], part(i, h, 0)))

    def m_dq(u):
        i, h = divmod(u, H)
        put(u, 0, dot(qq[u % 2][...], part(i, h, 1), 0, 0) * (HEAD_DIM**-0.5))

    rows = tiles(SEQ, 48)
    srows = tiles(S8, 64) + ([(S8, 8)] if S8 < SEQ else [])
    for t, n in rows:
        load(0, t, n)
    at_scr[...] = a_ref[...].reshape(PAIR * SP, D).T
    pre = [partial(load, 1, t, n) for t, n in rows]
    nu = PAIR * H
    score(0)
    dprob(0)
    for k in range(nu):
        ms = []
        if k + 1 < nu:
            ms += [partial(score, k + 1), partial(dprob, k + 1)]
        if k >= 1:
            ms += [partial(m_dv, k - 1), partial(m_dk, k - 1), partial(m_dq, k - 1)]
        vs = [partial(f, k, t, n) for f in (v_prob, v_ds) for t, n in srows]
        vs += pre[3 * k : 3 * k + 3]
        weave(ms, vs)
    assert 3 * nu >= len(pre)
    m_dv(nu - 1)
    m_dk(nu - 1)
    m_dq(nu - 1)
    acc = {}

    def m_da(i):
        da_scr[i * SP : (i + 1) * SP, :] = dot(d_scr[i * SP : (i + 1) * SP, :], w_ref[...], 1, 1)

    def m_tq(c, w):
        tq_ref[:, c : c + w] += dot(at_scr[...], d_scr[:, c : c + w])

    def add(key, v):
        f = v.shape[0] // 8 * 8
        if f:
            x = jnp.sum(v[:f].reshape(f // 8, 8, D), axis=0)
            acc[key] = x if key not in acc else acc[key] + x
        if f < v.shape[0]:
            x = jnp.sum(v[f:], axis=0, keepdims=True)
            key = key + "tail"
            acc[key] = x if key not in acc else acc[key] + x

    def v_back(i, t, n):
        at = slice(i * SP + t, i * SP + t + n)
        d = da_scr[at, :]
        xh = xh_ref[i, t : t + n, :]
        dxh = d * gain
        mean1 = jnp.mean(dxh, axis=-1, keepdims=True)
        mean2 = jnp.mean(dxh * xh, axis=-1, keepdims=True)
        y = r_ref[i, t : t + n, 0:1] * (dxh - mean1 - xh * mean2)
        for c in range(gs.shape[0]):
            gs[c, pl.ds(pl.multiple_of((j * PAIR + i) * TP + t, 8), n), :] = y[:, c * 128 : (c + 1) * 128]
        add("g", d * xh)
        add("e", d)

    cols = tiles(W3, 256)
    m_da(0)
    weave([partial(m_da, 1)] + [partial(m_tq, c, w) for c, w in cols[:2]], [partial(v_back, 0, t, n) for t, n in rows])
    weave([partial(m_tq, c, w) for c, w in cols[2:]], [partial(v_back, 1, t, n) for t, n in rows])
    tv_ref[0:8, :] += acc["g"]
    tv_ref[8:16, :] += acc["e"]
    if "gtail" in acc:
        tv_ref[0:1, :] += acc["gtail"]
        tv_ref[8:9, :] += acc["etail"]

    @pl.when(j == pl.num_programs(1) - 1)
    def _():
        for t in range(0, SEQ - 1, 2):
            gi_ref[t : t + 2] = (tokens(gs, t, TP) + dx1_ref[t : t + 2]).astype(BF)
        if SEQ % 2:
            gi_ref[SEQ - 1] = (token(gs, SEQ - 1, TP) + dx1_ref[SEQ - 1]).astype(BF)

    @pl.when((j == pl.num_programs(1) - 1) & (g == pl.num_programs(0) - 1))
    def _():
        for i in range(2):
            gv_ref[i : i + 1, :] = jnp.sum(tv_ref[8 * i : 8 * i + 8, :], axis=0, keepdims=True)
        for i in range(2, 6):
            gv_ref[i : i + 1, :] = jnp.sum(tv2_ref[8 * i : 8 * i + 8, :], axis=0, keepdims=True)
        if np_:
            r = D // np_
            nb = FF // np_
            sm[...] = jnp.zeros_like(sm)
            bias = jnp.sum(tc1_ref[...], axis=0, keepdims=True)
            for s in range(np_):
                sm[s, 0:6, 0:r] = gv_ref[0:6, s * r : (s + 1) * r]
                sm[s, 6:7, 0:nb] = bias[:, s * nb : (s + 1) * nb]
            wide = sm.shape[2]
            for k in range(0, np_, 2):
                for ref, flip in ((keep_ref, 0), (snd_ref, 1)):
                    s = me_ref[0] ^ (k + flip)
                    ref[k // 2, 0:r, :] = tq_ref[pl.ds(pl.multiple_of(s * r, 16), r), :].astype(ref.dtype)
                    ref[k // 2, r : r + EXTRA, 0:wide] = sm[s].astype(ref.dtype)
                    ref[k // 2, r : r + EXTRA, wide:] = jnp.zeros((EXTRA, W3 - wide), ref.dtype)


def back(me, a, xh, r, qkv, l, do, dx1, w, vec, tc1, tv2, deps, SEQ, np_):
    N, SP, D = a.shape
    TP = do.shape[0]
    W3 = 3 * D
    FF = tc1.shape[1]
    R = PAIR * SP
    tok = lambda t: pl.BlockSpec((t, GROUP, D), lambda g, j, *_: (0, g, 0))
    img = lambda r, d: pl.BlockSpec((PAIR, r, d), lambda g, j, *_: (g * (GROUP // PAIR) + j, 0, 0))
    v = pltpu.VMEM
    s = jax.ShapeDtypeStruct
    out_specs = [tok(SEQ)]
    out_shape = [s((SEQ, N, D), BF)]
    if np_:
        shape = (np_ // 2, D // np_ + EXTRA, W3)
        out_specs += [whole(*shape)] * 2
        out_shape += [s(shape, BF), s(shape, F32)]
        scratch = [v((D, W3), F32), v((np_, EXTRA, up(max(FF, D) // np_, 128)), F32), v((8, D), F32)]
    else:
        out_specs += [whole(D, W3), whole(8, D)]
        out_shape += [s((D, W3), F32), s((8, D), F32)]
        scratch = []
    scratch += [v((D // 128, TP * GROUP, 128), F32)] * 2
    scratch += [v((R, D), BF), v((D, R), BF), v((R, W3), BF), v((R, D), F32)]
    scratch += [v((16, D), F32)] + [v((SP, SP), F32)] * 4 + [v((SP, SP), BF)] * 4
    return pl.pallas_call(
        partial(back_body, SEQ, SP, TP, D, FF, np_, len(deps)),
        grid_spec=pltpu.PrefetchScalarGridSpec(
            num_scalar_prefetch=1,
            grid=(N // GROUP, GROUP // PAIR),
            in_specs=[img(SP, D), img(SP, D), img(SP, 128), img(SP, W3), img(8, SP), tok(TP), tok(TP)]
            + [full(w), full(vec), full(tc1), full(tv2)]
            + [pl.BlockSpec(memory_space=pl.ANY)] * len(deps),
            out_specs=out_specs,
            scratch_shapes=scratch,
        ),
        out_shape=out_shape,
        name="back",
        **params(40 * 10**9, 30 * 10**6),
    )(me, a, xh, r, qkv, l, do, dx1, w, vec, tc1, tv2, *deps)


def adam_body(np_, count, slots, where, flag_ref, gid_ref, scale_ref, *refs):
    pieces, refs = refs[:np_], refs[np_:]
    weights, firsts, seconds, outs = refs[:count], refs[count : 2 * count], refs[2 * count : 3 * count], refs[3 * count :]
    for k, (p, row, col) in enumerate(where):
        r, c = weights[k].shape
        xs = [x[row : row + r, col : col + c].astype(F32) for x in pieces]
        grad = (xs[0] if len(xs) == 1 else (xs[0] + xs[1]) + (xs[2] + xs[3])) / slots
        flag = flag_ref[p].astype(F32)
        lr = scale_ref[gid_ref[p]]
        first = BETA_ONE * firsts[k][...] + (1.0 - BETA_ONE) * grad
        second = BETA_TWO * seconds[k][...] + (1.0 - BETA_TWO) * grad * grad
        direction = first / (1.0 - BETA_ONE**ADAM_STEPS) / (jnp.sqrt(second / (1.0 - BETA_TWO**ADAM_STEPS)) + ADAM_EPS)
        weight = weights[k][...]
        outs[k][...] = grad
        outs[count + k][...] = weight - LEARN_RATE * lr * (direction + DECAY_RATE * flag * weight)
        outs[2 * count + k][...] = first
        outs[3 * count + k][...] = second


def adam(flags, gids, scales, pieces, arrays, slots, where):
    smem = pl.BlockSpec(memory_space=pltpu.SMEM)
    vmem = pl.BlockSpec(memory_space=pltpu.VMEM)
    mine = [[xs[p] for p, _, _ in where] for xs in arrays]
    shapes = [jax.ShapeDtypeStruct(w.shape, F32) for w in mine[0]]
    return pl.pallas_call(
        partial(adam_body, len(pieces), len(where), slots, where),
        in_specs=[smem] * 3 + [vmem] * (len(pieces) + 3 * len(where)),
        out_specs=[vmem] * (4 * len(where)),
        out_shape=shapes * 4,
        name="adam",
        **params(10**9, 5 * 10**6),
    )(flags, gids, scales, *pieces, *mine[0], *mine[1], *mine[2])


def pairs(n, k):
    return [(i, i ^ k) for i in range(n)]


def touch_body(*refs):
    pass


def touch(dep, xs):
    spec = pl.BlockSpec(memory_space=pl.ANY)
    return pl.pallas_call(
        touch_body,
        in_specs=[spec] * (len(xs) + 1),
        out_specs=[spec] * len(xs),
        out_shape=[jax.ShapeDtypeStruct(x.shape, x.dtype) for x in xs],
        input_output_aliases={k: k for k in range(len(xs))},
        name="touch",
    )(*xs, dep)


def fetch(x, n):
    return [x] + [lax.ppermute(x, "fsdp", pairs(n, k)) for k in range(2, n, 2)]


def fetch_core(own, n):
    other = [lax.ppermute(x, "fsdp", pairs(n, 1)) for x in own]
    return [x for both in zip(own, other) for x in both]


def halve(snd, keep, n):
    h = keep + lax.ppermute(snd, "fsdp", pairs(n, 1)).astype(F32)
    return h[0], [h[k].astype(BF) for k in range(1, n // 2)]


def along_z(xs, n):
    return [lax.ppermute(x, "fsdp", pairs(n, 2 * k + 2)) for k, x in enumerate(xs)]


def finish(own, got, d):
    for piece in got:
        own = own + piece.astype(F32)
    b = own.astype(BF)
    return [b] + [lax.ppermute(b, "dp", pairs(d, k)) for k in range(1, d)]


def local(
    images, cotangent, counts,
    w_qkv, w_proj, w_fc1, w_fc2, b_fc1, vectors,
    m_qkv, m_proj, m_fc1, m_fc2, m_bias1, m_vectors,
    v_qkv, v_proj, v_fc1, v_fc2, v_bias1, v_vectors,
    decay_flags, group_ids, group_scales,
):
    n = lax.axis_size("fsdp")
    d = lax.axis_size("dp")
    N, SEQ, D = images.shape
    r = w_qkv.shape[0]
    FF = w_fc1.shape[1]
    T = 20
    TP = up(SEQ, T)
    direct = n in (2, 4, 8) and d == 4 and r % 16 == 0
    x = jnp.transpose(images, (1, 0, 2))
    cot = jnp.transpose(cotangent, (1, 0, 2))
    me = lax.axis_index("fsdp").astype(jnp.int32).reshape(1)
    rows = lambda b: b.reshape(1, -1)
    weights = [w_qkv, w_proj, w_fc1, w_fc2.T, rows(b_fc1), vectors]
    firsts = [m_qkv, m_proj, m_fc1, m_fc2.T, rows(m_bias1), m_vectors]
    seconds = [v_qkv, v_proj, v_fc1, v_fc2.T, rows(v_bias1), v_vectors]
    pack_a, pack_b = pack(weights[0], weights[5], weights[4], weights[2], weights[3], weights[1])
    xh, rf = norm(x)
    if direct:
        half_a = touch(rf, fetch(pack_a, n))
        pieces_a = fetch_core(half_a, n)
        half_b = fetch(touch(half_a[-1], [pack_b])[0], n)
        qkv, o, logs, a, wq, vec, c1 = attend(me, xh, pieces_a, None, None, FF, SEQ, TP)
        pieces_b = fetch_core(touch(vec, half_b), n)
        out, dx1, do, tc1, tv2, snd, keep = feed(me, counts, x, o, cot, c1, vec, pieces_b, (), T)
        own_b, sends = halve(snd, keep, n)
        got_b = along_z(sends, n)
        gi, snd, keep = back(me, a, xh, rf, qkv, logs, do, dx1, wq, vec, tc1, tv2, sends, SEQ, n)
        snd, *got_b = touch(vec, [snd, *got_b])
        own_a, sends = halve(snd, keep, n)
        got_a = along_z(sends, n)
        pb = finish(own_b, got_b, d)
        pa = finish(own_a, got_a, d)
    else:
        all_a = lax.all_gather(pack_a, "fsdp", axis=0, tiled=False)
        all_b = lax.all_gather(pack_b, "fsdp", axis=0, tiled=True)
        wq = all_a[:, :r].reshape(D, 3 * D)
        nb = FF // n
        vec = jnp.transpose(all_a[:, r : r + 8, :r], (1, 0, 2)).reshape(8, D).astype(F32)
        c1 = jnp.broadcast_to(all_a[:, r + 6, :nb].reshape(1, FF), (8, FF)).astype(F32)
        ws = (all_b[:, 2 * FF :], all_b[:, :FF], all_b[:, FF : 2 * FF])
        qkv, o, logs, a = attend(me, xh, (), wq, vec, FF, SEQ, TP)
        out, dx1, do, tc1, tv2, tp, t1, t2 = feed(me, counts, x, o, cot, c1, vec, (), ws, T)
        gi, tq, gv = back(me, a, xh, rf, qkv, logs, do, dx1, wq, vec, tc1, tv2, (), SEQ, 0)
        share = lambda g, axis: lax.psum(
            lax.psum_scatter(g, "fsdp", scatter_dimension=axis, tiled=True).astype(BF), "dp"
        ).astype(F32)
        pb = [share(jnp.concatenate([t1, t2, tp], axis=1), 0)]
        small = jnp.zeros((8, 3 * D), F32).at[:6, :r].set(share(gv[:6], 1))
        small = small.at[6, :nb].set(share(jnp.sum(tc1, axis=0), 0))
        pa = [jnp.concatenate([share(tq, 0), small], axis=0)]
    arrays = (weights, firsts, seconds)
    slots = float(N * n * d)
    where_a = ((0, 0, 0), (4, r + 6, 0), (5, r, 0))
    where_b = ((1, 0, 2 * FF), (2, 0, 0), (3, 0, FF))
    res = [None] * 24
    for pieces, where in ((pb, where_b), (pa, where_a)):
        got = adam(decay_flags, group_ids, group_scales, pieces, arrays, slots, where)
        for j in range(4):
            for k, (p, _, _) in enumerate(where):
                res[6 * j + p] = got[3 * j + k]
    for k in range(4):
        res[6 * k + 3] = res[6 * k + 3].T
        res[6 * k + 4] = res[6 * k + 4].reshape(-1)
    return (jnp.transpose(out, (1, 0, 2)), jnp.transpose(gi, (1, 0, 2)), *res)


def solution(mesh):
    P = PartitionSpec
    both = ("dp", "fsdp")
    six = (P("fsdp", None), P("fsdp", None), P("fsdp", None), P(None, "fsdp"), P("fsdp"), P(None, "fsdp"))
    data = (P(both, None, None), P(both, None, None))
    return jax.shard_map(
        local,
        mesh=mesh,
        in_specs=(*data, P(both), *six, *six, *six, P(), P(), P()),
        out_specs=(*data, *six, *six, *six, *six),
        check_vma=False,
    )
```

```python
import math
from functools import partial

import jax
import jax.numpy as jnp
from jax import lax
from jax.experimental import pallas as pl
from jax.experimental.pallas import tpu as pltpu
from jax.sharding import PartitionSpec

BF = jnp.bfloat16
F32 = jnp.float32
HEAD_DIM = 64
EPS_LN = 1e-06
LEARN_RATE = 0.2
BETA_ONE = 0.9
BETA_TWO = 0.999
ADAM_EPS = 1e-08
DECAY_RATE = 0.5
ADAM_STEPS = 10.0
GROUP = 8
PAIR = 4
EXTRA = 8
ROOT_HALF = math.sqrt(0.5)


def up(n, m):
    return (n + m - 1) // m * m


def dot(a, b, ca=1, cb=0):
    return lax.dot_general(a, b, (((ca,), (cb,)), ((), ())), preferred_element_type=F32)


def tiles(n, w):
    return [(a, min(w, n - a)) for a in range(0, n, w)]


def params(flops=0, nbytes=0):
    return dict(
        compiler_params=pltpu.CompilerParams(vmem_limit_bytes=58 << 20),
        cost_estimate=pl.CostEstimate(flops=flops, bytes_accessed=nbytes, transcendentals=0),
    )


def weave(ms, vs):
    k = 0
    for a, f in enumerate(ms):
        f()
        while k * len(ms) < len(vs) * (a + 1):
            vs[k]()
            k += 1
    for f in vs[k:]:
        f()


def norm_rows(x):
    c = x - jnp.mean(x, axis=-1, keepdims=True)
    r = lax.rsqrt(jnp.mean(c * c, axis=-1, keepdims=True) + EPS_LN)
    return c * r, r


def gelu_pair(u):
    phi = 0.5 + 0.5 * lax.erf(u * ROOT_HALF)
    e = jnp.exp2((-0.5 * math.log2(math.e)) * (u * u))
    return u * phi, phi + (u * (1.0 / math.sqrt(2.0 * math.pi))) * e


def full(a):
    return pl.BlockSpec(a.shape, lambda *_: (0,) * len(a.shape))


def whole(*shape):
    return pl.BlockSpec(shape, lambda *_: (0,) * len(shape))


def spread(src, dst, seq):
    for t, n in tiles(seq, 20):
        x = src[t : t + n].astype(F32).reshape(n * GROUP, src.shape[2])
        for c in range(dst.shape[0]):
            dst[c, t * GROUP : (t + n) * GROUP, :] = x[:, c * 128 : (c + 1) * 128]


def image(ref, i, t, n):
    return jnp.concatenate(
        [ref[c, pl.ds(t * GROUP + i, n, stride=GROUP), :] for c in range(ref.shape[0])], axis=1
    )


def token(ref, t, tp):
    return jnp.concatenate(
        [ref[c, pl.ds(t, GROUP, stride=tp), :] for c in range(ref.shape[0])], axis=1
    )


def tokens(ref, t, tp):
    return jnp.stack([token(ref, t, tp), token(ref, t + 1, tp)])


def pack_body(r, wq_ref, vec_ref, b_ref, w1_ref, w2_ref, wp_ref, a_ref, b_out, sm):
    FF = w1_ref.shape[1]
    a_ref[0:r, :] = wq_ref[...].astype(BF)
    sm[...] = jnp.zeros_like(sm)
    sm[0 : vec_ref.shape[0], 0 : vec_ref.shape[1]] = vec_ref[...]
    sm[6:7, 0 : b_ref.shape[1]] = b_ref[...]
    a_ref[r : r + EXTRA, :] = sm[...].astype(BF)
    b_out[:, 0:FF] = w1_ref[...].astype(BF)
    b_out[:, FF : 2 * FF] = w2_ref[...].astype(BF)
    b_out[:, 2 * FF :] = wp_ref[...].astype(BF)


def pack(wq, vec, b, w1, w2t, wp):
    r, W3 = wq.shape
    FF = w1.shape[1]
    C = 2 * FF + wp.shape[1]
    return pl.pallas_call(
        partial(pack_body, r),
        out_shape=[jax.ShapeDtypeStruct((r + EXTRA, W3), BF), jax.ShapeDtypeStruct((r, C), BF)],
        scratch_shapes=[pltpu.VMEM((EXTRA, W3), F32)],
        name="pack",
        **params(),
    )(wq, vec, b, w1, w2t, wp)


def norm_body(SEQ, D, x_ref, xh_ref, r_ref, xs):
    j = pl.program_id(1)

    @pl.when(j == 0)
    def _():
        spread(x_ref, xs, SEQ)

    for i in range(PAIR):
        for t, n in tiles(SEQ, 48):
            xh, r = norm_rows(image(xs, j * PAIR + i, t, n))
            xh_ref[i, t : t + n, :] = xh
            r_ref[i, t : t + n, :] = jnp.broadcast_to(r, (n, 128))


def norm(x):
    SEQ, N, D = x.shape
    SP = up(SEQ, 16)
    tok = pl.BlockSpec((SEQ, GROUP, D), lambda g, j: (0, g, 0))
    img = lambda d: pl.BlockSpec((PAIR, SP, d), lambda g, j: (g * (GROUP // PAIR) + j, 0, 0))
    return pl.pallas_call(
        partial(norm_body, SEQ, D),
        grid=(N // GROUP, GROUP // PAIR),
        in_specs=[tok],
        out_specs=[img(D), img(128)],
        out_shape=[jax.ShapeDtypeStruct((N, SP, d), F32) for d in (D, 128)],
        scratch_shapes=[pltpu.VMEM((D // 128, up(SEQ, 8) * GROUP, 128), F32)],
        name="norm",
        **params(8 * 10**9, 15 * 10**6),
    )(x)


def attend_body(SEQ, SP, TP, D, np_, me_ref, xh_ref, *refs):
    H = D // HEAD_DIM
    g = pl.program_id(0)
    j = pl.program_id(1)
    if np_:
        pieces, refs = refs[:np_], refs[np_:]
        qkv_ref, o_ref, l_ref, a_ref, w_ref, vec_ref, c1_ref, sm = refs[:8]
        refs = refs[8:]
    else:
        w_ref, vec_ref, qkv_ref, o_ref, l_ref, a_ref = refs[:6]
        refs = refs[6:]
    os_, a_scr, s0, s1, p0, p1 = refs

    @pl.when((g == 0) & (j == 0))
    def _():
        for ref in (a_scr, p0, p1, os_):
            ref[...] = jnp.zeros_like(ref)
        if np_:
            r = pieces[0].shape[0] - EXTRA
            for k in range(np_):
                s = me_ref[0] ^ k
                w_ref[pl.ds(pl.multiple_of(s * r, 16), r), :] = pieces[k][0:r, :]
                sm[s] = pieces[k][r : r + EXTRA, 0 : sm.shape[2]].astype(F32)
            nb = c1_ref.shape[1] // np_
            vec_ref[...] = jnp.concatenate([sm[s, :, 0:r] for s in range(np_)], axis=1)
            c1_ref[...] = jnp.broadcast_to(
                jnp.concatenate([sm[s, 6:7, 0:nb] for s in range(np_)], axis=1), c1_ref.shape
            )

    gain = vec_ref[0:1, :]
    shift = vec_ref[1:2, :]
    ss = (s0, s1)
    pp = (p0, p1)
    st = {}
    S8 = SEQ // 8 * 8

    def ln(i, t, n):
        y = (xh_ref[i, t : t + n, :] * gain + shift).astype(BF)
        a_scr[i * SP + t : i * SP + t + n, :] = y
        a_ref[i, t : t + n, :] = y

    def qkv(t, c, w):
        y = dot(a_scr[...], w_ref[:, t * D + c : t * D + c + w])
        if t == 0:
            y = y * (HEAD_DIM**-0.5)
        qkv_ref[:, :, t * D + c : t * D + c + w] = y.astype(BF).reshape(PAIR, SP, w)

    def score(u):
        i, h = divmod(u, H)
        lo = h * HEAD_DIM
        ss[u % 2][...] = dot(
            qkv_ref[i, :, D + lo : D + lo + HEAD_DIM], qkv_ref[i, :, lo : lo + HEAD_DIM], 1, 1
        )

    def tile(ref, t, n):
        x = ref[t : t + n, :]
        if t + n > SEQ:
            x = jnp.where(lax.broadcasted_iota(jnp.int32, (n, 1), 0) < SEQ - t, x, -1e30)
        return x

    def vmax(u, t, n):
        m = jnp.max(tile(ss[u % 2], t, n).reshape(n // 8, 8, SP), axis=0)
        st[u] = m if t == 0 else jnp.maximum(st[u], m)
        if t + n >= SEQ:
            st[u] = jnp.max(st[u], axis=0, keepdims=True)

    def vexp(u, t, n):
        i, h = divmod(u, H)
        p = jnp.exp(tile(ss[u % 2], t, n) - st[u])
        ss[u % 2][t : t + n, :] = p
        total = jnp.sum(p.reshape(n // 8, 8, SP), axis=0)
        k = ("l", u)
        st[k] = total if t == 0 else st[k] + total
        if t + n >= SEQ:
            total = jnp.sum(st[k], axis=0, keepdims=True)
            l_ref[i, h : h + 1, :] = st[u] + jnp.log(total)
            st[k] = 1.0 / total

    def vnorm(u, t, n):
        pp[u % 2][t : t + n, :] = (ss[u % 2][t : t + n, :] * st[("l", u)]).astype(BF)

    def mix(u):
        i, h = divmod(u, H)
        lo = 2 * D + h * HEAD_DIM
        y = dot(pp[u % 2][...], qkv_ref[i, :, lo : lo + HEAD_DIM], 0, 0)
        if h % 2 == 0:
            st["o"] = y
        else:
            y = jnp.concatenate([st["o"], y], axis=1)
            os_[h // 2, pl.ds(pl.multiple_of((j * PAIR + i) * TP, 8), SEQ), :] = y[:SEQ]

    for i in range(PAIR):
        for t, n in tiles(SEQ, 48):
            ln(i, t, n)
    c0 = min(256, D)
    hb = c0 // HEAD_DIM
    for t in range(3):
        qkv(t, 0, c0)
    rest = [partial(qkv, t, c, w) for c, w in tiles(D, 256)[1:] for t in range(3)]
    srows = tiles(S8, 64) + ([(S8, 8)] if S8 < SEQ else [])
    order = [i * H + h for i in range(PAIR) for h in range(hb)]
    order += [i * H + h for i in range(PAIR) for h in range(hb, H)]
    nu = len(order)
    score(order[0])
    for k, u in enumerate(order):
        ms = rest[k : k + 1]
        if k + 1 < nu:
            ms.append(partial(score, order[k + 1]))
        if k >= 1:
            ms.append(partial(mix, order[k - 1]))
        vs = [partial(f, u, t, n) for f in (vmax, vexp, vnorm) for t, n in srows]
        weave(ms, vs)
    nu = order[-1] + 1
    mix(nu - 1)
    for i in range(PAIR):
        a_ref[i, SEQ:SP, :] = jnp.zeros((SP - SEQ, D), BF)

    @pl.when(j == pl.num_programs(1) - 1)
    def _():
        for t in range(0, TP, 2):
            o_ref[t : t + 2] = tokens(os_, t, TP).astype(BF)


def attend(me, xh, pieces, w, vec, FF, SEQ, TP):
    N, SP, D = xh.shape
    W3 = 3 * D
    np_ = len(pieces)
    tok = lambda t: pl.BlockSpec((t, GROUP, D), lambda g, j, *_: (0, g, 0))
    img = lambda r, d: pl.BlockSpec((PAIR, r, d), lambda g, j, *_: (g * (GROUP // PAIR) + j, 0, 0))
    v = pltpu.VMEM
    s = jax.ShapeDtypeStruct
    ins = list(pieces) if np_ else [w, vec]
    out_specs = [img(SP, W3), tok(TP), img(8, SP), img(SP, D)]
    out_shape = [s((N, SP, W3), BF), s((TP, N, D), BF), s((N, 8, SP), F32), s((N, SP, D), BF)]
    scratch = [v((D // 128, TP * GROUP, 128), F32), v((PAIR * SP, D), BF)]
    scratch += [v((SP, SP), F32)] * 2 + [v((SP, SP), BF)] * 2
    if np_:
        out_specs += [whole(D, W3), whole(8, D), whole(8, FF)]
        out_shape += [s((D, W3), BF), s((8, D), F32), s((8, FF), F32)]
        scratch = [v((np_, EXTRA, up(max(FF, D) // np_, 128)), F32)] + scratch
    return pl.pallas_call(
        partial(attend_body, SEQ, SP, TP, D, np_),
        grid_spec=pltpu.PrefetchScalarGridSpec(
            num_scalar_prefetch=1,
            grid=(N // GROUP, GROUP // PAIR),
            in_specs=[img(SP, D)] + [full(a) for a in ins],
            out_specs=out_specs,
            scratch_shapes=scratch,
        ),
        out_shape=out_shape,
        name="attend",
        **params(20 * 10**9, 25 * 10**6),
    )(me, xh, *ins)


def feed_body(SEQ, D, FF, T, N, np_, me_ref, cnt_ref, x_ref, o_ref, cot_ref, c1_ref, vec_ref, *refs):
    s = pl.program_id(0)
    R = T * N
    RT = 2 * N
    HR = R // 2
    if np_:
        pieces, refs = refs[:np_], refs[np_:]
        out_ref, dx1_ref, do_ref, tc1_ref, tv_ref, snd_ref, keep_ref = refs[:7]
        wp_ref, w1_ref, w2t_ref, tp_ref, t1_ref, t2_ref = refs[7:13]
        refs = refs[13:]
    else:
        wp_ref, w1_ref, w2t_ref, out_ref, dx1_ref, do_ref, tc1_ref, tv_ref, tp_ref, t1_ref, t2_ref = refs[:11]
        refs = refs[11:]
    b_scr, bt_scr, dy_scr, dyt_scr, xh_scr, r_scr, x1_scr, u0, u1, d0, d1, g_scr, du_scr, y_scr, db_scr, dx_scr = refs

    @pl.when(s == 0)
    def _():
        for ref in (tp_ref, t1_ref, t2_ref, tc1_ref, tv_ref):
            ref[...] = jnp.zeros_like(ref)
        if np_:
            r = pieces[0].shape[0]
            for k in range(np_):
                at = pl.ds(pl.multiple_of((me_ref[0] ^ k) * r, 16), r)
                w1_ref[at, :] = pieces[k][:, 0:FF]
                w2t_ref[at, :] = pieces[k][:, FF : 2 * FF]
                wp_ref[at, :] = pieces[k][:, 2 * FF :]

    cp = vec_ref[2:3, :]
    g2 = vec_ref[3:4, :]
    e2 = vec_ref[4:5, :]
    c2 = vec_ref[5:6, :]
    io = lax.broadcasted_iota(jnp.int32, (RT, 1), 0)
    real = lax.rem(io, N) < cnt_ref[0]
    lim = SEQ * N - s * R
    acc = {}

    def rows(ref, r):
        return ref[r // N : r // N + 2].reshape(RT, D)

    def add(key, v):
        v = jnp.sum(v.reshape(v.shape[0] // 8, 8, v.shape[1]), axis=0)
        acc[key] = v if key not in acc else acc[key] + v

    def m_proj(h):
        x1_scr[h : h + HR, :] = dot(o_ref[h // N : (h + HR) // N].reshape(HR, D), wp_ref[...])

    def v_norm(r):
        inside = (io + r) < lim
        x = jnp.where(inside, rows(x_ref, r).astype(F32), 0.0)
        dy_scr[r : r + RT, :] = jnp.where(real & inside, rows(cot_ref, r), jnp.zeros((), BF))
        x1 = x + x1_scr[r : r + RT, :] + cp
        x1_scr[r : r + RT, :] = x1 + c2
        xh, rr = norm_rows(x1)
        xh_scr[r : r + RT, :] = xh
        r_scr[r : r + RT, :] = jnp.broadcast_to(rr, (RT, 128))
        b_scr[r : r + RT, :] = (xh * g2 + e2).astype(BF)

    cols = tiles(FF, 256)
    us = (u0, u1)
    ds = (d0, d1)

    def m_u(i, h, HR=HR):
        c, w = cols[i]
        us[i % 2][h : h + HR, :w] = dot(b_scr[h : h + HR, :], w1_ref[:, c : c + w]) + c1_ref[0:1, c : c + w]

    def m_d(i, h, HR=HR):
        c, w = cols[i]
        ds[i % 2][h : h + HR, :w] = dot(dy_scr[h : h + HR, :], w2t_ref[:, c : c + w])

    def v_gelu(i, r):
        c, w = cols[i]
        ga, dg = gelu_pair(us[i % 2][r : r + 16, :w])
        g_scr[r : r + 16, c : c + w] = ga.astype(BF)
        du = ds[i % 2][r : r + 16, :w] * dg
        du_scr[r : r + 16, c : c + w] = du.astype(BF)
        add(("c1", i), du)

    def m_t1(i):
        c, w = cols[i]
        t1_ref[:, c : c + w] += dot(bt_scr[...], du_scr[:, c : c + w])

    def m_t2(i):
        c, w = cols[i]
        t2_ref[:, c : c + w] += dot(dyt_scr[...], g_scr[:, c : c + w])

    def m_y(h, HR=HR):
        y_scr[h : h + HR, :] = dot(g_scr[h : h + HR, :], w2t_ref[...], 1, 1)

    def m_db(h, HR=HR):
        db_scr[h : h + HR, :] = dot(du_scr[h : h + HR, :], w1_ref[...], 1, 1)

    def v_out(r):
        y = x1_scr[r : r + RT, :] + y_scr[r : r + RT, :]
        out_ref[r // N : r // N + 2] = jnp.where(real, y, 0.0).astype(BF).reshape(2, N, D)

    def v_back(r):
        db = db_scr[r : r + RT, :]
        xh = xh_scr[r : r + RT, :]
        dyf = dy_scr[r : r + RT, :].astype(F32)
        dxh = db * g2
        mean1 = jnp.mean(dxh, axis=-1, keepdims=True)
        mean2 = jnp.mean(dxh * xh, axis=-1, keepdims=True)
        dx = dyf + r_scr[r : r + RT, 0:1] * (dxh - mean1 - xh * mean2)
        add("g2", db * xh)
        add("e2", db)
        add("c2", dyf)
        add("cp", dx)
        dx1_ref[r // N : r // N + 2] = dx.reshape(2, N, D)
        dx_scr[r : r + RT, :] = dx.astype(BF)

    def m_do(h):
        y = dot(dx_scr[h : h + HR, :], wp_ref[...], 1, 1)
        do_ref[h // N : (h + HR) // N] = y.astype(BF).reshape(HR // N, N, D)

    def m_tp():
        tp_ref[...] += dot(o_ref[...].reshape(R, D), dx_scr[...], 0, 0)

    first = list(range(0, HR, RT))
    second = list(range(HR, R, RT))
    last = len(cols) - 1
    m_proj(0)
    weave([partial(m_proj, HR)], [partial(v_norm, r) for r in first])
    weave([partial(m_u, 0, 0), partial(m_d, 0, 0)], [partial(v_norm, r) for r in second])
    bt_scr[...] = b_scr[...].T
    dyt_scr[...] = dy_scr[...].T
    m_u(0, HR)
    m_d(0, HR)
    for i in range(len(cols)):
        ms = []
        if i < last:
            ms += [partial(f, i + 1, 0, R) for f in (m_u, m_d)]
        if i >= 1:
            ms += [partial(m_t1, i - 1), partial(m_t2, i - 1)]
        weave(ms, [partial(v_gelu, i, r) for r in range(0, R, 16)])
        c, w = cols[i]
        tc1_ref[:, c : c + w] += acc[("c1", i)]
    m_db(0, R)
    weave([partial(m_y, 0, R)], [partial(v_back, r) for r in first + second])
    weave([partial(m_do, 0), partial(m_do, HR), m_tp, partial(m_t1, last), partial(m_t2, last)], [partial(v_out, r) for r in first + second])
    for i, k in ((2, "cp"), (3, "g2"), (4, "e2"), (5, "c2")):
        tv_ref[i * 8 : i * 8 + 8, :] += acc[k]

    if np_:

        @pl.when(s == pl.num_programs(0) - 1)
        def _():
            r = D // np_
            for k in range(0, np_, 2):
                for ref, flip in ((keep_ref, 0), (snd_ref, 1)):
                    at = pl.ds(pl.multiple_of((me_ref[0] ^ (k + flip)) * r, 16), r)
                    ref[k // 2, :, 0:FF] = t1_ref[at, :].astype(ref.dtype)
                    ref[k // 2, :, FF : 2 * FF] = t2_ref[at, :].astype(ref.dtype)
                    ref[k // 2, :, 2 * FF :] = tp_ref[at, :].astype(ref.dtype)


def feed(me, cnt, x, o, cot, c1, vec, pieces, weights, T):
    SEQ, N, D = x.shape
    TP = o.shape[0]
    FF = c1.shape[1]
    np_ = len(pieces)
    R = T * N
    v = pltpu.VMEM
    s = jax.ShapeDtypeStruct
    blk = pl.BlockSpec((T, N, D), lambda i, *_: (i, 0, 0))
    ins = list(pieces) if np_ else list(weights)
    out_specs = [blk, blk, blk, whole(8, FF), whole(64, D)]
    out_shape = [s((SEQ, N, D), BF), s((TP, N, D), F32), s((TP, N, D), BF), s((8, FF), F32), s((64, D), F32)]
    scratch = []
    if np_:
        shape = (np_ // 2, D // np_, 2 * FF + D)
        out_specs += [whole(*shape)] * 2
        out_shape += [s(shape, BF), s(shape, F32)]
        scratch += [v((D, D), BF), v((D, FF), BF), v((D, FF), BF), v((D, D), F32), v((D, FF), F32), v((D, FF), F32)]
    else:
        out_specs += [whole(D, D), whole(D, FF), whole(D, FF)]
        out_shape += [s((D, D), F32), s((D, FF), F32), s((D, FF), F32)]
    scratch += [v((R, D), BF), v((D, R), BF), v((R, D), BF), v((D, R), BF), v((R, D), F32), v((R, 128), F32), v((R, D), F32)]
    scratch += [v((R, 256), F32)] * 4 + [v((R, FF), BF)] * 2 + [v((R, D), F32)] * 2 + [v((R, D), BF)]
    return pl.pallas_call(
        partial(feed_body, SEQ, D, FF, T, N, np_),
        grid_spec=pltpu.PrefetchScalarGridSpec(
            num_scalar_prefetch=2,
            grid=(TP // T,),
            in_specs=[blk, blk, blk, full(c1), full(vec)] + [full(a) for a in ins],
            out_specs=out_specs,
            scratch_shapes=scratch,
        ),
        out_shape=out_shape,
        name="feed",
        **params(45 * 10**9, 30 * 10**6),
    )(me, cnt, x, o, cot, c1, vec, *ins)


def back_body(SEQ, SP, TP, D, FF, np_, DEPS, me_ref, a_ref, xh_ref, r_ref, qkv_ref, l_ref, do_ref, dx1_ref, w_ref, vec_ref, tc1_ref, tv2_ref, *refs):
    gi_ref, refs = refs[DEPS], refs[DEPS + 1 :]
    if np_:
        snd_ref, keep_ref, tq_ref, sm = refs[:4]
        gv_ref, refs = refs[4], refs[5:]
    else:
        tq_ref, gv_ref, refs = refs[0], refs[1], refs[2:]
    dos, gs, dob, at_scr, d_scr, da_scr, tv_ref, s0, s1, e0, e1, p0, p1, q0, q1 = refs
    H = D // HEAD_DIM
    W3 = 3 * D
    g = pl.program_id(0)
    j = pl.program_id(1)

    @pl.when((g == 0) & (j == 0))
    def _():
        for ref in (d_scr, p0, p1, q0, q1, dob, tq_ref, tv_ref):
            ref[...] = jnp.zeros_like(ref)

    @pl.when(j == 0)
    def _():
        spread(do_ref, dos, SEQ)

    gain = vec_ref[0:1, :]
    ss = (s0, s1)
    es = (e0, e1)
    pp = (p0, p1)
    qq = (q0, q1)
    st = {}
    S8 = SEQ // 8 * 8

    def load(i, t, n):
        dob[i * SP + t : i * SP + t + n, :] = image(dos, j * PAIR + i, t, n).astype(BF)

    def part(i, h, t):
        lo = t * D + h * HEAD_DIM
        return qkv_ref[i, :, lo : lo + HEAD_DIM]

    def dpart(i, h):
        return dob[i * SP : (i + 1) * SP, h * HEAD_DIM : (h + 1) * HEAD_DIM]

    def score(u):
        i, h = divmod(u, H)
        ss[u % 2][...] = dot(part(i, h, 1), part(i, h, 0), 1, 1)

    def dprob(u):
        i, h = divmod(u, H)
        es[u % 2][...] = dot(part(i, h, 2), dpart(i, h), 1, 1)

    def v_prob(u, t, n):
        i, h = divmod(u, H)
        p = jnp.exp(ss[u % 2][t : t + n, :] - l_ref[i, h : h + 1, :])
        if t + n > SEQ:
            p = jnp.where(lax.broadcasted_iota(jnp.int32, (n, 1), 0) < SEQ - t, p, 0.0)
        ss[u % 2][t : t + n, :] = p
        pp[u % 2][t : t + n, :] = p.astype(BF)
        x = jnp.sum((p * es[u % 2][t : t + n, :]).reshape(n // 8, 8, SP), axis=0)
        st[u] = x if t == 0 else st[u] + x
        if t + n >= SEQ:
            st[u] = jnp.sum(st[u], axis=0, keepdims=True)

    def v_ds(u, t, n):
        qq[u % 2][t : t + n, :] = (ss[u % 2][t : t + n, :] * (es[u % 2][t : t + n, :] - st[u])).astype(BF)

    def put(u, t, y):
        i, h = divmod(u, H)
        if h % 2 == 0:
            st[("d", t)] = y
        else:
            y = jnp.concatenate([st[("d", t)], y], axis=1).astype(BF)
            lo = t * D + (h - 1) * HEAD_DIM
            d_scr[i * SP : i * SP + SEQ, lo : lo + 2 * HEAD_DIM] = y[:SEQ]

    def m_dv(u):
        put(u, 2, dot(pp[u % 2][...], dpart(*divmod(u, H))))

    def m_dk(u):
        i, h = divmod(u, H)
        put(u, 1, dot(qq[u % 2][...], part(i, h, 0)))

    def m_dq(u):
        i, h = divmod(u, H)
        put(u, 0, dot(qq[u % 2][...], part(i, h, 1), 0, 0) * (HEAD_DIM**-0.5))

    rows = tiles(SEQ, 48)
    srows = tiles(S8, 64) + ([(S8, 8)] if S8 < SEQ else [])
    for t, n in rows:
        load(0, t, n)
    at_scr[...] = a_ref[...].reshape(PAIR * SP, D).T
    pre = [partial(load, i, t, n) for i in range(1, PAIR) for t, n in rows]
    nu = PAIR * H
    score(0)
    dprob(0)
    for k in range(nu):
        ms = []
        if k + 1 < nu:
            ms += [partial(score, k + 1), partial(dprob, k + 1)]
        if k >= 1:
            ms += [partial(m_dv, k - 1), partial(m_dk, k - 1), partial(m_dq, k - 1)]
        vs = [partial(f, k, t, n) for f in (v_prob, v_ds) for t, n in srows]
        vs += pre[k : k + 1]
        weave(ms, vs)
    m_dv(nu - 1)
    m_dk(nu - 1)
    m_dq(nu - 1)
    acc = {}

    def m_da():
        da_scr[...] = dot(d_scr[...], w_ref[...], 1, 1)

    def m_tq(c, w):
        tq_ref[:, c : c + w] += dot(at_scr[...], d_scr[:, c : c + w])

    def add(key, v):
        f = v.shape[0] // 8 * 8
        if f:
            x = jnp.sum(v[:f].reshape(f // 8, 8, D), axis=0)
            acc[key] = x if key not in acc else acc[key] + x
        if f < v.shape[0]:
            x = jnp.sum(v[f:], axis=0, keepdims=True)
            key = key + "tail"
            acc[key] = x if key not in acc else acc[key] + x

    def v_back(i, t, n):
        at = slice(i * SP + t, i * SP + t + n)
        d = da_scr[at, :]
        xh = xh_ref[i, t : t + n, :]
        dxh = d * gain
        mean1 = jnp.mean(dxh, axis=-1, keepdims=True)
        mean2 = jnp.mean(dxh * xh, axis=-1, keepdims=True)
        y = r_ref[i, t : t + n, 0:1] * (dxh - mean1 - xh * mean2)
        for c in range(gs.shape[0]):
            gs[c, pl.ds(pl.multiple_of((j * PAIR + i) * TP + t, 8), n), :] = y[:, c * 128 : (c + 1) * 128]
        add("g", d * xh)
        add("e", d)

    cols = tiles(W3, 256)
    m_da()
    weave([partial(m_tq, c, w) for c, w in cols], [partial(v_back, i, t, n) for i in range(PAIR) for t, n in rows])
    tv_ref[0:8, :] += acc["g"]
    tv_ref[8:16, :] += acc["e"]
    if "gtail" in acc:
        tv_ref[0:1, :] += acc["gtail"]
        tv_ref[8:9, :] += acc["etail"]

    @pl.when(j == pl.num_programs(1) - 1)
    def _():
        for t in range(0, SEQ - 1, 2):
            gi_ref[t : t + 2] = (tokens(gs, t, TP) + dx1_ref[t : t + 2]).astype(BF)
        if SEQ % 2:
            gi_ref[SEQ - 1] = (token(gs, SEQ - 1, TP) + dx1_ref[SEQ - 1]).astype(BF)

    @pl.when((j == pl.num_programs(1) - 1) & (g == pl.num_programs(0) - 1))
    def _():
        for i in range(2):
            gv_ref[i : i + 1, :] = jnp.sum(tv_ref[8 * i : 8 * i + 8, :], axis=0, keepdims=True)
        for i in range(2, 6):
            gv_ref[i : i + 1, :] = jnp.sum(tv2_ref[8 * i : 8 * i + 8, :], axis=0, keepdims=True)
        if np_:
            r = D // np_
            nb = FF // np_
            sm[...] = jnp.zeros_like(sm)
            bias = jnp.sum(tc1_ref[...], axis=0, keepdims=True)
            for s in range(np_):
                sm[s, 0:6, 0:r] = gv_ref[0:6, s * r : (s + 1) * r]
                sm[s, 6:7, 0:nb] = bias[:, s * nb : (s + 1) * nb]
            wide = sm.shape[2]
            for k in range(0, np_, 2):
                for ref, flip in ((keep_ref, 0), (snd_ref, 1)):
                    s = me_ref[0] ^ (k + flip)
                    ref[k // 2, 0:r, :] = tq_ref[pl.ds(pl.multiple_of(s * r, 16), r), :].astype(ref.dtype)
                    ref[k // 2, r : r + EXTRA, 0:wide] = sm[s].astype(ref.dtype)
                    ref[k // 2, r : r + EXTRA, wide:] = jnp.zeros((EXTRA, W3 - wide), ref.dtype)


def back(me, a, xh, r, qkv, l, do, dx1, w, vec, tc1, tv2, deps, SEQ, np_):
    N, SP, D = a.shape
    TP = do.shape[0]
    W3 = 3 * D
    FF = tc1.shape[1]
    R = PAIR * SP
    tok = lambda t: pl.BlockSpec((t, GROUP, D), lambda g, j, *_: (0, g, 0))
    img = lambda r, d: pl.BlockSpec((PAIR, r, d), lambda g, j, *_: (g * (GROUP // PAIR) + j, 0, 0))
    v = pltpu.VMEM
    s = jax.ShapeDtypeStruct
    out_specs = [tok(SEQ)]
    out_shape = [s((SEQ, N, D), BF)]
    if np_:
        shape = (np_ // 2, D // np_ + EXTRA, W3)
        out_specs += [whole(*shape)] * 2
        out_shape += [s(shape, BF), s(shape, F32)]
        scratch = [v((D, W3), F32), v((np_, EXTRA, up(max(FF, D) // np_, 128)), F32), v((8, D), F32)]
    else:
        out_specs += [whole(D, W3), whole(8, D)]
        out_shape += [s((D, W3), F32), s((8, D), F32)]
        scratch = []
    scratch += [v((D // 128, TP * GROUP, 128), F32)] * 2
    scratch += [v((R, D), BF), v((D, R), BF), v((R, W3), BF), v((R, D), F32)]
    scratch += [v((16, D), F32)] + [v((SP, SP), F32)] * 4 + [v((SP, SP), BF)] * 4
    return pl.pallas_call(
        partial(back_body, SEQ, SP, TP, D, FF, np_, len(deps)),
        grid_spec=pltpu.PrefetchScalarGridSpec(
            num_scalar_prefetch=1,
            grid=(N // GROUP, GROUP // PAIR),
            in_specs=[img(SP, D), img(SP, D), img(SP, 128), img(SP, W3), img(8, SP), tok(TP), tok(TP)]
            + [full(w), full(vec), full(tc1), full(tv2)]
            + [pl.BlockSpec(memory_space=pl.ANY)] * len(deps),
            out_specs=out_specs,
            scratch_shapes=scratch,
        ),
        out_shape=out_shape,
        name="back",
        **params(40 * 10**9, 30 * 10**6),
    )(me, a, xh, r, qkv, l, do, dx1, w, vec, tc1, tv2, *deps)


def adam_body(np_, count, slots, where, flag_ref, gid_ref, scale_ref, *refs):
    pieces, refs = refs[:np_], refs[np_:]
    weights, firsts, seconds, outs = refs[:count], refs[count : 2 * count], refs[2 * count : 3 * count], refs[3 * count :]
    for k, (p, row, col) in enumerate(where):
        r, c = weights[k].shape
        xs = [x[row : row + r, col : col + c].astype(F32) for x in pieces]
        grad = (xs[0] if len(xs) == 1 else (xs[0] + xs[1]) + (xs[2] + xs[3])) / slots
        flag = flag_ref[p].astype(F32)
        lr = scale_ref[gid_ref[p]]
        first = BETA_ONE * firsts[k][...] + (1.0 - BETA_ONE) * grad
        second = BETA_TWO * seconds[k][...] + (1.0 - BETA_TWO) * grad * grad
        direction = first / (1.0 - BETA_ONE**ADAM_STEPS) / (jnp.sqrt(second / (1.0 - BETA_TWO**ADAM_STEPS)) + ADAM_EPS)
        weight = weights[k][...]
        outs[k][...] = grad
        outs[count + k][...] = weight - LEARN_RATE * lr * (direction + DECAY_RATE * flag * weight)
        outs[2 * count + k][...] = first
        outs[3 * count + k][...] = second


def adam(flags, gids, scales, pieces, arrays, slots, where):
    smem = pl.BlockSpec(memory_space=pltpu.SMEM)
    vmem = pl.BlockSpec(memory_space=pltpu.VMEM)
    mine = [[xs[p] for p, _, _ in where] for xs in arrays]
    shapes = [jax.ShapeDtypeStruct(w.shape, F32) for w in mine[0]]
    return pl.pallas_call(
        partial(adam_body, len(pieces), len(where), slots, where),
        in_specs=[smem] * 3 + [vmem] * (len(pieces) + 3 * len(where)),
        out_specs=[vmem] * (4 * len(where)),
        out_shape=shapes * 4,
        name="adam",
        **params(10**9, 5 * 10**6),
    )(flags, gids, scales, *pieces, *mine[0], *mine[1], *mine[2])


def pairs(n, k):
    return [(i, i ^ k) for i in range(n)]


def touch_body(*refs):
    pass


def touch(dep, xs):
    spec = pl.BlockSpec(memory_space=pl.ANY)
    return pl.pallas_call(
        touch_body,
        in_specs=[spec] * (len(xs) + 1),
        out_specs=[spec] * len(xs),
        out_shape=[jax.ShapeDtypeStruct(x.shape, x.dtype) for x in xs],
        input_output_aliases={k: k for k in range(len(xs))},
        name="touch",
    )(*xs, dep)


def fetch(x, n):
    return [x] + [lax.ppermute(x, "fsdp", pairs(n, k)) for k in range(2, n, 2)]


def fetch_core(own, n):
    other = [lax.ppermute(x, "fsdp", pairs(n, 1)) for x in own]
    return [x for both in zip(own, other) for x in both]


def halve(snd, keep, n):
    h = keep + lax.ppermute(snd, "fsdp", pairs(n, 1)).astype(F32)
    return h[0], [h[k].astype(BF) for k in range(1, n // 2)]


def along_z(xs, n):
    return [lax.ppermute(x, "fsdp", pairs(n, 2 * k + 2)) for k, x in enumerate(xs)]


def finish(own, got, d):
    for piece in got:
        own = own + piece.astype(F32)
    b = own.astype(BF)
    return [b] + [lax.ppermute(b, "dp", pairs(d, k)) for k in range(1, d)]


def local(
    images, cotangent, counts,
    w_qkv, w_proj, w_fc1, w_fc2, b_fc1, vectors,
    m_qkv, m_proj, m_fc1, m_fc2, m_bias1, m_vectors,
    v_qkv, v_proj, v_fc1, v_fc2, v_bias1, v_vectors,
    decay_flags, group_ids, group_scales,
):
    n = lax.axis_size("fsdp")
    d = lax.axis_size("dp")
    N, SEQ, D = images.shape
    r = w_qkv.shape[0]
    FF = w_fc1.shape[1]
    T = 20
    TP = up(SEQ, T)
    direct = n in (2, 4, 8) and d == 4 and r % 16 == 0
    x = jnp.transpose(images, (1, 0, 2))
    cot = jnp.transpose(cotangent, (1, 0, 2))
    me = lax.axis_index("fsdp").astype(jnp.int32).reshape(1)
    rows = lambda b: b.reshape(1, -1)
    weights = [w_qkv, w_proj, w_fc1, w_fc2.T, rows(b_fc1), vectors]
    firsts = [m_qkv, m_proj, m_fc1, m_fc2.T, rows(m_bias1), m_vectors]
    seconds = [v_qkv, v_proj, v_fc1, v_fc2.T, rows(v_bias1), v_vectors]
    pack_a, pack_b = pack(weights[0], weights[5], weights[4], weights[2], weights[3], weights[1])
    xh, rf = norm(x)
    if direct:
        half_a = touch(rf, fetch(pack_a, n))
        pieces_a = fetch_core(half_a, n)
        half_b = fetch(touch(half_a[-1], [pack_b])[0], n)
        qkv, o, logs, a, wq, vec, c1 = attend(me, xh, pieces_a, None, None, FF, SEQ, TP)
        pieces_b = fetch_core(touch(vec, half_b), n)
        out, dx1, do, tc1, tv2, snd, keep = feed(me, counts, x, o, cot, c1, vec, pieces_b, (), T)
        own_b, sends = halve(snd, keep, n)
        got_b = along_z(sends, n)
        gi, snd, keep = back(me, a, xh, rf, qkv, logs, do, dx1, wq, vec, tc1, tv2, sends, SEQ, n)
        snd, *got_b = touch(vec, [snd, *got_b])
        own_a, sends = halve(snd, keep, n)
        got_a = along_z(sends, n)
        pb = finish(own_b, got_b, d)
        pa = finish(own_a, got_a, d)
    else:
        all_a = lax.all_gather(pack_a, "fsdp", axis=0, tiled=False)
        all_b = lax.all_gather(pack_b, "fsdp", axis=0, tiled=True)
        wq = all_a[:, :r].reshape(D, 3 * D)
        nb = FF // n
        vec = jnp.transpose(all_a[:, r : r + 8, :r], (1, 0, 2)).reshape(8, D).astype(F32)
        c1 = jnp.broadcast_to(all_a[:, r + 6, :nb].reshape(1, FF), (8, FF)).astype(F32)
        ws = (all_b[:, 2 * FF :], all_b[:, :FF], all_b[:, FF : 2 * FF])
        qkv, o, logs, a = attend(me, xh, (), wq, vec, FF, SEQ, TP)
        out, dx1, do, tc1, tv2, tp, t1, t2 = feed(me, counts, x, o, cot, c1, vec, (), ws, T)
        gi, tq, gv = back(me, a, xh, rf, qkv, logs, do, dx1, wq, vec, tc1, tv2, (), SEQ, 0)
        share = lambda g, axis: lax.psum(
            lax.psum_scatter(g, "fsdp", scatter_dimension=axis, tiled=True).astype(BF), "dp"
        ).astype(F32)
        pb = [share(jnp.concatenate([t1, t2, tp], axis=1), 0)]
        small = jnp.zeros((8, 3 * D), F32).at[:6, :r].set(share(gv[:6], 1))
        small = small.at[6, :nb].set(share(jnp.sum(tc1, axis=0), 0))
        pa = [jnp.concatenate([share(tq, 0), small], axis=0)]
    arrays = (weights, firsts, seconds)
    slots = float(N * n * d)
    where_a = ((0, 0, 0), (4, r + 6, 0), (5, r, 0))
    where_b = ((1, 0, 2 * FF), (2, 0, 0), (3, 0, FF))
    res = [None] * 24
    for pieces, where in ((pb, where_b), (pa, where_a)):
        got = adam(decay_flags, group_ids, group_scales, pieces, arrays, slots, where)
        for j in range(4):
            for k, (p, _, _) in enumerate(where):
                res[6 * j + p] = got[3 * j + k]
    for k in range(4):
        res[6 * k + 3] = res[6 * k + 3].T
        res[6 * k + 4] = res[6 * k + 4].reshape(-1)
    return (jnp.transpose(out, (1, 0, 2)), jnp.transpose(gi, (1, 0, 2)), *res)


def solution(mesh):
    P = PartitionSpec
    both = ("dp", "fsdp")
    six = (P("fsdp", None), P("fsdp", None), P("fsdp", None), P(None, "fsdp"), P("fsdp"), P(None, "fsdp"))
    data = (P(both, None, None), P(both, None, None))
    return jax.shard_map(
        local,
        mesh=mesh,
        in_specs=(*data, P(both), *six, *six, *six, P(), P(), P()),
        out_specs=(*data, *six, *six, *six, *six),
        check_vma=False,
    )
```

```python
import math
from functools import partial

import jax
import jax.numpy as jnp
from jax import lax
from jax.experimental import pallas as pl
from jax.experimental.pallas import tpu as pltpu
from jax.sharding import PartitionSpec

BF = jnp.bfloat16
F32 = jnp.float32
HEAD_DIM = 64
EPS_LN = 1e-06
LEARN_RATE = 0.2
BETA_ONE = 0.9
BETA_TWO = 0.999
ADAM_EPS = 1e-08
DECAY_RATE = 0.5
ADAM_STEPS = 10.0
GROUP = 8
PAIR = 4
EXTRA = 8
ROOT_HALF = math.sqrt(0.5)


def up(n, m):
    return (n + m - 1) // m * m


def dot(a, b, ca=1, cb=0):
    return lax.dot_general(a, b, (((ca,), (cb,)), ((), ())), preferred_element_type=F32)


def tiles(n, w):
    return [(a, min(w, n - a)) for a in range(0, n, w)]


def params(flops=0, nbytes=0):
    return dict(
        compiler_params=pltpu.CompilerParams(vmem_limit_bytes=58 << 20),
        cost_estimate=pl.CostEstimate(flops=flops, bytes_accessed=nbytes, transcendentals=0),
    )


def weave(ms, vs):
    k = 0
    for a, f in enumerate(ms):
        f()
        while k * len(ms) < len(vs) * (a + 1):
            vs[k]()
            k += 1
    for f in vs[k:]:
        f()


def norm_rows(x):
    c = x - jnp.mean(x, axis=-1, keepdims=True)
    r = lax.rsqrt(jnp.mean(c * c, axis=-1, keepdims=True) + EPS_LN)
    return c * r, r


def gelu_pair(u):
    phi = 0.5 + 0.5 * lax.erf(u * ROOT_HALF)
    e = jnp.exp2((-0.5 * math.log2(math.e)) * (u * u))
    return u * phi, phi + (u * (1.0 / math.sqrt(2.0 * math.pi))) * e


def full(a):
    return pl.BlockSpec(a.shape, lambda *_: (0,) * len(a.shape))


def whole(*shape):
    return pl.BlockSpec(shape, lambda *_: (0,) * len(shape))


def spread(src, dst, seq):
    for t, n in tiles(seq, 20):
        x = src[t : t + n].astype(F32).reshape(n * GROUP, src.shape[2])
        for c in range(dst.shape[0]):
            dst[c, t * GROUP : (t + n) * GROUP, :] = x[:, c * 128 : (c + 1) * 128]


def image(ref, i, t, n):
    return jnp.concatenate(
        [ref[c, pl.ds(t * GROUP + i, n, stride=GROUP), :] for c in range(ref.shape[0])], axis=1
    )


def token(ref, t, tp):
    return jnp.concatenate(
        [ref[c, pl.ds(t, GROUP, stride=tp), :] for c in range(ref.shape[0])], axis=1
    )


def tokens(ref, t, tp):
    return jnp.stack([token(ref, t, tp), token(ref, t + 1, tp)])


def pack_body(r, wq_ref, vec_ref, b_ref, w1_ref, w2_ref, wp_ref, a_ref, b_out, sm):
    FF = w1_ref.shape[1]
    a_ref[0:r, :] = wq_ref[...].astype(BF)
    sm[...] = jnp.zeros_like(sm)
    sm[0 : vec_ref.shape[0], 0 : vec_ref.shape[1]] = vec_ref[...]
    sm[6:7, 0 : b_ref.shape[1]] = b_ref[...]
    a_ref[r : r + EXTRA, :] = sm[...].astype(BF)
    b_out[:, 0:FF] = w1_ref[...].astype(BF)
    b_out[:, FF : 2 * FF] = w2_ref[...].astype(BF)
    b_out[:, 2 * FF :] = wp_ref[...].astype(BF)


def pack(wq, vec, b, w1, w2t, wp):
    r, W3 = wq.shape
    FF = w1.shape[1]
    C = 2 * FF + wp.shape[1]
    return pl.pallas_call(
        partial(pack_body, r),
        out_shape=[jax.ShapeDtypeStruct((r + EXTRA, W3), BF), jax.ShapeDtypeStruct((r, C), BF)],
        scratch_shapes=[pltpu.VMEM((EXTRA, W3), F32)],
        name="pack",
        **params(),
    )(wq, vec, b, w1, w2t, wp)


def norm_body(SEQ, D, x_ref, xh_ref, r_ref, xs):
    j = pl.program_id(1)

    @pl.when(j == 0)
    def _():
        spread(x_ref, xs, SEQ)

    for i in range(PAIR):
        for t, n in tiles(SEQ, 48):
            xh, r = norm_rows(image(xs, j * PAIR + i, t, n))
            xh_ref[i, t : t + n, :] = xh
            r_ref[i, t : t + n, :] = jnp.broadcast_to(r, (n, 128))


def norm(x):
    SEQ, N, D = x.shape
    SP = up(SEQ, 16)
    tok = pl.BlockSpec((SEQ, GROUP, D), lambda g, j: (0, g, 0))
    img = lambda d: pl.BlockSpec((PAIR, SP, d), lambda g, j: (g * (GROUP // PAIR) + j, 0, 0))
    return pl.pallas_call(
        partial(norm_body, SEQ, D),
        grid=(N // GROUP, GROUP // PAIR),
        in_specs=[tok],
        out_specs=[img(D), img(128)],
        out_shape=[jax.ShapeDtypeStruct((N, SP, d), F32) for d in (D, 128)],
        scratch_shapes=[pltpu.VMEM((D // 128, up(SEQ, 8) * GROUP, 128), F32)],
        name="norm",
        **params(8 * 10**9, 15 * 10**6),
    )(x)


def attend_body(SEQ, SP, TP, D, np_, me_ref, xh_ref, *refs):
    H = D // HEAD_DIM
    g = pl.program_id(0)
    j = pl.program_id(1)
    if np_:
        pieces, refs = refs[:np_], refs[np_:]
        qkv_ref, o_ref, p_ref, a_ref, w_ref, vec_ref, c1_ref, sm = refs[:8]
        refs = refs[8:]
    else:
        w_ref, vec_ref, qkv_ref, o_ref, p_ref, a_ref = refs[:6]
        refs = refs[6:]
    os_, a_scr, s0, s1 = refs

    @pl.when((g == 0) & (j == 0))
    def _():
        for ref in (a_scr, os_):
            ref[...] = jnp.zeros_like(ref)
        if np_:
            r = pieces[0].shape[0] - EXTRA
            for k in range(np_):
                s = me_ref[0] ^ k
                w_ref[pl.ds(pl.multiple_of(s * r, 16), r), :] = pieces[k][0:r, :]
                sm[s] = pieces[k][r : r + EXTRA, 0 : sm.shape[2]].astype(F32)
            nb = c1_ref.shape[1] // np_
            vec_ref[...] = jnp.concatenate([sm[s, :, 0:r] for s in range(np_)], axis=1)
            c1_ref[...] = jnp.broadcast_to(
                jnp.concatenate([sm[s, 6:7, 0:nb] for s in range(np_)], axis=1), c1_ref.shape
            )

    gain = vec_ref[0:1, :]
    shift = vec_ref[1:2, :]
    ss = (s0, s1)
    st = {}
    S8 = SEQ // 16 * 16

    def ln(i, t, n):
        y = (xh_ref[i, t : t + n, :] * gain + shift).astype(BF)
        a_scr[i * SP + t : i * SP + t + n, :] = y
        a_ref[i, t : t + n, :] = y

    def qkv(t, c, w):
        y = dot(a_scr[...], w_ref[:, t * D + c : t * D + c + w])
        if t == 0:
            y = y * (HEAD_DIM**-0.5)
        qkv_ref[:, :, t * D + c : t * D + c + w] = y.astype(BF).reshape(PAIR, SP, w)

    def score(u):
        i, h = divmod(u, H)
        lo = h * HEAD_DIM
        ss[u % 2][...] = dot(
            qkv_ref[i, :, D + lo : D + lo + HEAD_DIM], qkv_ref[i, :, lo : lo + HEAD_DIM], 1, 1
        )

    def tile(ref, t, n):
        x = ref[t : t + n, :]
        if t + n > SEQ:
            x = jnp.where(lax.broadcasted_iota(jnp.int32, (n, 1), 0) < SEQ - t, x, -1e30)
        return x

    def vmax(u, t, n):
        m = jnp.max(tile(ss[u % 2], t, n).reshape(n // 8, 8, SP), axis=0)
        st[u] = m if t == 0 else jnp.maximum(st[u], m)
        if t + n >= SEQ:
            st[u] = jnp.max(st[u], axis=0, keepdims=True)

    def vexp(u, t, n):
        p = jnp.exp(tile(ss[u % 2], t, n) - st[u])
        ss[u % 2][t : t + n, :] = p
        total = jnp.sum(p.reshape(n // 8, 8, SP), axis=0)
        k = ("l", u)
        st[k] = total if t == 0 else st[k] + total
        if t + n >= SEQ:
            total = jnp.sum(st[k], axis=0, keepdims=True)
            st[k] = 1.0 / total

    def vnorm(u, t, n):
        i, h = divmod(u, H)
        p_ref[i, h, t : t + n, :] = (ss[u % 2][t : t + n, :] * st[("l", u)]).astype(BF)

    def mix(u):
        i, h = divmod(u, H)
        lo = 2 * D + h * HEAD_DIM
        y = dot(p_ref[i, h], qkv_ref[i, :, lo : lo + HEAD_DIM], 0, 0)
        if h % 2 == 0:
            st["o"] = y
        else:
            y = jnp.concatenate([st["o"], y], axis=1)
            os_[h // 2, pl.ds(pl.multiple_of((j * PAIR + i) * TP, 8), SEQ), :] = y[:SEQ]

    for i in range(PAIR):
        for t, n in tiles(SEQ, 48):
            ln(i, t, n)
    c0 = min(256, D)
    hb = c0 // HEAD_DIM
    for t in range(3):
        qkv(t, 0, c0)
    rest = [partial(qkv, t, c, w) for c, w in tiles(D, 256)[1:] for t in range(3)]
    srows = tiles(S8, 64) + ([(S8, SP - S8)] if S8 < SEQ else [])
    order = [i * H + h for i in range(PAIR) for h in range(hb)]
    order += [i * H + h for i in range(PAIR) for h in range(hb, H)]
    nu = len(order)
    score(order[0])
    for k, u in enumerate(order):
        ms = rest[k : k + 1]
        if k + 1 < nu:
            ms.append(partial(score, order[k + 1]))
        if k >= 1:
            ms.append(partial(mix, order[k - 1]))
        vs = [partial(f, u, t, n) for f in (vmax, vexp, vnorm) for t, n in srows]
        weave(ms, vs)
    nu = order[-1] + 1
    mix(nu - 1)
    for i in range(PAIR):
        a_ref[i, SEQ:SP, :] = jnp.zeros((SP - SEQ, D), BF)

    @pl.when(j == pl.num_programs(1) - 1)
    def _():
        for t in range(0, TP, 2):
            o_ref[t : t + 2] = tokens(os_, t, TP).astype(BF)


def attend(me, xh, pieces, w, vec, FF, SEQ, TP):
    N, SP, D = xh.shape
    W3 = 3 * D
    np_ = len(pieces)
    tok = lambda t: pl.BlockSpec((t, GROUP, D), lambda g, j, *_: (0, g, 0))
    img = lambda r, d: pl.BlockSpec((PAIR, r, d), lambda g, j, *_: (g * (GROUP // PAIR) + j, 0, 0))
    probs = pl.BlockSpec((PAIR, D // HEAD_DIM, SP, SP), lambda g, j, *_: (g * (GROUP // PAIR) + j, 0, 0, 0))
    v = pltpu.VMEM
    s = jax.ShapeDtypeStruct
    ins = list(pieces) if np_ else [w, vec]
    out_specs = [img(SP, W3), tok(TP), probs, img(SP, D)]
    out_shape = [s((N, SP, W3), BF), s((TP, N, D), BF), s((N, D // HEAD_DIM, SP, SP), BF), s((N, SP, D), BF)]
    scratch = [v((D // 128, TP * GROUP, 128), F32), v((PAIR * SP, D), BF)]
    scratch += [v((SP, SP), F32)] * 2
    if np_:
        out_specs += [whole(D, W3), whole(8, D), whole(8, FF)]
        out_shape += [s((D, W3), BF), s((8, D), F32), s((8, FF), F32)]
        scratch = [v((np_, EXTRA, up(max(FF, D) // np_, 128)), F32)] + scratch
    return pl.pallas_call(
        partial(attend_body, SEQ, SP, TP, D, np_),
        grid_spec=pltpu.PrefetchScalarGridSpec(
            num_scalar_prefetch=1,
            grid=(N // GROUP, GROUP // PAIR),
            in_specs=[img(SP, D)] + [full(a) for a in ins],
            out_specs=out_specs,
            scratch_shapes=scratch,
        ),
        out_shape=out_shape,
        name="attend",
        **params(20 * 10**9, 25 * 10**6),
    )(me, xh, *ins)


def feed_body(SEQ, D, FF, T, N, np_, me_ref, cnt_ref, x_ref, o_ref, cot_ref, c1_ref, vec_ref, *refs):
    s = pl.program_id(0)
    R = T * N
    RT = 2 * N
    HR = R // 2
    if np_:
        pieces, refs = refs[:np_], refs[np_:]
        out_ref, dx1_ref, do_ref, tc1_ref, tv_ref, snd_ref, keep_ref = refs[:7]
        wp_ref, w1_ref, w2t_ref, tp_ref, t1_ref, t2_ref = refs[7:13]
        refs = refs[13:]
    else:
        wp_ref, w1_ref, w2t_ref, out_ref, dx1_ref, do_ref, tc1_ref, tv_ref, tp_ref, t1_ref, t2_ref = refs[:11]
        refs = refs[11:]
    b_scr, bt_scr, dy_scr, dyt_scr, xh_scr, r_scr, x1_scr, u0, u1, d0, d1, g_scr, du_scr, y_scr, db_scr, dx_scr = refs

    @pl.when(s == 0)
    def _():
        for ref in (tp_ref, t1_ref, t2_ref, tc1_ref, tv_ref):
            ref[...] = jnp.zeros_like(ref)
        if np_:
            r = pieces[0].shape[0]
            for k in range(np_):
                at = pl.ds(pl.multiple_of((me_ref[0] ^ k) * r, 16), r)
                w1_ref[at, :] = pieces[k][:, 0:FF]
                w2t_ref[at, :] = pieces[k][:, FF : 2 * FF]
                wp_ref[at, :] = pieces[k][:, 2 * FF :]

    cp = vec_ref[2:3, :]
    g2 = vec_ref[3:4, :]
    e2 = vec_ref[4:5, :]
    c2 = vec_ref[5:6, :]
    io = lax.broadcasted_iota(jnp.int32, (RT, 1), 0)
    real = lax.rem(io, N) < cnt_ref[0]
    lim = SEQ * N - s * R
    acc = {}

    def rows(ref, r):
        return ref[r // N : r // N + 2].reshape(RT, D)

    def add(key, v):
        v = jnp.sum(v.reshape(v.shape[0] // 8, 8, v.shape[1]), axis=0)
        acc[key] = v if key not in acc else acc[key] + v

    def m_proj(h):
        x1_scr[h : h + HR, :] = dot(o_ref[h // N : (h + HR) // N].reshape(HR, D), wp_ref[...])

    def v_norm(r):
        inside = (io + r) < lim
        x = jnp.where(inside, rows(x_ref, r).astype(F32), 0.0)
        dy_scr[r : r + RT, :] = jnp.where(real & inside, rows(cot_ref, r), jnp.zeros((), BF))
        x1 = x + x1_scr[r : r + RT, :] + cp
        x1_scr[r : r + RT, :] = x1 + c2
        xh, rr = norm_rows(x1)
        xh_scr[r : r + RT, :] = xh
        r_scr[r : r + RT, :] = jnp.broadcast_to(rr, (RT, 128))
        b_scr[r : r + RT, :] = (xh * g2 + e2).astype(BF)

    cols = tiles(FF, 256)
    us = (u0, u1)
    ds = (d0, d1)

    def m_u(i, h, HR=HR):
        c, w = cols[i]
        us[i % 2][h : h + HR, :w] = dot(b_scr[h : h + HR, :], w1_ref[:, c : c + w]) + c1_ref[0:1, c : c + w]

    def m_d(i, h, HR=HR):
        c, w = cols[i]
        ds[i % 2][h : h + HR, :w] = dot(dy_scr[h : h + HR, :], w2t_ref[:, c : c + w])

    def v_gelu(i, r):
        c, w = cols[i]
        ga, dg = gelu_pair(us[i % 2][r : r + 16, :w])
        g_scr[r : r + 16, c : c + w] = ga.astype(BF)
        du = ds[i % 2][r : r + 16, :w] * dg
        du_scr[r : r + 16, c : c + w] = du.astype(BF)
        add(("c1", i), du)

    def m_t1(i):
        c, w = cols[i]
        t1_ref[:, c : c + w] += dot(bt_scr[...], du_scr[:, c : c + w])

    def m_t2(i):
        c, w = cols[i]
        t2_ref[:, c : c + w] += dot(dyt_scr[...], g_scr[:, c : c + w])

    def m_y(h, HR=HR):
        y_scr[h : h + HR, :] = dot(g_scr[h : h + HR, :], w2t_ref[...], 1, 1)

    def m_db(h, HR=HR):
        db_scr[h : h + HR, :] = dot(du_scr[h : h + HR, :], w1_ref[...], 1, 1)

    def v_out(r):
        y = x1_scr[r : r + RT, :] + y_scr[r : r + RT, :]
        out_ref[r // N : r // N + 2] = jnp.where(real, y, 0.0).astype(BF).reshape(2, N, D)

    def v_back(r):
        db = db_scr[r : r + RT, :]
        xh = xh_scr[r : r + RT, :]
        dyf = dy_scr[r : r + RT, :].astype(F32)
        dxh = db * g2
        mean1 = jnp.mean(dxh, axis=-1, keepdims=True)
        mean2 = jnp.mean(dxh * xh, axis=-1, keepdims=True)
        dx = dyf + r_scr[r : r + RT, 0:1] * (dxh - mean1 - xh * mean2)
        add("g2", db * xh)
        add("e2", db)
        add("c2", dyf)
        add("cp", dx)
        dx1_ref[r // N : r // N + 2] = dx.reshape(2, N, D)
        dx_scr[r : r + RT, :] = dx.astype(BF)

    def m_do(h):
        y = dot(dx_scr[h : h + HR, :], wp_ref[...], 1, 1)
        do_ref[h // N : (h + HR) // N] = y.astype(BF).reshape(HR // N, N, D)

    def m_tp():
        tp_ref[...] += dot(o_ref[...].reshape(R, D), dx_scr[...], 0, 0)

    first = list(range(0, HR, RT))
    second = list(range(HR, R, RT))
    last = len(cols) - 1
    m_proj(0)
    weave([partial(m_proj, HR)], [partial(v_norm, r) for r in first])
    weave([partial(m_u, 0, 0), partial(m_d, 0, 0)], [partial(v_norm, r) for r in second])
    bt_scr[...] = b_scr[...].T
    dyt_scr[...] = dy_scr[...].T
    m_u(0, HR)
    m_d(0, HR)
    for i in range(len(cols)):
        ms = []
        if i < last:
            ms += [partial(f, i + 1, 0, R) for f in (m_u, m_d)]
        if i >= 1:
            ms += [partial(m_t1, i - 1), partial(m_t2, i - 1)]
        weave(ms, [partial(v_gelu, i, r) for r in range(0, R, 16)])
        c, w = cols[i]
        tc1_ref[:, c : c + w] += acc[("c1", i)]
    m_db(0, R)
    weave([partial(m_y, 0, R)], [partial(v_back, r) for r in first + second])
    weave([partial(m_do, 0), partial(m_do, HR), m_tp, partial(m_t1, last), partial(m_t2, last)], [partial(v_out, r) for r in first + second])
    for i, k in ((2, "cp"), (3, "g2"), (4, "e2"), (5, "c2")):
        tv_ref[i * 8 : i * 8 + 8, :] += acc[k]

    if np_:

        @pl.when(s == pl.num_programs(0) - 1)
        def _():
            r = D // np_
            for k in range(0, np_, 2):
                for ref, flip in ((keep_ref, 0), (snd_ref, 1)):
                    at = pl.ds(pl.multiple_of((me_ref[0] ^ (k + flip)) * r, 16), r)
                    ref[k // 2, :, 0:FF] = t1_ref[at, :].astype(ref.dtype)
                    ref[k // 2, :, FF : 2 * FF] = t2_ref[at, :].astype(ref.dtype)
                    ref[k // 2, :, 2 * FF :] = tp_ref[at, :].astype(ref.dtype)


def feed(me, cnt, x, o, cot, c1, vec, pieces, weights, T):
    SEQ, N, D = x.shape
    TP = o.shape[0]
    FF = c1.shape[1]
    np_ = len(pieces)
    R = T * N
    v = pltpu.VMEM
    s = jax.ShapeDtypeStruct
    blk = pl.BlockSpec((T, N, D), lambda i, *_: (i, 0, 0))
    ins = list(pieces) if np_ else list(weights)
    out_specs = [blk, blk, blk, whole(8, FF), whole(64, D)]
    out_shape = [s((SEQ, N, D), BF), s((TP, N, D), F32), s((TP, N, D), BF), s((8, FF), F32), s((64, D), F32)]
    scratch = []
    if np_:
        shape = (np_ // 2, D // np_, 2 * FF + D)
        out_specs += [whole(*shape)] * 2
        out_shape += [s(shape, BF), s(shape, F32)]
        scratch += [v((D, D), BF), v((D, FF), BF), v((D, FF), BF), v((D, D), F32), v((D, FF), F32), v((D, FF), F32)]
    else:
        out_specs += [whole(D, D), whole(D, FF), whole(D, FF)]
        out_shape += [s((D, D), F32), s((D, FF), F32), s((D, FF), F32)]
    scratch += [v((R, D), BF), v((D, R), BF), v((R, D), BF), v((D, R), BF), v((R, D), F32), v((R, 128), F32), v((R, D), F32)]
    scratch += [v((R, 256), F32)] * 4 + [v((R, FF), BF)] * 2 + [v((R, D), F32)] * 2 + [v((R, D), BF)]
    return pl.pallas_call(
        partial(feed_body, SEQ, D, FF, T, N, np_),
        grid_spec=pltpu.PrefetchScalarGridSpec(
            num_scalar_prefetch=2,
            grid=(TP // T,),
            in_specs=[blk, blk, blk, full(c1), full(vec)] + [full(a) for a in ins],
            out_specs=out_specs,
            scratch_shapes=scratch,
        ),
        out_shape=out_shape,
        name="feed",
        **params(45 * 10**9, 30 * 10**6),
    )(me, cnt, x, o, cot, c1, vec, *ins)


def back_body(SEQ, SP, TP, D, FF, np_, DEPS, me_ref, a_ref, xh_ref, r_ref, qkv_ref, p_ref, do_ref, dx1_ref, w_ref, vec_ref, tc1_ref, tv2_ref, *refs):
    gi_ref, refs = refs[DEPS], refs[DEPS + 1 :]
    if np_:
        snd_ref, keep_ref, tq_ref, sm = refs[:4]
        gv_ref, refs = refs[4], refs[5:]
    else:
        tq_ref, gv_ref, refs = refs[0], refs[1], refs[2:]
    dos, gs, dob, at_scr, d_scr, da_scr, tv_ref, e0, e1, q0, q1 = refs
    H = D // HEAD_DIM
    W3 = 3 * D
    g = pl.program_id(0)
    j = pl.program_id(1)

    @pl.when((g == 0) & (j == 0))
    def _():
        for ref in (d_scr, dob, tq_ref, tv_ref):
            ref[...] = jnp.zeros_like(ref)

    @pl.when(j == 0)
    def _():
        spread(do_ref, dos, SEQ)

    gain = vec_ref[0:1, :]
    es = (e0, e1)
    qq = (q0, q1)
    st = {}
    S8 = SEQ // 16 * 16

    def load(i, t, n):
        dob[i * SP + t : i * SP + t + n, :] = image(dos, j * PAIR + i, t, n).astype(BF)

    def part(i, h, t):
        lo = t * D + h * HEAD_DIM
        return qkv_ref[i, :, lo : lo + HEAD_DIM]

    def dpart(i, h):
        return dob[i * SP : (i + 1) * SP, h * HEAD_DIM : (h + 1) * HEAD_DIM]

    def dprob(u):
        i, h = divmod(u, H)
        es[u % 2][...] = dot(part(i, h, 2), dpart(i, h), 1, 1)

    def v_inner(u, t, n):
        x = p_ref[divmod(u, H) + (slice(t, t + n),)].astype(F32) * es[u % 2][t : t + n, :]
        x = jnp.sum(x.reshape(n // 8, 8, SP), axis=0)
        st[u] = x if t == 0 else st[u] + x
        if t + n >= SEQ:
            st[u] = jnp.sum(st[u], axis=0, keepdims=True)

    def v_ds(u, t, n):
        p = p_ref[divmod(u, H) + (slice(t, t + n),)].astype(F32)
        qq[u % 2][t : t + n, :] = (p * (es[u % 2][t : t + n, :] - st[u])).astype(BF)

    def put(u, t, y):
        i, h = divmod(u, H)
        if h % 2 == 0:
            st[("d", t)] = y
        else:
            y = jnp.concatenate([st[("d", t)], y], axis=0).T if t == 0 else jnp.concatenate([st[("d", t)], y], axis=1)
            y = y.astype(BF)
            lo = t * D + (h - 1) * HEAD_DIM
            d_scr[i * SP : i * SP + SEQ, lo : lo + 2 * HEAD_DIM] = y[:SEQ]

    def m_dv(u):
        put(u, 2, dot(p_ref[divmod(u, H)], dpart(*divmod(u, H))))

    def m_dk(u):
        i, h = divmod(u, H)
        put(u, 1, dot(qq[u % 2][...], part(i, h, 0)))

    def m_dq(u):
        i, h = divmod(u, H)
        put(u, 0, dot(part(i, h, 1), qq[u % 2][...], 0, 0) * (HEAD_DIM**-0.5))

    rows = tiles(SEQ, 48)
    srows = tiles(S8, 64) + ([(S8, SP - S8)] if S8 < SEQ else [])
    for t, n in rows:
        load(0, t, n)
    at_scr[...] = a_ref[...].reshape(PAIR * SP, D).T
    pre = [partial(load, i, t, n) for i in range(1, PAIR) for t, n in rows]
    nu = PAIR * H
    dprob(0)
    for k in range(nu):
        ms = []
        if k + 1 < nu:
            ms.append(partial(dprob, k + 1))
        if k >= 1:
            ms += [partial(m_dv, k - 1), partial(m_dk, k - 1), partial(m_dq, k - 1)]
        vs = [partial(f, k, t, n) for f in (v_inner, v_ds) for t, n in srows]
        vs += pre[k : k + 1]
        weave(ms, vs)
    m_dv(nu - 1)
    m_dk(nu - 1)
    m_dq(nu - 1)
    acc = {}

    def m_da():
        da_scr[...] = dot(d_scr[...], w_ref[...], 1, 1)

    def m_tq(c, w):
        tq_ref[:, c : c + w] += dot(at_scr[...], d_scr[:, c : c + w])

    def add(key, v):
        f = v.shape[0] // 8 * 8
        if f:
            x = jnp.sum(v[:f].reshape(f // 8, 8, D), axis=0)
            acc[key] = x if key not in acc else acc[key] + x
        if f < v.shape[0]:
            x = jnp.sum(v[f:], axis=0, keepdims=True)
            key = key + "tail"
            acc[key] = x if key not in acc else acc[key] + x

    def v_back(i, t, n):
        at = slice(i * SP + t, i * SP + t + n)
        d = da_scr[at, :]
        xh = xh_ref[i, t : t + n, :]
        dxh = d * gain
        mean1 = jnp.mean(dxh, axis=-1, keepdims=True)
        mean2 = jnp.mean(dxh * xh, axis=-1, keepdims=True)
        y = r_ref[i, t : t + n, 0:1] * (dxh - mean1 - xh * mean2)
        for c in range(gs.shape[0]):
            gs[c, pl.ds(pl.multiple_of((j * PAIR + i) * TP + t, 8), n), :] = y[:, c * 128 : (c + 1) * 128]
        add("g", d * xh)
        add("e", d)

    cols = tiles(W3, 256)
    m_da()
    weave([partial(m_tq, c, w) for c, w in cols], [partial(v_back, i, t, n) for i in range(PAIR) for t, n in rows])
    tv_ref[0:8, :] += acc["g"]
    tv_ref[8:16, :] += acc["e"]
    if "gtail" in acc:
        tv_ref[0:1, :] += acc["gtail"]
        tv_ref[8:9, :] += acc["etail"]

    @pl.when(j == pl.num_programs(1) - 1)
    def _():
        for t in range(0, SEQ - 1, 2):
            gi_ref[t : t + 2] = (tokens(gs, t, TP) + dx1_ref[t : t + 2]).astype(BF)
        if SEQ % 2:
            gi_ref[SEQ - 1] = (token(gs, SEQ - 1, TP) + dx1_ref[SEQ - 1]).astype(BF)

    @pl.when((j == pl.num_programs(1) - 1) & (g == pl.num_programs(0) - 1))
    def _():
        for i in range(2):
            gv_ref[i : i + 1, :] = jnp.sum(tv_ref[8 * i : 8 * i + 8, :], axis=0, keepdims=True)
        for i in range(2, 6):
            gv_ref[i : i + 1, :] = jnp.sum(tv2_ref[8 * i : 8 * i + 8, :], axis=0, keepdims=True)
        if np_:
            r = D // np_
            nb = FF // np_
            sm[...] = jnp.zeros_like(sm)
            bias = jnp.sum(tc1_ref[...], axis=0, keepdims=True)
            for s in range(np_):
                sm[s, 0:6, 0:r] = gv_ref[0:6, s * r : (s + 1) * r]
                sm[s, 6:7, 0:nb] = bias[:, s * nb : (s + 1) * nb]
            wide = sm.shape[2]
            for k in range(0, np_, 2):
                for ref, flip in ((keep_ref, 0), (snd_ref, 1)):
                    s = me_ref[0] ^ (k + flip)
                    ref[k // 2, 0:r, :] = tq_ref[pl.ds(pl.multiple_of(s * r, 16), r), :].astype(ref.dtype)
                    ref[k // 2, r : r + EXTRA, 0:wide] = sm[s].astype(ref.dtype)
                    ref[k // 2, r : r + EXTRA, wide:] = jnp.zeros((EXTRA, W3 - wide), ref.dtype)


def back(me, a, xh, r, qkv, probs, do, dx1, w, vec, tc1, tv2, deps, SEQ, np_):
    N, SP, D = a.shape
    TP = do.shape[0]
    W3 = 3 * D
    FF = tc1.shape[1]
    R = PAIR * SP
    tok = lambda t: pl.BlockSpec((t, GROUP, D), lambda g, j, *_: (0, g, 0))
    img = lambda r, d: pl.BlockSpec((PAIR, r, d), lambda g, j, *_: (g * (GROUP // PAIR) + j, 0, 0))
    v = pltpu.VMEM
    s = jax.ShapeDtypeStruct
    prob = pl.BlockSpec((PAIR, D // HEAD_DIM, SP, SP), lambda g, j, *_: (g * (GROUP // PAIR) + j, 0, 0, 0))
    out_specs = [tok(SEQ)]
    out_shape = [s((SEQ, N, D), BF)]
    if np_:
        shape = (np_ // 2, D // np_ + EXTRA, W3)
        out_specs += [whole(*shape)] * 2
        out_shape += [s(shape, BF), s(shape, F32)]
        scratch = [v((D, W3), F32), v((np_, EXTRA, up(max(FF, D) // np_, 128)), F32), v((8, D), F32)]
    else:
        out_specs += [whole(D, W3), whole(8, D)]
        out_shape += [s((D, W3), F32), s((8, D), F32)]
        scratch = []
    scratch += [v((D // 128, TP * GROUP, 128), F32)] * 2
    scratch += [v((R, D), BF), v((D, R), BF), v((R, W3), BF), v((R, D), F32)]
    scratch += [v((16, D), F32)] + [v((SP, SP), F32)] * 2 + [v((SP, SP), BF)] * 2
    return pl.pallas_call(
        partial(back_body, SEQ, SP, TP, D, FF, np_, len(deps)),
        grid_spec=pltpu.PrefetchScalarGridSpec(
            num_scalar_prefetch=1,
            grid=(N // GROUP, GROUP // PAIR),
            in_specs=[img(SP, D), img(SP, D), img(SP, 128), img(SP, W3), prob, tok(TP), tok(TP)]
            + [full(w), full(vec), full(tc1), full(tv2)]
            + [pl.BlockSpec(memory_space=pl.ANY)] * len(deps),
            out_specs=out_specs,
            scratch_shapes=scratch,
        ),
        out_shape=out_shape,
        name="back",
        **params(40 * 10**9, 30 * 10**6),
    )(me, a, xh, r, qkv, probs, do, dx1, w, vec, tc1, tv2, *deps)


def adam_body(np_, count, slots, where, flag_ref, gid_ref, scale_ref, *refs):
    pieces, refs = refs[:np_], refs[np_:]
    weights, firsts, seconds, outs = refs[:count], refs[count : 2 * count], refs[2 * count : 3 * count], refs[3 * count :]
    for k, (p, row, col) in enumerate(where):
        r, c = weights[k].shape
        xs = [x[row : row + r, col : col + c].astype(F32) for x in pieces]
        grad = (xs[0] if len(xs) == 1 else (xs[0] + xs[1]) + (xs[2] + xs[3])) / slots
        flag = flag_ref[p].astype(F32)
        lr = scale_ref[gid_ref[p]]
        first = BETA_ONE * firsts[k][...] + (1.0 - BETA_ONE) * grad
        second = BETA_TWO * seconds[k][...] + (1.0 - BETA_TWO) * grad * grad
        direction = first / (1.0 - BETA_ONE**ADAM_STEPS) / (jnp.sqrt(second / (1.0 - BETA_TWO**ADAM_STEPS)) + ADAM_EPS)
        weight = weights[k][...]
        outs[k][...] = grad
        outs[count + k][...] = weight - LEARN_RATE * lr * (direction + DECAY_RATE * flag * weight)
        outs[2 * count + k][...] = first
        outs[3 * count + k][...] = second


def adam(flags, gids, scales, pieces, arrays, slots, where):
    smem = pl.BlockSpec(memory_space=pltpu.SMEM)
    vmem = pl.BlockSpec(memory_space=pltpu.VMEM)
    mine = [[xs[p] for p, _, _ in where] for xs in arrays]
    shapes = [jax.ShapeDtypeStruct(w.shape, F32) for w in mine[0]]
    return pl.pallas_call(
        partial(adam_body, len(pieces), len(where), slots, where),
        in_specs=[smem] * 3 + [vmem] * (len(pieces) + 3 * len(where)),
        out_specs=[vmem] * (4 * len(where)),
        out_shape=shapes * 4,
        name="adam",
        **params(10**9, 5 * 10**6),
    )(flags, gids, scales, *pieces, *mine[0], *mine[1], *mine[2])


def pairs(n, k):
    return [(i, i ^ k) for i in range(n)]


def touch_body(*refs):
    pass


def touch(dep, xs):
    spec = pl.BlockSpec(memory_space=pl.ANY)
    return pl.pallas_call(
        touch_body,
        in_specs=[spec] * (len(xs) + 1),
        out_specs=[spec] * len(xs),
        out_shape=[jax.ShapeDtypeStruct(x.shape, x.dtype) for x in xs],
        input_output_aliases={k: k for k in range(len(xs))},
        name="touch",
    )(*xs, dep)


def fetch(x, n):
    return [x] + [lax.ppermute(x, "fsdp", pairs(n, k)) for k in range(2, n, 2)]


def fetch_core(own, n):
    other = [lax.ppermute(x, "fsdp", pairs(n, 1)) for x in own]
    return [x for both in zip(own, other) for x in both]


def halve(snd, keep, n):
    h = keep + lax.ppermute(snd, "fsdp", pairs(n, 1)).astype(F32)
    return h[0], [h[k].astype(BF) for k in range(1, n // 2)]


def along_z(xs, n):
    return [lax.ppermute(x, "fsdp", pairs(n, 2 * k + 2)) for k, x in enumerate(xs)]


def finish(own, got, d):
    for piece in got:
        own = own + piece.astype(F32)
    b = own.astype(BF)
    return [b] + [lax.ppermute(b, "dp", pairs(d, k)) for k in range(1, d)]


def local(
    images, cotangent, counts,
    w_qkv, w_proj, w_fc1, w_fc2, b_fc1, vectors,
    m_qkv, m_proj, m_fc1, m_fc2, m_bias1, m_vectors,
    v_qkv, v_proj, v_fc1, v_fc2, v_bias1, v_vectors,
    decay_flags, group_ids, group_scales,
):
    n = lax.axis_size("fsdp")
    d = lax.axis_size("dp")
    N, SEQ, D = images.shape
    r = w_qkv.shape[0]
    FF = w_fc1.shape[1]
    T = 20
    TP = up(SEQ, T)
    direct = n in (2, 4, 8) and d == 4 and r % 16 == 0
    x = jnp.transpose(images, (1, 0, 2))
    cot = jnp.transpose(cotangent, (1, 0, 2))
    me = lax.axis_index("fsdp").astype(jnp.int32).reshape(1)
    rows = lambda b: b.reshape(1, -1)
    weights = [w_qkv, w_proj, w_fc1, w_fc2.T, rows(b_fc1), vectors]
    firsts = [m_qkv, m_proj, m_fc1, m_fc2.T, rows(m_bias1), m_vectors]
    seconds = [v_qkv, v_proj, v_fc1, v_fc2.T, rows(v_bias1), v_vectors]
    pack_a, pack_b = pack(weights[0], weights[5], weights[4], weights[2], weights[3], weights[1])
    xh, rf = norm(x)
    if direct:
        half_a = touch(rf, fetch(pack_a, n))
        pieces_a = fetch_core(half_a, n)
        half_b = fetch(touch(half_a[-1], [pack_b])[0], n)
        qkv, o, probs, a, wq, vec, c1 = attend(me, xh, pieces_a, None, None, FF, SEQ, TP)
        pieces_b = fetch_core(touch(vec, half_b), n)
        out, dx1, do, tc1, tv2, snd, keep = feed(me, counts, x, o, cot, c1, vec, pieces_b, (), T)
        own_b, sends = halve(snd, keep, n)
        got_b = along_z(sends, n)
        gi, snd, keep = back(me, a, xh, rf, qkv, probs, do, dx1, wq, vec, tc1, tv2, sends, SEQ, n)
        snd, *got_b = touch(vec, [snd, *got_b])
        own_a, sends = halve(snd, keep, n)
        got_a = along_z(sends, n)
        pb = finish(own_b, got_b, d)
        pa = finish(own_a, got_a, d)
    else:
        all_a = lax.all_gather(pack_a, "fsdp", axis=0, tiled=False)
        all_b = lax.all_gather(pack_b, "fsdp", axis=0, tiled=True)
        wq = all_a[:, :r].reshape(D, 3 * D)
        nb = FF // n
        vec = jnp.transpose(all_a[:, r : r + 8, :r], (1, 0, 2)).reshape(8, D).astype(F32)
        c1 = jnp.broadcast_to(all_a[:, r + 6, :nb].reshape(1, FF), (8, FF)).astype(F32)
        ws = (all_b[:, 2 * FF :], all_b[:, :FF], all_b[:, FF : 2 * FF])
        qkv, o, probs, a = attend(me, xh, (), wq, vec, FF, SEQ, TP)
        out, dx1, do, tc1, tv2, tp, t1, t2 = feed(me, counts, x, o, cot, c1, vec, (), ws, T)
        gi, tq, gv = back(me, a, xh, rf, qkv, probs, do, dx1, wq, vec, tc1, tv2, (), SEQ, 0)
        share = lambda g, axis: lax.psum(
            lax.psum_scatter(g, "fsdp", scatter_dimension=axis, tiled=True).astype(BF), "dp"
        ).astype(F32)
        pb = [share(jnp.concatenate([t1, t2, tp], axis=1), 0)]
        small = jnp.zeros((8, 3 * D), F32).at[:6, :r].set(share(gv[:6], 1))
        small = small.at[6, :nb].set(share(jnp.sum(tc1, axis=0), 0))
        pa = [jnp.concatenate([share(tq, 0), small], axis=0)]
    arrays = (weights, firsts, seconds)
    slots = float(N * n * d)
    where_a = ((0, 0, 0), (4, r + 6, 0), (5, r, 0))
    where_b = ((1, 0, 2 * FF), (2, 0, 0), (3, 0, FF))
    res = [None] * 24
    for pieces, where in ((pb, where_b), (pa, where_a)):
        got = adam(decay_flags, group_ids, group_scales, pieces, arrays, slots, where)
        for j in range(4):
            for k, (p, _, _) in enumerate(where):
                res[6 * j + p] = got[3 * j + k]
    for k in range(4):
        res[6 * k + 3] = res[6 * k + 3].T
        res[6 * k + 4] = res[6 * k + 4].reshape(-1)
    return (jnp.transpose(out, (1, 0, 2)), jnp.transpose(gi, (1, 0, 2)), *res)


def solution(mesh):
    P = PartitionSpec
    both = ("dp", "fsdp")
    six = (P("fsdp", None), P("fsdp", None), P("fsdp", None), P(None, "fsdp"), P("fsdp"), P(None, "fsdp"))
    data = (P(both, None, None), P(both, None, None))
    return jax.shard_map(
        local,
        mesh=mesh,
        in_specs=(*data, P(both), *six, *six, *six, P(), P(), P()),
        out_specs=(*data, *six, *six, *six, *six),
        check_vma=False,
    )
```

```python
import math
from functools import partial

import jax
import jax.numpy as jnp
from jax import lax
from jax.experimental import pallas as pl
from jax.experimental.pallas import tpu as pltpu
from jax.sharding import PartitionSpec

BF = jnp.bfloat16
F32 = jnp.float32
HEAD_DIM = 64
EPS_LN = 1e-06
LEARN_RATE = 0.2
BETA_ONE = 0.9
BETA_TWO = 0.999
ADAM_EPS = 1e-08
DECAY_RATE = 0.5
ADAM_STEPS = 10.0
GROUP = 8
PAIR = 4
EXTRA = 8
ROOT_HALF = math.sqrt(0.5)


def up(n, m):
    return (n + m - 1) // m * m


def dot(a, b, ca=1, cb=0):
    return lax.dot_general(a, b, (((ca,), (cb,)), ((), ())), preferred_element_type=F32)


def tiles(n, w):
    return [(a, min(w, n - a)) for a in range(0, n, w)]


def params(flops=0, nbytes=0):
    return dict(
        compiler_params=pltpu.CompilerParams(vmem_limit_bytes=58 << 20),
        cost_estimate=pl.CostEstimate(flops=flops, bytes_accessed=nbytes, transcendentals=0),
    )


def weave(ms, vs):
    k = 0
    for a, f in enumerate(ms):
        f()
        while k * len(ms) < len(vs) * (a + 1):
            vs[k]()
            k += 1
    for f in vs[k:]:
        f()


def norm_rows(x):
    c = x - jnp.mean(x, axis=-1, keepdims=True)
    r = lax.rsqrt(jnp.mean(c * c, axis=-1, keepdims=True) + EPS_LN)
    return c * r, r


def gelu_pair(u):
    phi = 0.5 + 0.5 * lax.erf(u * ROOT_HALF)
    e = jnp.exp2((-0.5 * math.log2(math.e)) * (u * u))
    return u * phi, phi + (u * (1.0 / math.sqrt(2.0 * math.pi))) * e


def full(a):
    return pl.BlockSpec(a.shape, lambda *_: (0,) * len(a.shape))


def whole(*shape):
    return pl.BlockSpec(shape, lambda *_: (0,) * len(shape))


def spread(src, dst, seq):
    for t, n in tiles(seq, 20):
        x = src[t : t + n].astype(F32).reshape(n * GROUP, src.shape[2])
        for c in range(dst.shape[0]):
            dst[c, t * GROUP : (t + n) * GROUP, :] = x[:, c * 128 : (c + 1) * 128]


def image(ref, i, t, n):
    return jnp.concatenate(
        [ref[c, pl.ds(t * GROUP + i, n, stride=GROUP), :] for c in range(ref.shape[0])], axis=1
    )


def token(ref, t, tp):
    return jnp.concatenate(
        [ref[c, pl.ds(t, GROUP, stride=tp), :] for c in range(ref.shape[0])], axis=1
    )


def tokens(ref, t, tp):
    return jnp.stack([token(ref, t, tp), token(ref, t + 1, tp)])


def pack_body(r, wq_ref, vec_ref, b_ref, w1_ref, w2_ref, wp_ref, a_ref, b_out, sm):
    FF = w1_ref.shape[1]
    a_ref[0:r, :] = wq_ref[...].astype(BF)
    sm[...] = jnp.zeros_like(sm)
    sm[0 : vec_ref.shape[0], 0 : vec_ref.shape[1]] = vec_ref[...]
    sm[6:7, 0 : b_ref.shape[1]] = b_ref[...]
    a_ref[r : r + EXTRA, :] = sm[...].astype(BF)
    b_out[:, 0:FF] = w1_ref[...].astype(BF)
    b_out[:, FF : 2 * FF] = w2_ref[...].astype(BF)
    b_out[:, 2 * FF :] = wp_ref[...].astype(BF)


def pack(wq, vec, b, w1, w2t, wp):
    r, W3 = wq.shape
    FF = w1.shape[1]
    C = 2 * FF + wp.shape[1]
    return pl.pallas_call(
        partial(pack_body, r),
        out_shape=[jax.ShapeDtypeStruct((r + EXTRA, W3), BF), jax.ShapeDtypeStruct((r, C), BF)],
        scratch_shapes=[pltpu.VMEM((EXTRA, W3), F32)],
        name="pack",
        **params(),
    )(wq, vec, b, w1, w2t, wp)


def norm_body(SEQ, D, x_ref, xh_ref, r_ref, xs):
    j = pl.program_id(1)

    @pl.when(j == 0)
    def _():
        spread(x_ref, xs, SEQ)

    for i in range(PAIR):
        for t, n in tiles(SEQ, 48):
            xh, r = norm_rows(image(xs, j * PAIR + i, t, n))
            xh_ref[i, t : t + n, :] = xh
            r_ref[i, t : t + n, :] = jnp.broadcast_to(r, (n, 128))


def norm(x):
    SEQ, N, D = x.shape
    SP = up(SEQ, 16)
    tok = pl.BlockSpec((SEQ, GROUP, D), lambda g, j: (0, g, 0))
    img = lambda d: pl.BlockSpec((PAIR, SP, d), lambda g, j: (g * (GROUP // PAIR) + j, 0, 0))
    return pl.pallas_call(
        partial(norm_body, SEQ, D),
        grid=(N // GROUP, GROUP // PAIR),
        in_specs=[tok],
        out_specs=[img(D), img(128)],
        out_shape=[jax.ShapeDtypeStruct((N, SP, d), F32) for d in (D, 128)],
        scratch_shapes=[pltpu.VMEM((D // 128, up(SEQ, 8) * GROUP, 128), F32)],
        name="norm",
        **params(8 * 10**9, 15 * 10**6),
    )(x)


def attend_body(SEQ, SP, TP, D, np_, me_ref, xh_ref, *refs):
    H = D // HEAD_DIM
    g = pl.program_id(0)
    j = pl.program_id(1)
    if np_:
        pieces, refs = refs[:np_], refs[np_:]
        qkv_ref, o_ref, p_ref, a_ref, w_ref, vec_ref, c1_ref, sm = refs[:8]
        refs = refs[8:]
    else:
        w_ref, vec_ref, qkv_ref, o_ref, p_ref, a_ref = refs[:6]
        refs = refs[6:]
    os_, a_scr, s0, s1 = refs

    @pl.when((g == 0) & (j == 0))
    def _():
        for ref in (a_scr, os_):
            ref[...] = jnp.zeros_like(ref)
        if np_:
            r = pieces[0].shape[0] - EXTRA
            for k in range(np_):
                s = me_ref[0] ^ k
                w_ref[pl.ds(pl.multiple_of(s * r, 16), r), :] = pieces[k][0:r, :]
                sm[s] = pieces[k][r : r + EXTRA, 0 : sm.shape[2]].astype(F32)
            nb = c1_ref.shape[1] // np_
            vec_ref[...] = jnp.concatenate([sm[s, :, 0:r] for s in range(np_)], axis=1)
            c1_ref[...] = jnp.broadcast_to(
                jnp.concatenate([sm[s, 6:7, 0:nb] for s in range(np_)], axis=1), c1_ref.shape
            )

    gain = vec_ref[0:1, :]
    shift = vec_ref[1:2, :]
    ss = (s0, s1)
    st = {}
    S8 = SEQ // 16 * 16

    def ln(i, t, n):
        y = (xh_ref[i, t : t + n, :] * gain + shift).astype(BF)
        a_scr[i * SP + t : i * SP + t + n, :] = y
        a_ref[i, t : t + n, :] = y

    def qkv(t, c, w):
        y = dot(a_scr[...], w_ref[:, t * D + c : t * D + c + w])
        if t == 0:
            y = y * (HEAD_DIM**-0.5)
        qkv_ref[:, :, t * D + c : t * D + c + w] = y.astype(BF).reshape(PAIR, SP, w)

    def score(u):
        i, h = divmod(u, H)
        lo = h * HEAD_DIM
        ss[u % 2][...] = dot(
            qkv_ref[i, :, D + lo : D + lo + HEAD_DIM], qkv_ref[i, :, lo : lo + HEAD_DIM], 1, 1
        )

    def tile(ref, t, n):
        x = ref[t : t + n, :]
        if t + n > SEQ:
            x = jnp.where(lax.broadcasted_iota(jnp.int32, (n, 1), 0) < SEQ - t, x, -1e30)
        return x

    def vmax(u, t, n):
        m = jnp.max(tile(ss[u % 2], t, n).reshape(n // 8, 8, SP), axis=0)
        st[u] = m if t == 0 else jnp.maximum(st[u], m)
        if t + n >= SEQ:
            st[u] = jnp.max(st[u], axis=0, keepdims=True)

    def vexp(u, t, n):
        p = jnp.exp(tile(ss[u % 2], t, n) - st[u])
        ss[u % 2][t : t + n, :] = p
        total = jnp.sum(p.reshape(n // 8, 8, SP), axis=0)
        k = ("l", u)
        st[k] = total if t == 0 else st[k] + total
        if t + n >= SEQ:
            total = jnp.sum(st[k], axis=0, keepdims=True)
            st[k] = 1.0 / total

    def vnorm(u, t, n):
        i, h = divmod(u, H)
        p_ref[i, h, t : t + n, :] = (ss[u % 2][t : t + n, :] * st[("l", u)]).astype(BF)

    def mix(u):
        i, h = divmod(u, H)
        lo = 2 * D + h * HEAD_DIM
        y = dot(p_ref[i, h], qkv_ref[i, :, lo : lo + HEAD_DIM], 0, 0)
        if h % 2 == 0:
            st["o"] = y
        else:
            y = jnp.concatenate([st["o"], y], axis=1)
            os_[h // 2, pl.ds(pl.multiple_of((j * PAIR + i) * TP, 8), SEQ), :] = y[:SEQ]

    for i in range(PAIR):
        for t, n in tiles(SEQ, 48):
            ln(i, t, n)
    c0 = min(256, D)
    hb = c0 // HEAD_DIM
    for t in range(3):
        qkv(t, 0, c0)
    rest = [partial(qkv, t, c, w) for c, w in tiles(D, 256)[1:] for t in range(3)]
    srows = tiles(S8, 64) + ([(S8, SP - S8)] if S8 < SEQ else [])
    order = [i * H + h for i in range(PAIR) for h in range(hb)]
    order += [i * H + h for i in range(PAIR) for h in range(hb, H)]
    nu = len(order)
    score(order[0])
    for k, u in enumerate(order):
        ms = rest[k : k + 1]
        if k + 1 < nu:
            ms.append(partial(score, order[k + 1]))
        if k >= 1:
            ms.append(partial(mix, order[k - 1]))
        vs = [partial(f, u, t, n) for f in (vmax, vexp, vnorm) for t, n in srows]
        weave(ms, vs)
    nu = order[-1] + 1
    mix(nu - 1)
    for i in range(PAIR):
        a_ref[i, SEQ:SP, :] = jnp.zeros((SP - SEQ, D), BF)

    @pl.when(j == pl.num_programs(1) - 1)
    def _():
        for t in range(0, TP, 2):
            o_ref[t : t + 2] = tokens(os_, t, TP).astype(BF)


def attend(me, xh, pieces, w, vec, FF, SEQ, TP):
    N, SP, D = xh.shape
    W3 = 3 * D
    np_ = len(pieces)
    tok = lambda t: pl.BlockSpec((t, GROUP, D), lambda g, j, *_: (0, g, 0))
    img = lambda r, d: pl.BlockSpec((PAIR, r, d), lambda g, j, *_: (g * (GROUP // PAIR) + j, 0, 0))
    probs = pl.BlockSpec((PAIR, D // HEAD_DIM, SP, SP), lambda g, j, *_: (g * (GROUP // PAIR) + j, 0, 0, 0))
    v = pltpu.VMEM
    s = jax.ShapeDtypeStruct
    ins = list(pieces) if np_ else [w, vec]
    out_specs = [img(SP, W3), tok(TP), probs, img(SP, D)]
    out_shape = [s((N, SP, W3), BF), s((TP, N, D), BF), s((N, D // HEAD_DIM, SP, SP), BF), s((N, SP, D), BF)]
    scratch = [v((D // 128, TP * GROUP, 128), F32), v((PAIR * SP, D), BF)]
    scratch += [v((SP, SP), F32)] * 2
    if np_:
        out_specs += [whole(D, W3), whole(8, D), whole(8, FF)]
        out_shape += [s((D, W3), BF), s((8, D), F32), s((8, FF), F32)]
        scratch = [v((np_, EXTRA, up(max(FF, D) // np_, 128)), F32)] + scratch
    return pl.pallas_call(
        partial(attend_body, SEQ, SP, TP, D, np_),
        grid_spec=pltpu.PrefetchScalarGridSpec(
            num_scalar_prefetch=1,
            grid=(N // GROUP, GROUP // PAIR),
            in_specs=[img(SP, D)] + [full(a) for a in ins],
            out_specs=out_specs,
            scratch_shapes=scratch,
        ),
        out_shape=out_shape,
        name="attend",
        **params(20 * 10**9, 25 * 10**6),
    )(me, xh, *ins)


def feed_body(SEQ, D, FF, T, N, np_, me_ref, cnt_ref, x_ref, o_ref, cot_ref, c1_ref, vec_ref, *refs):
    s = pl.program_id(0)
    R = T * N
    RT = 2 * N
    HR = R // 2
    if np_:
        pieces, refs = refs[:np_], refs[np_:]
        out_ref, dx1_ref, do_ref, tc1_ref, tv_ref, snd_ref, keep_ref = refs[:7]
        wp_ref, w1_ref, w2t_ref, tp_ref, t1_ref, t2_ref = refs[7:13]
        refs = refs[13:]
    else:
        wp_ref, w1_ref, w2t_ref, out_ref, dx1_ref, do_ref, tc1_ref, tv_ref, tp_ref, t1_ref, t2_ref = refs[:11]
        refs = refs[11:]
    b_scr, bt_scr, dy_scr, dyt_scr, xh_scr, r_scr, x1_scr, u0, u1, d0, d1, g_scr, du_scr, y_scr, db_scr, dx_scr = refs

    @pl.when(s == 0)
    def _():
        for ref in (tp_ref, t1_ref, t2_ref, tc1_ref, tv_ref, bt_scr, dyt_scr, g_scr, du_scr):
            ref[...] = jnp.zeros_like(ref)
        if np_:
            r = pieces[0].shape[0]
            for k in range(np_):
                at = pl.ds(pl.multiple_of((me_ref[0] ^ k) * r, 16), r)
                w1_ref[at, :] = pieces[k][:, 0:FF]
                w2t_ref[at, :] = pieces[k][:, FF : 2 * FF]
                wp_ref[at, :] = pieces[k][:, 2 * FF :]

    cp = vec_ref[2:3, :]
    g2 = vec_ref[3:4, :]
    e2 = vec_ref[4:5, :]
    c2 = vec_ref[5:6, :]
    io = lax.broadcasted_iota(jnp.int32, (RT, 1), 0)
    real = lax.rem(io, N) < cnt_ref[0]
    lim = SEQ * N - s * R
    acc = {}

    def rows(ref, r):
        return ref[r // N : r // N + 2].reshape(RT, D)

    def add(key, v):
        v = jnp.sum(v.reshape(v.shape[0] // 8, 8, v.shape[1]), axis=0)
        acc[key] = v if key not in acc else acc[key] + v

    def m_proj(h):
        x1_scr[h : h + HR, :] = dot(o_ref[h // N : (h + HR) // N].reshape(HR, D), wp_ref[...])

    def v_norm(r):
        inside = (io + r) < lim
        x = jnp.where(inside, rows(x_ref, r).astype(F32), 0.0)
        dy_scr[r : r + RT, :] = jnp.where(real & inside, rows(cot_ref, r), jnp.zeros((), BF))
        x1 = x + x1_scr[r : r + RT, :] + cp
        x1_scr[r : r + RT, :] = x1 + c2
        xh, rr = norm_rows(x1)
        xh_scr[r : r + RT, :] = xh
        r_scr[r : r + RT, :] = jnp.broadcast_to(rr, (RT, 128))
        b_scr[r : r + RT, :] = (xh * g2 + e2).astype(BF)

    cols = tiles(FF, 256)
    us = (u0, u1)
    ds = (d0, d1)

    def m_u(i, h, HR=HR):
        c, w = cols[i]
        us[i % 2][h : h + HR, :w] = dot(b_scr[h : h + HR, :], w1_ref[:, c : c + w]) + c1_ref[0:1, c : c + w]

    def m_d(i, h, HR=HR):
        c, w = cols[i]
        ds[i % 2][h : h + HR, :w] = dot(dy_scr[h : h + HR, :], w2t_ref[:, c : c + w])

    def v_gelu(i, r):
        c, w = cols[i]
        ga, dg = gelu_pair(us[i % 2][r : r + 16, :w])
        g_scr[r : r + 16, c : c + w] = ga.astype(BF)
        du = ds[i % 2][r : r + 16, :w] * dg
        du_scr[r : r + 16, c : c + w] = du.astype(BF)
        add(("c1", i), du)

    def m_t1(i):
        c, w = cols[i]
        t1_ref[:, c : c + w] += dot(bt_scr[...], du_scr[:, c : c + w])

    def m_t2(i):
        c, w = cols[i]
        t2_ref[:, c : c + w] += dot(dyt_scr[...], g_scr[:, c : c + w])

    def m_y(h, HR=HR):
        y_scr[h : h + HR, :] = dot(g_scr[h : h + HR, :], w2t_ref[...], 1, 1)

    def m_db(h, HR=HR):
        db_scr[h : h + HR, :] = dot(du_scr[h : h + HR, :], w1_ref[...], 1, 1)

    def v_out(r):
        y = x1_scr[r : r + RT, :] + y_scr[r : r + RT, :]
        out_ref[r // N : r // N + 2] = jnp.where(real, y, 0.0).astype(BF).reshape(2, N, D)

    def v_back(r):
        db = db_scr[r : r + RT, :]
        xh = xh_scr[r : r + RT, :]
        dyf = dy_scr[r : r + RT, :].astype(F32)
        dxh = db * g2
        mean1 = jnp.mean(dxh, axis=-1, keepdims=True)
        mean2 = jnp.mean(dxh * xh, axis=-1, keepdims=True)
        dx = dyf + r_scr[r : r + RT, 0:1] * (dxh - mean1 - xh * mean2)
        add("g2", db * xh)
        add("e2", db)
        add("c2", dyf)
        add("cp", dx)
        dx1_ref[r // N : r // N + 2] = dx.reshape(2, N, D)
        dx_scr[r : r + RT, :] = dx.astype(BF)

    def m_do(h):
        y = dot(dx_scr[h : h + HR, :], wp_ref[...], 1, 1)
        do_ref[h // N : (h + HR) // N] = y.astype(BF).reshape(HR // N, N, D)

    def m_tp():
        tp_ref[...] += dot(o_ref[...].reshape(R, D), dx_scr[...], 0, 0)

    first = list(range(0, HR, RT))
    second = list(range(HR, R, RT))
    last = len(cols) - 1
    def turn(dst, src):
        dst[...] = src[...].T

    m_proj(0)
    weave([partial(m_proj, HR), partial(m_t1, last)], [partial(v_norm, r) for r in first])
    weave([partial(m_t2, last), partial(m_u, 0, 0), partial(m_d, 0, 0)], [partial(v_norm, r) for r in second])
    weave([partial(m_u, 0, HR), partial(m_d, 0, HR)], [partial(turn, bt_scr, b_scr), partial(turn, dyt_scr, dy_scr)])
    for i in range(len(cols)):
        ms = []
        if i < last:
            ms += [partial(f, i + 1, 0, R) for f in (m_u, m_d)]
        if i >= 1:
            ms += [partial(m_t1, i - 1), partial(m_t2, i - 1)]
        weave(ms, [partial(v_gelu, i, r) for r in range(0, R, 16)])
        c, w = cols[i]
        tc1_ref[:, c : c + w] += acc[("c1", i)]
    m_db(0, R)
    weave([partial(m_y, 0, R)], [partial(v_back, r) for r in first + second])
    weave([partial(m_do, 0), partial(m_do, HR), m_tp], [partial(v_out, r) for r in first + second])
    for i, k in ((2, "cp"), (3, "g2"), (4, "e2"), (5, "c2")):
        tv_ref[i * 8 : i * 8 + 8, :] += acc[k]

    @pl.when(s == pl.num_programs(0) - 1)
    def _():
        m_t1(last)
        m_t2(last)
        if np_:
            r = D // np_
            for k in range(0, np_, 2):
                for ref, flip in ((keep_ref, 0), (snd_ref, 1)):
                    at = pl.ds(pl.multiple_of((me_ref[0] ^ (k + flip)) * r, 16), r)
                    ref[k // 2, :, 0:FF] = t1_ref[at, :].astype(ref.dtype)
                    ref[k // 2, :, FF : 2 * FF] = t2_ref[at, :].astype(ref.dtype)
                    ref[k // 2, :, 2 * FF :] = tp_ref[at, :].astype(ref.dtype)


def feed(me, cnt, x, o, cot, c1, vec, pieces, weights, T):
    SEQ, N, D = x.shape
    TP = o.shape[0]
    FF = c1.shape[1]
    np_ = len(pieces)
    R = T * N
    v = pltpu.VMEM
    s = jax.ShapeDtypeStruct
    blk = pl.BlockSpec((T, N, D), lambda i, *_: (i, 0, 0))
    ins = list(pieces) if np_ else list(weights)
    out_specs = [blk, blk, blk, whole(8, FF), whole(64, D)]
    out_shape = [s((SEQ, N, D), BF), s((TP, N, D), F32), s((TP, N, D), BF), s((8, FF), F32), s((64, D), F32)]
    scratch = []
    if np_:
        shape = (np_ // 2, D // np_, 2 * FF + D)
        out_specs += [whole(*shape)] * 2
        out_shape += [s(shape, BF), s(shape, F32)]
        scratch += [v((D, D), BF), v((D, FF), BF), v((D, FF), BF), v((D, D), F32), v((D, FF), F32), v((D, FF), F32)]
    else:
        out_specs += [whole(D, D), whole(D, FF), whole(D, FF)]
        out_shape += [s((D, D), F32), s((D, FF), F32), s((D, FF), F32)]
    scratch += [v((R, D), BF), v((D, R), BF), v((R, D), BF), v((D, R), BF), v((R, D), F32), v((R, 128), F32), v((R, D), F32)]
    scratch += [v((R, 256), F32)] * 4 + [v((R, FF), BF)] * 2 + [v((R, D), F32)] * 2 + [v((R, D), BF)]
    return pl.pallas_call(
        partial(feed_body, SEQ, D, FF, T, N, np_),
        grid_spec=pltpu.PrefetchScalarGridSpec(
            num_scalar_prefetch=2,
            grid=(TP // T,),
            in_specs=[blk, blk, blk, full(c1), full(vec)] + [full(a) for a in ins],
            out_specs=out_specs,
            scratch_shapes=scratch,
        ),
        out_shape=out_shape,
        name="feed",
        **params(45 * 10**9, 30 * 10**6),
    )(me, cnt, x, o, cot, c1, vec, *ins)


def back_body(SEQ, SP, TP, D, FF, np_, DEPS, me_ref, a_ref, xh_ref, r_ref, qkv_ref, p_ref, do_ref, dx1_ref, w_ref, vec_ref, tc1_ref, tv2_ref, *refs):
    gi_ref, refs = refs[DEPS], refs[DEPS + 1 :]
    if np_:
        snd_ref, keep_ref, tq_ref, sm = refs[:4]
        gv_ref, refs = refs[4], refs[5:]
    else:
        tq_ref, gv_ref, refs = refs[0], refs[1], refs[2:]
    dos, gs, dob, at_scr, d_scr, da_scr, tv_ref, e0, e1, q0, q1 = refs
    H = D // HEAD_DIM
    W3 = 3 * D
    g = pl.program_id(0)
    j = pl.program_id(1)

    @pl.when((g == 0) & (j == 0))
    def _():
        for ref in (d_scr, dob, tq_ref, tv_ref):
            ref[...] = jnp.zeros_like(ref)

    @pl.when(j == 0)
    def _():
        spread(do_ref, dos, SEQ)

    gain = vec_ref[0:1, :]
    es = (e0, e1)
    qq = (q0, q1)
    st = {}
    S8 = SEQ // 16 * 16

    def load(i, t, n):
        dob[i * SP + t : i * SP + t + n, :] = image(dos, j * PAIR + i, t, n).astype(BF)

    def part(i, h, t):
        lo = t * D + h * HEAD_DIM
        return qkv_ref[i, :, lo : lo + HEAD_DIM]

    def dpart(i, h):
        return dob[i * SP : (i + 1) * SP, h * HEAD_DIM : (h + 1) * HEAD_DIM]

    def dprob(u):
        i, h = divmod(u, H)
        es[u % 2][...] = dot(part(i, h, 2), dpart(i, h), 1, 1)

    def v_inner(u, t, n):
        x = p_ref[divmod(u, H) + (slice(t, t + n),)].astype(F32) * es[u % 2][t : t + n, :]
        x = jnp.sum(x.reshape(n // 8, 8, SP), axis=0)
        st[u] = x if t == 0 else st[u] + x
        if t + n >= SEQ:
            st[u] = jnp.sum(st[u], axis=0, keepdims=True)

    def v_ds(u, t, n):
        p = p_ref[divmod(u, H) + (slice(t, t + n),)].astype(F32)
        qq[u % 2][t : t + n, :] = (p * (es[u % 2][t : t + n, :] - st[u])).astype(BF)

    def put(u, t, y):
        i, h = divmod(u, H)
        if h % 2 == 0:
            st[("d", t)] = y
        else:
            y = jnp.concatenate([st[("d", t)], y], axis=0).T if t == 0 else jnp.concatenate([st[("d", t)], y], axis=1)
            y = y.astype(BF)
            lo = t * D + (h - 1) * HEAD_DIM
            d_scr[i * SP : i * SP + SEQ, lo : lo + 2 * HEAD_DIM] = y[:SEQ]

    def m_dv(u):
        put(u, 2, dot(p_ref[divmod(u, H)], dpart(*divmod(u, H))))

    def m_dk(u):
        i, h = divmod(u, H)
        put(u, 1, dot(qq[u % 2][...], part(i, h, 0)))

    def m_dq(u):
        i, h = divmod(u, H)
        put(u, 0, dot(part(i, h, 1), qq[u % 2][...], 0, 0) * (HEAD_DIM**-0.5))

    rows = tiles(SEQ, 48)
    srows = tiles(S8, 64) + ([(S8, SP - S8)] if S8 < SEQ else [])
    for t, n in rows:
        load(0, t, n)
    at_scr[...] = a_ref[...].reshape(PAIR * SP, D).T
    pre = [partial(load, i, t, n) for i in range(1, PAIR) for t, n in rows]
    nu = PAIR * H
    dprob(0)
    for k in range(nu):
        ms = []
        if k + 1 < nu:
            ms.append(partial(dprob, k + 1))
        if k >= 1:
            ms += [partial(m_dv, k - 1), partial(m_dk, k - 1), partial(m_dq, k - 1)]
        vs = [partial(f, k, t, n) for f in (v_inner, v_ds) for t, n in srows]
        vs += pre[k : k + 1]
        weave(ms, vs)
    m_dv(nu - 1)
    m_dk(nu - 1)
    m_dq(nu - 1)
    acc = {}

    def m_da():
        da_scr[...] = dot(d_scr[...], w_ref[...], 1, 1)

    def m_tq(c, w):
        tq_ref[:, c : c + w] += dot(at_scr[...], d_scr[:, c : c + w])

    def add(key, v):
        f = v.shape[0] // 8 * 8
        if f:
            x = jnp.sum(v[:f].reshape(f // 8, 8, D), axis=0)
            acc[key] = x if key not in acc else acc[key] + x
        if f < v.shape[0]:
            x = jnp.sum(v[f:], axis=0, keepdims=True)
            key = key + "tail"
            acc[key] = x if key not in acc else acc[key] + x

    def v_back(i, t, n):
        at = slice(i * SP + t, i * SP + t + n)
        d = da_scr[at, :]
        xh = xh_ref[i, t : t + n, :]
        dxh = d * gain
        mean1 = jnp.mean(dxh, axis=-1, keepdims=True)
        mean2 = jnp.mean(dxh * xh, axis=-1, keepdims=True)
        y = r_ref[i, t : t + n, 0:1] * (dxh - mean1 - xh * mean2)
        for c in range(gs.shape[0]):
            gs[c, pl.ds(pl.multiple_of((j * PAIR + i) * TP + t, 8), n), :] = y[:, c * 128 : (c + 1) * 128]
        add("g", d * xh)
        add("e", d)

    cols = tiles(W3, 256)
    m_da()
    weave([partial(m_tq, c, w) for c, w in cols], [partial(v_back, i, t, n) for i in range(PAIR) for t, n in rows])
    tv_ref[0:8, :] += acc["g"]
    tv_ref[8:16, :] += acc["e"]
    if "gtail" in acc:
        tv_ref[0:1, :] += acc["gtail"]
        tv_ref[8:9, :] += acc["etail"]

    @pl.when(j == pl.num_programs(1) - 1)
    def _():
        for t in range(0, SEQ - 1, 2):
            gi_ref[t : t + 2] = (tokens(gs, t, TP) + dx1_ref[t : t + 2]).astype(BF)
        if SEQ % 2:
            gi_ref[SEQ - 1] = (token(gs, SEQ - 1, TP) + dx1_ref[SEQ - 1]).astype(BF)

    @pl.when((j == pl.num_programs(1) - 1) & (g == pl.num_programs(0) - 1))
    def _():
        for i in range(2):
            gv_ref[i : i + 1, :] = jnp.sum(tv_ref[8 * i : 8 * i + 8, :], axis=0, keepdims=True)
        for i in range(2, 6):
            gv_ref[i : i + 1, :] = jnp.sum(tv2_ref[8 * i : 8 * i + 8, :], axis=0, keepdims=True)
        if np_:
            r = D // np_
            nb = FF // np_
            sm[...] = jnp.zeros_like(sm)
            bias = jnp.sum(tc1_ref[...], axis=0, keepdims=True)
            for s in range(np_):
                sm[s, 0:6, 0:r] = gv_ref[0:6, s * r : (s + 1) * r]
                sm[s, 6:7, 0:nb] = bias[:, s * nb : (s + 1) * nb]
            wide = sm.shape[2]
            for k in range(0, np_, 2):
                for ref, flip in ((keep_ref, 0), (snd_ref, 1)):
                    s = me_ref[0] ^ (k + flip)
                    ref[k // 2, 0:r, :] = tq_ref[pl.ds(pl.multiple_of(s * r, 16), r), :].astype(ref.dtype)
                    ref[k // 2, r : r + EXTRA, 0:wide] = sm[s].astype(ref.dtype)
                    ref[k // 2, r : r + EXTRA, wide:] = jnp.zeros((EXTRA, W3 - wide), ref.dtype)


def back(me, a, xh, r, qkv, probs, do, dx1, w, vec, tc1, tv2, deps, SEQ, np_):
    N, SP, D = a.shape
    TP = do.shape[0]
    W3 = 3 * D
    FF = tc1.shape[1]
    R = PAIR * SP
    tok = lambda t: pl.BlockSpec((t, GROUP, D), lambda g, j, *_: (0, g, 0))
    img = lambda r, d: pl.BlockSpec((PAIR, r, d), lambda g, j, *_: (g * (GROUP // PAIR) + j, 0, 0))
    v = pltpu.VMEM
    s = jax.ShapeDtypeStruct
    prob = pl.BlockSpec((PAIR, D // HEAD_DIM, SP, SP), lambda g, j, *_: (g * (GROUP // PAIR) + j, 0, 0, 0))
    out_specs = [tok(SEQ)]
    out_shape = [s((SEQ, N, D), BF)]
    if np_:
        shape = (np_ // 2, D // np_ + EXTRA, W3)
        out_specs += [whole(*shape)] * 2
        out_shape += [s(shape, BF), s(shape, F32)]
        scratch = [v((D, W3), F32), v((np_, EXTRA, up(max(FF, D) // np_, 128)), F32), v((8, D), F32)]
    else:
        out_specs += [whole(D, W3), whole(8, D)]
        out_shape += [s((D, W3), F32), s((8, D), F32)]
        scratch = []
    scratch += [v((D // 128, TP * GROUP, 128), F32)] * 2
    scratch += [v((R, D), BF), v((D, R), BF), v((R, W3), BF), v((R, D), F32)]
    scratch += [v((16, D), F32)] + [v((SP, SP), F32)] * 2 + [v((SP, SP), BF)] * 2
    return pl.pallas_call(
        partial(back_body, SEQ, SP, TP, D, FF, np_, len(deps)),
        grid_spec=pltpu.PrefetchScalarGridSpec(
            num_scalar_prefetch=1,
            grid=(N // GROUP, GROUP // PAIR),
            in_specs=[img(SP, D), img(SP, D), img(SP, 128), img(SP, W3), prob, tok(TP), tok(TP)]
            + [full(w), full(vec), full(tc1), full(tv2)]
            + [pl.BlockSpec(memory_space=pl.ANY)] * len(deps),
            out_specs=out_specs,
            scratch_shapes=scratch,
        ),
        out_shape=out_shape,
        name="back",
        **params(40 * 10**9, 30 * 10**6),
    )(me, a, xh, r, qkv, probs, do, dx1, w, vec, tc1, tv2, *deps)


def adam_body(np_, count, slots, where, flag_ref, gid_ref, scale_ref, *refs):
    pieces, refs = refs[:np_], refs[np_:]
    weights, firsts, seconds, outs = refs[:count], refs[count : 2 * count], refs[2 * count : 3 * count], refs[3 * count :]
    for k, (p, row, col) in enumerate(where):
        r, c = weights[k].shape
        xs = [x[row : row + r, col : col + c].astype(F32) for x in pieces]
        grad = (xs[0] if len(xs) == 1 else (xs[0] + xs[1]) + (xs[2] + xs[3])) / slots
        flag = flag_ref[p].astype(F32)
        lr = scale_ref[gid_ref[p]]
        first = BETA_ONE * firsts[k][...] + (1.0 - BETA_ONE) * grad
        second = BETA_TWO * seconds[k][...] + (1.0 - BETA_TWO) * grad * grad
        direction = first / (1.0 - BETA_ONE**ADAM_STEPS) / (jnp.sqrt(second / (1.0 - BETA_TWO**ADAM_STEPS)) + ADAM_EPS)
        weight = weights[k][...]
        outs[k][...] = grad
        outs[count + k][...] = weight - LEARN_RATE * lr * (direction + DECAY_RATE * flag * weight)
        outs[2 * count + k][...] = first
        outs[3 * count + k][...] = second


def adam(flags, gids, scales, pieces, arrays, slots, where):
    smem = pl.BlockSpec(memory_space=pltpu.SMEM)
    vmem = pl.BlockSpec(memory_space=pltpu.VMEM)
    mine = [[xs[p] for p, _, _ in where] for xs in arrays]
    shapes = [jax.ShapeDtypeStruct(w.shape, F32) for w in mine[0]]
    return pl.pallas_call(
        partial(adam_body, len(pieces), len(where), slots, where),
        in_specs=[smem] * 3 + [vmem] * (len(pieces) + 3 * len(where)),
        out_specs=[vmem] * (4 * len(where)),
        out_shape=shapes * 4,
        name="adam",
        **params(10**9, 5 * 10**6),
    )(flags, gids, scales, *pieces, *mine[0], *mine[1], *mine[2])


def pairs(n, k):
    return [(i, i ^ k) for i in range(n)]


def touch_body(*refs):
    pass


def touch(dep, xs):
    spec = pl.BlockSpec(memory_space=pl.ANY)
    return pl.pallas_call(
        touch_body,
        in_specs=[spec] * (len(xs) + 1),
        out_specs=[spec] * len(xs),
        out_shape=[jax.ShapeDtypeStruct(x.shape, x.dtype) for x in xs],
        input_output_aliases={k: k for k in range(len(xs))},
        name="touch",
    )(*xs, dep)


def fetch(x, n):
    return [x] + [lax.ppermute(x, "fsdp", pairs(n, k)) for k in range(2, n, 2)]


def fetch_core(own, n):
    other = [lax.ppermute(x, "fsdp", pairs(n, 1)) for x in own]
    return [x for both in zip(own, other) for x in both]


def halve(snd, keep, n):
    h = keep + lax.ppermute(snd, "fsdp", pairs(n, 1)).astype(F32)
    return h[0], [h[k].astype(BF) for k in range(1, n // 2)]


def along_z(xs, n):
    return [lax.ppermute(x, "fsdp", pairs(n, 2 * k + 2)) for k, x in enumerate(xs)]


def finish(own, got, d):
    for piece in got:
        own = own + piece.astype(F32)
    b = own.astype(BF)
    return [b] + [lax.ppermute(b, "dp", pairs(d, k)) for k in range(1, d)]


def local(
    images, cotangent, counts,
    w_qkv, w_proj, w_fc1, w_fc2, b_fc1, vectors,
    m_qkv, m_proj, m_fc1, m_fc2, m_bias1, m_vectors,
    v_qkv, v_proj, v_fc1, v_fc2, v_bias1, v_vectors,
    decay_flags, group_ids, group_scales,
):
    n = lax.axis_size("fsdp")
    d = lax.axis_size("dp")
    N, SEQ, D = images.shape
    r = w_qkv.shape[0]
    FF = w_fc1.shape[1]
    T = 20
    TP = up(SEQ, T)
    direct = n in (2, 4, 8) and d == 4 and r % 16 == 0
    x = jnp.transpose(images, (1, 0, 2))
    cot = jnp.transpose(cotangent, (1, 0, 2))
    me = lax.axis_index("fsdp").astype(jnp.int32).reshape(1)
    rows = lambda b: b.reshape(1, -1)
    weights = [w_qkv, w_proj, w_fc1, w_fc2.T, rows(b_fc1), vectors]
    firsts = [m_qkv, m_proj, m_fc1, m_fc2.T, rows(m_bias1), m_vectors]
    seconds = [v_qkv, v_proj, v_fc1, v_fc2.T, rows(v_bias1), v_vectors]
    pack_a, pack_b = pack(weights[0], weights[5], weights[4], weights[2], weights[3], weights[1])
    xh, rf = norm(x)
    if direct:
        half_a = touch(rf, fetch(pack_a, n))
        pieces_a = fetch_core(half_a, n)
        half_b = fetch(touch(half_a[-1], [pack_b])[0], n)
        qkv, o, probs, a, wq, vec, c1 = attend(me, xh, pieces_a, None, None, FF, SEQ, TP)
        pieces_b = fetch_core(touch(vec, half_b), n)
        out, dx1, do, tc1, tv2, snd, keep = feed(me, counts, x, o, cot, c1, vec, pieces_b, (), T)
        own_b, sends = halve(snd, keep, n)
        got_b = along_z(sends, n)
        gi, snd, keep = back(me, a, xh, rf, qkv, probs, do, dx1, wq, vec, tc1, tv2, sends, SEQ, n)
        snd, *got_b = touch(vec, [snd, *got_b])
        own_a, sends = halve(snd, keep, n)
        got_a = along_z(sends, n)
        pb = finish(own_b, got_b, d)
        pa = finish(own_a, got_a, d)
    else:
        all_a = lax.all_gather(pack_a, "fsdp", axis=0, tiled=False)
        all_b = lax.all_gather(pack_b, "fsdp", axis=0, tiled=True)
        wq = all_a[:, :r].reshape(D, 3 * D)
        nb = FF // n
        vec = jnp.transpose(all_a[:, r : r + 8, :r], (1, 0, 2)).reshape(8, D).astype(F32)
        c1 = jnp.broadcast_to(all_a[:, r + 6, :nb].reshape(1, FF), (8, FF)).astype(F32)
        ws = (all_b[:, 2 * FF :], all_b[:, :FF], all_b[:, FF : 2 * FF])
        qkv, o, probs, a = attend(me, xh, (), wq, vec, FF, SEQ, TP)
        out, dx1, do, tc1, tv2, tp, t1, t2 = feed(me, counts, x, o, cot, c1, vec, (), ws, T)
        gi, tq, gv = back(me, a, xh, rf, qkv, probs, do, dx1, wq, vec, tc1, tv2, (), SEQ, 0)
        share = lambda g, axis: lax.psum(
            lax.psum_scatter(g, "fsdp", scatter_dimension=axis, tiled=True).astype(BF), "dp"
        ).astype(F32)
        pb = [share(jnp.concatenate([t1, t2, tp], axis=1), 0)]
        small = jnp.zeros((8, 3 * D), F32).at[:6, :r].set(share(gv[:6], 1))
        small = small.at[6, :nb].set(share(jnp.sum(tc1, axis=0), 0))
        pa = [jnp.concatenate([share(tq, 0), small], axis=0)]
    arrays = (weights, firsts, seconds)
    slots = float(N * n * d)
    where_a = ((0, 0, 0), (4, r + 6, 0), (5, r, 0))
    where_b = ((1, 0, 2 * FF), (2, 0, 0), (3, 0, FF))
    res = [None] * 24
    for pieces, where in ((pb, where_b), (pa, where_a)):
        got = adam(decay_flags, group_ids, group_scales, pieces, arrays, slots, where)
        for j in range(4):
            for k, (p, _, _) in enumerate(where):
                res[6 * j + p] = got[3 * j + k]
    for k in range(4):
        res[6 * k + 3] = res[6 * k + 3].T
        res[6 * k + 4] = res[6 * k + 4].reshape(-1)
    return (jnp.transpose(out, (1, 0, 2)), jnp.transpose(gi, (1, 0, 2)), *res)


def solution(mesh):
    P = PartitionSpec
    both = ("dp", "fsdp")
    six = (P("fsdp", None), P("fsdp", None), P("fsdp", None), P(None, "fsdp"), P("fsdp"), P(None, "fsdp"))
    data = (P(both, None, None), P(both, None, None))
    return jax.shard_map(
        local,
        mesh=mesh,
        in_specs=(*data, P(both), *six, *six, *six, P(), P(), P()),
        out_specs=(*data, *six, *six, *six, *six),
        check_vma=False,
    )
```

```python
import math
from functools import partial

import jax
import jax.numpy as jnp
from jax import lax
from jax.experimental import pallas as pl
from jax.experimental.pallas import tpu as pltpu
from jax.sharding import PartitionSpec

BF = jnp.bfloat16
F32 = jnp.float32
HEAD_DIM = 64
EPS_LN = 1e-06
LEARN_RATE = 0.2
BETA_ONE = 0.9
BETA_TWO = 0.999
ADAM_EPS = 1e-08
DECAY_RATE = 0.5
ADAM_STEPS = 10.0
GROUP = 8
PAIR = 4
EXTRA = 8
ROOT_HALF = math.sqrt(0.5)


def up(n, m):
    return (n + m - 1) // m * m


def dot(a, b, ca=1, cb=0):
    return lax.dot_general(a, b, (((ca,), (cb,)), ((), ())), preferred_element_type=F32)


def tiles(n, w):
    return [(a, min(w, n - a)) for a in range(0, n, w)]


def params(flops=0, nbytes=0):
    return dict(
        compiler_params=pltpu.CompilerParams(vmem_limit_bytes=58 << 20),
        cost_estimate=pl.CostEstimate(flops=flops, bytes_accessed=nbytes, transcendentals=0),
    )


def weave(ms, vs):
    k = 0
    for a, f in enumerate(ms):
        f()
        while k * len(ms) < len(vs) * (a + 1):
            vs[k]()
            k += 1
    for f in vs[k:]:
        f()


def norm_rows(x):
    c = x - jnp.mean(x, axis=-1, keepdims=True)
    r = lax.rsqrt(jnp.mean(c * c, axis=-1, keepdims=True) + EPS_LN)
    return c * r, r


def gelu_pair(u):
    phi = 0.5 + 0.5 * lax.erf(u * ROOT_HALF)
    e = jnp.exp2((-0.5 * math.log2(math.e)) * (u * u))
    return u * phi, phi + (u * (1.0 / math.sqrt(2.0 * math.pi))) * e


def full(a):
    return pl.BlockSpec(a.shape, lambda *_: (0,) * len(a.shape))


def whole(*shape):
    return pl.BlockSpec(shape, lambda *_: (0,) * len(shape))


def spread(src, dst, seq):
    for t, n in tiles(seq, 20):
        x = src[t : t + n].astype(F32).reshape(n * GROUP, src.shape[2])
        for c in range(dst.shape[0]):
            dst[c, t * GROUP : (t + n) * GROUP, :] = x[:, c * 128 : (c + 1) * 128]


def image(ref, i, t, n):
    return jnp.concatenate(
        [ref[c, pl.ds(t * GROUP + i, n, stride=GROUP), :] for c in range(ref.shape[0])], axis=1
    )


def token(ref, t, tp):
    return jnp.concatenate(
        [ref[c, pl.ds(t, GROUP, stride=tp), :] for c in range(ref.shape[0])], axis=1
    )


def tokens(ref, t, tp):
    return jnp.stack([token(ref, t, tp), token(ref, t + 1, tp)])


def pack_body(r, wq_ref, vec_ref, b_ref, w1_ref, w2_ref, wp_ref, a_ref, b_out, sm):
    FF = w1_ref.shape[1]
    a_ref[0:r, :] = wq_ref[...].astype(BF)
    sm[...] = jnp.zeros_like(sm)
    sm[0 : vec_ref.shape[0], 0 : vec_ref.shape[1]] = vec_ref[...]
    sm[6:7, 0 : b_ref.shape[1]] = b_ref[...]
    a_ref[r : r + EXTRA, :] = sm[...].astype(BF)
    b_out[:, 0:FF] = w1_ref[...].astype(BF)
    b_out[:, FF : 2 * FF] = w2_ref[...].astype(BF)
    b_out[:, 2 * FF :] = wp_ref[...].astype(BF)


def pack(wq, vec, b, w1, w2t, wp):
    r, W3 = wq.shape
    FF = w1.shape[1]
    C = 2 * FF + wp.shape[1]
    return pl.pallas_call(
        partial(pack_body, r),
        out_shape=[jax.ShapeDtypeStruct((r + EXTRA, W3), BF), jax.ShapeDtypeStruct((r, C), BF)],
        scratch_shapes=[pltpu.VMEM((EXTRA, W3), F32)],
        name="pack",
        **params(),
    )(wq, vec, b, w1, w2t, wp)


def norm_body(SEQ, D, x_ref, xh_ref, r_ref, xs):
    j = pl.program_id(1)

    @pl.when(j == 0)
    def _():
        spread(x_ref, xs, SEQ)

    for i in range(PAIR):
        for t, n in tiles(SEQ, 48):
            xh, r = norm_rows(image(xs, j * PAIR + i, t, n))
            xh_ref[i, t : t + n, :] = xh
            r_ref[i, t : t + n, :] = jnp.broadcast_to(r, (n, 128))


def norm(x):
    SEQ, N, D = x.shape
    SP = up(SEQ, 16)
    tok = pl.BlockSpec((SEQ, GROUP, D), lambda g, j: (0, g, 0))
    img = lambda d: pl.BlockSpec((PAIR, SP, d), lambda g, j: (g * (GROUP // PAIR) + j, 0, 0))
    return pl.pallas_call(
        partial(norm_body, SEQ, D),
        grid=(N // GROUP, GROUP // PAIR),
        in_specs=[tok],
        out_specs=[img(D), img(128)],
        out_shape=[jax.ShapeDtypeStruct((N, SP, d), F32) for d in (D, 128)],
        scratch_shapes=[pltpu.VMEM((D // 128, up(SEQ, 8) * GROUP, 128), F32)],
        name="norm",
        **params(8 * 10**9, 15 * 10**6),
    )(x)


def attend_body(SEQ, SP, TP, D, np_, me_ref, xh_ref, *refs):
    H = D // HEAD_DIM
    g = pl.program_id(0)
    j = pl.program_id(1)
    if np_:
        pieces, refs = refs[:np_], refs[np_:]
        qkv_ref, o_ref, p_ref, a_ref, w_ref, vec_ref, c1_ref, sm = refs[:8]
        refs = refs[8:]
    else:
        w_ref, vec_ref, qkv_ref, o_ref, p_ref, a_ref = refs[:6]
        refs = refs[6:]
    os_, a_scr, s0, s1 = refs

    @pl.when((g == 0) & (j == 0))
    def _():
        for ref in (a_scr, os_):
            ref[...] = jnp.zeros_like(ref)
        if np_:
            r = pieces[0].shape[0] - EXTRA
            for k in range(np_):
                s = me_ref[0] ^ k
                w_ref[pl.ds(pl.multiple_of(s * r, 16), r), :] = pieces[k][0:r, :]
                sm[s] = pieces[k][r : r + EXTRA, 0 : sm.shape[2]].astype(F32)
            nb = c1_ref.shape[1] // np_
            vec_ref[...] = jnp.concatenate([sm[s, :, 0:r] for s in range(np_)], axis=1)
            c1_ref[...] = jnp.broadcast_to(
                jnp.concatenate([sm[s, 6:7, 0:nb] for s in range(np_)], axis=1), c1_ref.shape
            )

    gain = vec_ref[0:1, :]
    shift = vec_ref[1:2, :]
    ss = (s0, s1)
    st = {}
    S8 = SEQ // 16 * 16

    def ln(i, t, n):
        y = (xh_ref[i, t : t + n, :] * gain + shift).astype(BF)
        a_scr[i * SP + t : i * SP + t + n, :] = y
        a_ref[i, t : t + n, :] = y

    def qkv(t, c, w):
        y = dot(a_scr[...], w_ref[:, t * D + c : t * D + c + w])
        if t == 0:
            y = y * (HEAD_DIM**-0.5)
        qkv_ref[:, :, t * D + c : t * D + c + w] = y.astype(BF).reshape(PAIR, SP, w)

    def score(u):
        i, h = divmod(u, H)
        lo = h * HEAD_DIM
        ss[u % 2][...] = dot(
            qkv_ref[i, :, D + lo : D + lo + HEAD_DIM], qkv_ref[i, :, lo : lo + HEAD_DIM], 1, 1
        )

    def tile(ref, t, n):
        x = ref[t : t + n, :]
        if t + n > SEQ:
            x = jnp.where(lax.broadcasted_iota(jnp.int32, (n, 1), 0) < SEQ - t, x, -1e30)
        return x

    def vmax(u, t, n):
        m = jnp.max(tile(ss[u % 2], t, n).reshape(n // 8, 8, SP), axis=0)
        st[u] = m if t == 0 else jnp.maximum(st[u], m)
        if t + n >= SEQ:
            st[u] = jnp.max(st[u], axis=0, keepdims=True)

    def vexp(u, t, n):
        p = jnp.exp(tile(ss[u % 2], t, n) - st[u])
        ss[u % 2][t : t + n, :] = p
        total = jnp.sum(p.reshape(n // 8, 8, SP), axis=0)
        k = ("l", u)
        st[k] = total if t == 0 else st[k] + total
        if t + n >= SEQ:
            total = jnp.sum(st[k], axis=0, keepdims=True)
            st[k] = 1.0 / total

    def vnorm(u, t, n):
        i, h = divmod(u, H)
        p_ref[i, h, t : t + n, :] = (ss[u % 2][t : t + n, :] * st[("l", u)]).astype(BF)

    def mix(u):
        i, h = divmod(u, H)
        lo = 2 * D + h * HEAD_DIM
        y = dot(p_ref[i, h], qkv_ref[i, :, lo : lo + HEAD_DIM], 0, 0)
        if h % 2 == 0:
            st["o"] = y
        else:
            y = jnp.concatenate([st["o"], y], axis=1)
            os_[h // 2, pl.ds(pl.multiple_of((j * PAIR + i) * TP, 8), SEQ), :] = y[:SEQ]

    for i in range(PAIR):
        for t, n in tiles(SEQ, 48):
            ln(i, t, n)
    c0 = min(256, D)
    hb = c0 // HEAD_DIM
    for t in range(3):
        qkv(t, 0, c0)
    rest = [partial(qkv, t, c, w) for c, w in tiles(D, 256)[1:] for t in range(3)]
    srows = tiles(S8, 64) + ([(S8, SP - S8)] if S8 < SEQ else [])
    order = [i * H + h for i in range(PAIR) for h in range(hb)]
    order += [i * H + h for i in range(PAIR) for h in range(hb, H)]
    nu = len(order)
    score(order[0])
    for k, u in enumerate(order):
        ms = rest[k : k + 1]
        if k >= 1:
            ms.append(partial(mix, order[k - 1]))
        if k + 1 < nu:
            ms.append(partial(score, order[k + 1]))
        vs = [partial(f, u, t, n) for f in (vmax, vexp, vnorm) for t, n in srows]
        weave(ms, vs)
    nu = order[-1] + 1
    mix(nu - 1)
    for i in range(PAIR):
        a_ref[i, SEQ:SP, :] = jnp.zeros((SP - SEQ, D), BF)

    @pl.when(j == pl.num_programs(1) - 1)
    def _():
        for t in range(0, TP, 2):
            o_ref[t : t + 2] = tokens(os_, t, TP).astype(BF)


def attend(me, xh, pieces, w, vec, FF, SEQ, TP):
    N, SP, D = xh.shape
    W3 = 3 * D
    np_ = len(pieces)
    tok = lambda t: pl.BlockSpec((t, GROUP, D), lambda g, j, *_: (0, g, 0))
    img = lambda r, d: pl.BlockSpec((PAIR, r, d), lambda g, j, *_: (g * (GROUP // PAIR) + j, 0, 0))
    probs = pl.BlockSpec((PAIR, D // HEAD_DIM, SP, SP), lambda g, j, *_: (g * (GROUP // PAIR) + j, 0, 0, 0))
    v = pltpu.VMEM
    s = jax.ShapeDtypeStruct
    ins = list(pieces) if np_ else [w, vec]
    out_specs = [img(SP, W3), tok(TP), probs, img(SP, D)]
    out_shape = [s((N, SP, W3), BF), s((TP, N, D), BF), s((N, D // HEAD_DIM, SP, SP), BF), s((N, SP, D), BF)]
    scratch = [v((D // 128, TP * GROUP, 128), F32), v((PAIR * SP, D), BF)]
    scratch += [v((SP, SP), F32)] * 2
    if np_:
        out_specs += [whole(D, W3), whole(8, D), whole(8, FF)]
        out_shape += [s((D, W3), BF), s((8, D), F32), s((8, FF), F32)]
        scratch = [v((np_, EXTRA, up(max(FF, D) // np_, 128)), F32)] + scratch
    return pl.pallas_call(
        partial(attend_body, SEQ, SP, TP, D, np_),
        grid_spec=pltpu.PrefetchScalarGridSpec(
            num_scalar_prefetch=1,
            grid=(N // GROUP, GROUP // PAIR),
            in_specs=[img(SP, D)] + [full(a) for a in ins],
            out_specs=out_specs,
            scratch_shapes=scratch,
        ),
        out_shape=out_shape,
        name="attend",
        **params(20 * 10**9, 25 * 10**6),
    )(me, xh, *ins)


def feed_body(SEQ, D, FF, T, N, np_, me_ref, cnt_ref, x_ref, o_ref, cot_ref, c1_ref, vec_ref, *refs):
    s = pl.program_id(0)
    R = T * N
    RT = 2 * N
    HR = R // 2
    if np_:
        pieces, refs = refs[:np_], refs[np_:]
        out_ref, dx1_ref, do_ref, tc1_ref, tv_ref, snd_ref, keep_ref = refs[:7]
        wp_ref, w1_ref, w2t_ref, tp_ref, t1_ref, t2_ref = refs[7:13]
        refs = refs[13:]
    else:
        wp_ref, w1_ref, w2t_ref, out_ref, dx1_ref, do_ref, tc1_ref, tv_ref, tp_ref, t1_ref, t2_ref = refs[:11]
        refs = refs[11:]
    b_scr, bt_scr, dy_scr, dyt_scr, xh_scr, r_scr, x1_scr, u0, u1, d0, d1, g_scr, du_scr, y_scr, db_scr, dx_scr = refs

    @pl.when(s == 0)
    def _():
        for ref in (tp_ref, t1_ref, t2_ref, tc1_ref, tv_ref, bt_scr, dyt_scr, g_scr, du_scr):
            ref[...] = jnp.zeros_like(ref)
        if np_:
            r = pieces[0].shape[0]
            for k in range(np_):
                at = pl.ds(pl.multiple_of((me_ref[0] ^ k) * r, 16), r)
                w1_ref[at, :] = pieces[k][:, 0:FF]
                w2t_ref[at, :] = pieces[k][:, FF : 2 * FF]
                wp_ref[at, :] = pieces[k][:, 2 * FF :]

    cp = vec_ref[2:3, :]
    g2 = vec_ref[3:4, :]
    e2 = vec_ref[4:5, :]
    c2 = vec_ref[5:6, :]
    io = lax.broadcasted_iota(jnp.int32, (RT, 1), 0)
    real = lax.rem(io, N) < cnt_ref[0]
    lim = SEQ * N - s * R
    acc = {}

    def rows(ref, r):
        return ref[r // N : r // N + 2].reshape(RT, D)

    def add(key, v):
        v = jnp.sum(v.reshape(v.shape[0] // 8, 8, v.shape[1]), axis=0)
        acc[key] = v if key not in acc else acc[key] + v

    def m_proj(h):
        x1_scr[h : h + HR, :] = dot(o_ref[h // N : (h + HR) // N].reshape(HR, D), wp_ref[...])

    def v_norm(r):
        inside = (io + r) < lim
        x = jnp.where(inside, rows(x_ref, r).astype(F32), 0.0)
        dy_scr[r : r + RT, :] = jnp.where(real & inside, rows(cot_ref, r), jnp.zeros((), BF))
        x1 = x + x1_scr[r : r + RT, :] + cp
        x1_scr[r : r + RT, :] = x1 + c2
        xh, rr = norm_rows(x1)
        xh_scr[r : r + RT, :] = xh
        r_scr[r : r + RT, :] = jnp.broadcast_to(rr, (RT, 128))
        b_scr[r : r + RT, :] = (xh * g2 + e2).astype(BF)

    cols = tiles(FF, 256)
    us = (u0, u1)
    ds = (d0, d1)

    def m_u(i, h, HR=HR):
        c, w = cols[i]
        us[i % 2][h : h + HR, :w] = dot(b_scr[h : h + HR, :], w1_ref[:, c : c + w]) + c1_ref[0:1, c : c + w]

    def m_d(i, h, HR=HR):
        c, w = cols[i]
        ds[i % 2][h : h + HR, :w] = dot(dy_scr[h : h + HR, :], w2t_ref[:, c : c + w])

    def v_gelu(i, r):
        c, w = cols[i]
        ga, dg = gelu_pair(us[i % 2][r : r + 16, :w])
        g_scr[r : r + 16, c : c + w] = ga.astype(BF)
        du = ds[i % 2][r : r + 16, :w] * dg
        du_scr[r : r + 16, c : c + w] = du.astype(BF)
        add(("c1", i), du)

    def m_t1(i):
        c, w = cols[i]
        t1_ref[:, c : c + w] += dot(bt_scr[...], du_scr[:, c : c + w])

    def m_t2(i):
        c, w = cols[i]
        t2_ref[:, c : c + w] += dot(dyt_scr[...], g_scr[:, c : c + w])

    def m_y(h, HR=HR):
        y_scr[h : h + HR, :] = dot(g_scr[h : h + HR, :], w2t_ref[...], 1, 1)

    def m_db(h, HR=HR):
        db_scr[h : h + HR, :] = dot(du_scr[h : h + HR, :], w1_ref[...], 1, 1)

    def v_out(r):
        y = x1_scr[r : r + RT, :] + y_scr[r : r + RT, :]
        out_ref[r // N : r // N + 2] = jnp.where(real, y, 0.0).astype(BF).reshape(2, N, D)

    def v_back(r):
        db = db_scr[r : r + RT, :]
        xh = xh_scr[r : r + RT, :]
        dyf = dy_scr[r : r + RT, :].astype(F32)
        dxh = db * g2
        mean1 = jnp.mean(dxh, axis=-1, keepdims=True)
        mean2 = jnp.mean(dxh * xh, axis=-1, keepdims=True)
        dx = dyf + r_scr[r : r + RT, 0:1] * (dxh - mean1 - xh * mean2)
        add("g2", db * xh)
        add("e2", db)
        add("c2", dyf)
        add("cp", dx)
        dx1_ref[r // N : r // N + 2] = dx.reshape(2, N, D)
        dx_scr[r : r + RT, :] = dx.astype(BF)

    def m_do(h):
        y = dot(dx_scr[h : h + HR, :], wp_ref[...], 1, 1)
        do_ref[h // N : (h + HR) // N] = y.astype(BF).reshape(HR // N, N, D)

    def m_tp():
        tp_ref[...] += dot(o_ref[...].reshape(R, D), dx_scr[...], 0, 0)

    first = list(range(0, HR, RT))
    second = list(range(HR, R, RT))
    last = len(cols) - 1
    def turn(dst, src):
        dst[...] = src[...].T

    m_proj(0)
    weave([partial(m_proj, HR), partial(m_t1, last)], [partial(v_norm, r) for r in first])
    weave([partial(m_t2, last), partial(m_u, 0, 0), partial(m_d, 0, 0)], [partial(v_norm, r) for r in second])
    weave([partial(m_u, 0, HR), partial(m_d, 0, HR)], [partial(turn, bt_scr, b_scr), partial(turn, dyt_scr, dy_scr)])
    for i in range(len(cols)):
        ms = []
        if i < last:
            ms += [partial(f, i + 1, 0, R) for f in (m_u, m_d)]
        if i >= 1:
            ms += [partial(m_t1, i - 1), partial(m_t2, i - 1)]
        weave(ms, [partial(v_gelu, i, r) for r in range(0, R, 16)])
        c, w = cols[i]
        tc1_ref[:, c : c + w] += acc[("c1", i)]
    m_db(0, R)
    weave([partial(m_y, 0, R)], [partial(v_back, r) for r in first + second])
    weave([partial(m_do, 0), partial(m_do, HR), m_tp], [partial(v_out, r) for r in first + second])
    for i, k in ((2, "cp"), (3, "g2"), (4, "e2"), (5, "c2")):
        tv_ref[i * 8 : i * 8 + 8, :] += acc[k]

    @pl.when(s == pl.num_programs(0) - 1)
    def _():
        m_t1(last)
        m_t2(last)
        if np_:
            r = D // np_
            for k in range(0, np_, 2):
                for ref, flip in ((keep_ref, 0), (snd_ref, 1)):
                    at = pl.ds(pl.multiple_of((me_ref[0] ^ (k + flip)) * r, 16), r)
                    ref[k // 2, :, 0:FF] = t1_ref[at, :].astype(ref.dtype)
                    ref[k // 2, :, FF : 2 * FF] = t2_ref[at, :].astype(ref.dtype)
                    ref[k // 2, :, 2 * FF :] = tp_ref[at, :].astype(ref.dtype)


def feed(me, cnt, x, o, cot, c1, vec, pieces, weights, T):
    SEQ, N, D = x.shape
    TP = o.shape[0]
    FF = c1.shape[1]
    np_ = len(pieces)
    R = T * N
    v = pltpu.VMEM
    s = jax.ShapeDtypeStruct
    blk = pl.BlockSpec((T, N, D), lambda i, *_: (i, 0, 0))
    ins = list(pieces) if np_ else list(weights)
    out_specs = [blk, blk, blk, whole(8, FF), whole(64, D)]
    out_shape = [s((SEQ, N, D), BF), s((TP, N, D), F32), s((TP, N, D), BF), s((8, FF), F32), s((64, D), F32)]
    scratch = []
    if np_:
        shape = (np_ // 2, D // np_, 2 * FF + D)
        out_specs += [whole(*shape)] * 2
        out_shape += [s(shape, BF), s(shape, F32)]
        scratch += [v((D, D), BF), v((D, FF), BF), v((D, FF), BF), v((D, D), F32), v((D, FF), F32), v((D, FF), F32)]
    else:
        out_specs += [whole(D, D), whole(D, FF), whole(D, FF)]
        out_shape += [s((D, D), F32), s((D, FF), F32), s((D, FF), F32)]
    scratch += [v((R, D), BF), v((D, R), BF), v((R, D), BF), v((D, R), BF), v((R, D), F32), v((R, 128), F32), v((R, D), F32)]
    scratch += [v((R, 256), F32)] * 4 + [v((R, FF), BF)] * 2 + [v((R, D), F32)] * 2 + [v((R, D), BF)]
    return pl.pallas_call(
        partial(feed_body, SEQ, D, FF, T, N, np_),
        grid_spec=pltpu.PrefetchScalarGridSpec(
            num_scalar_prefetch=2,
            grid=(TP // T,),
            in_specs=[blk, blk, blk, full(c1), full(vec)] + [full(a) for a in ins],
            out_specs=out_specs,
            scratch_shapes=scratch,
        ),
        out_shape=out_shape,
        name="feed",
        **params(45 * 10**9, 30 * 10**6),
    )(me, cnt, x, o, cot, c1, vec, *ins)


def back_body(SEQ, SP, TP, D, FF, np_, DEPS, me_ref, a_ref, xh_ref, r_ref, qkv_ref, p_ref, do_ref, dx1_ref, w_ref, vec_ref, tc1_ref, tv2_ref, *refs):
    gi_ref, refs = refs[DEPS], refs[DEPS + 1 :]
    if np_:
        snd_ref, keep_ref, tq_ref, sm = refs[:4]
        gv_ref, refs = refs[4], refs[5:]
    else:
        tq_ref, gv_ref, refs = refs[0], refs[1], refs[2:]
    dos, gs, dob, at_scr, d_scr, da_scr, tv_ref, e0, e1, q0, q1 = refs
    H = D // HEAD_DIM
    W3 = 3 * D
    g = pl.program_id(0)
    j = pl.program_id(1)

    @pl.when((g == 0) & (j == 0))
    def _():
        for ref in (d_scr, dob, tq_ref, tv_ref):
            ref[...] = jnp.zeros_like(ref)

    @pl.when(j == 0)
    def _():
        spread(do_ref, dos, SEQ)

    gain = vec_ref[0:1, :]
    es = (e0, e1)
    qq = (q0, q1)
    st = {}
    S8 = SEQ // 16 * 16

    def load(i, t, n):
        dob[i * SP + t : i * SP + t + n, :] = image(dos, j * PAIR + i, t, n).astype(BF)

    def part(i, h, t):
        lo = t * D + h * HEAD_DIM
        return qkv_ref[i, :, lo : lo + HEAD_DIM]

    def dpart(i, h):
        return dob[i * SP : (i + 1) * SP, h * HEAD_DIM : (h + 1) * HEAD_DIM]

    def dprob(u):
        i, h = divmod(u, H)
        es[u % 2][...] = dot(part(i, h, 2), dpart(i, h), 1, 1)

    def v_inner(u, t, n):
        x = p_ref[divmod(u, H) + (slice(t, t + n),)].astype(F32) * es[u % 2][t : t + n, :]
        x = jnp.sum(x.reshape(n // 8, 8, SP), axis=0)
        st[u] = x if t == 0 else st[u] + x
        if t + n >= SEQ:
            st[u] = jnp.sum(st[u], axis=0, keepdims=True)

    def v_ds(u, t, n):
        p = p_ref[divmod(u, H) + (slice(t, t + n),)].astype(F32)
        qq[u % 2][t : t + n, :] = (p * (es[u % 2][t : t + n, :] - st[u])).astype(BF)

    def put(u, t, y):
        i, h = divmod(u, H)
        if h % 2 == 0:
            st[("d", t)] = y
        else:
            y = jnp.concatenate([st[("d", t)], y], axis=0).T if t == 0 else jnp.concatenate([st[("d", t)], y], axis=1)
            y = y.astype(BF)
            lo = t * D + (h - 1) * HEAD_DIM
            d_scr[i * SP : i * SP + SEQ, lo : lo + 2 * HEAD_DIM] = y[:SEQ]

    def m_dv(u):
        put(u, 2, dot(p_ref[divmod(u, H)], dpart(*divmod(u, H))))

    def m_dk(u):
        i, h = divmod(u, H)
        put(u, 1, dot(qq[u % 2][...], part(i, h, 0)))

    def m_dq(u):
        i, h = divmod(u, H)
        put(u, 0, dot(part(i, h, 1), qq[u % 2][...], 0, 0) * (HEAD_DIM**-0.5))

    rows = tiles(SEQ, 48)
    srows = tiles(S8, 64) + ([(S8, SP - S8)] if S8 < SEQ else [])
    for t, n in rows:
        load(0, t, n)
    at_scr[...] = a_ref[...].reshape(PAIR * SP, D).T
    pre = [partial(load, i, t, n) for i in range(1, PAIR) for t, n in rows]
    nu = PAIR * H
    dprob(0)
    for k in range(nu):
        ms = []
        if k + 1 < nu:
            ms.append(partial(dprob, k + 1))
        ms.append(partial(m_dv, k))
        if k >= 1:
            ms += [partial(m_dq, k - 1), partial(m_dk, k - 1)]
        vs = [partial(f, k, t, n) for f in (v_inner, v_ds) for t, n in srows]
        vs += pre[k : k + 1]
        weave(ms, vs)
    m_dk(nu - 1)
    m_dq(nu - 1)
    acc = {}

    def m_da():
        da_scr[...] = dot(d_scr[...], w_ref[...], 1, 1)

    def m_tq(c, w):
        tq_ref[:, c : c + w] += dot(at_scr[...], d_scr[:, c : c + w])

    def add(key, v):
        f = v.shape[0] // 8 * 8
        if f:
            x = jnp.sum(v[:f].reshape(f // 8, 8, D), axis=0)
            acc[key] = x if key not in acc else acc[key] + x
        if f < v.shape[0]:
            x = jnp.sum(v[f:], axis=0, keepdims=True)
            key = key + "tail"
            acc[key] = x if key not in acc else acc[key] + x

    def v_back(i, t, n):
        at = slice(i * SP + t, i * SP + t + n)
        d = da_scr[at, :]
        xh = xh_ref[i, t : t + n, :]
        dxh = d * gain
        mean1 = jnp.mean(dxh, axis=-1, keepdims=True)
        mean2 = jnp.mean(dxh * xh, axis=-1, keepdims=True)
        y = r_ref[i, t : t + n, 0:1] * (dxh - mean1 - xh * mean2)
        for c in range(gs.shape[0]):
            gs[c, pl.ds(pl.multiple_of((j * PAIR + i) * TP + t, 8), n), :] = y[:, c * 128 : (c + 1) * 128]
        add("g", d * xh)
        add("e", d)

    cols = tiles(W3, 256)
    m_da()
    weave([partial(m_tq, c, w) for c, w in cols], [partial(v_back, i, t, n) for i in range(PAIR) for t, n in rows])
    tv_ref[0:8, :] += acc["g"]
    tv_ref[8:16, :] += acc["e"]
    if "gtail" in acc:
        tv_ref[0:1, :] += acc["gtail"]
        tv_ref[8:9, :] += acc["etail"]

    @pl.when(j == pl.num_programs(1) - 1)
    def _():
        for t in range(0, SEQ - 1, 2):
            gi_ref[t : t + 2] = (tokens(gs, t, TP) + dx1_ref[t : t + 2]).astype(BF)
        if SEQ % 2:
            gi_ref[SEQ - 1] = (token(gs, SEQ - 1, TP) + dx1_ref[SEQ - 1]).astype(BF)

    @pl.when((j == pl.num_programs(1) - 1) & (g == pl.num_programs(0) - 1))
    def _():
        for i in range(2):
            gv_ref[i : i + 1, :] = jnp.sum(tv_ref[8 * i : 8 * i + 8, :], axis=0, keepdims=True)
        for i in range(2, 6):
            gv_ref[i : i + 1, :] = jnp.sum(tv2_ref[8 * i : 8 * i + 8, :], axis=0, keepdims=True)
        if np_:
            r = D // np_
            nb = FF // np_
            sm[...] = jnp.zeros_like(sm)
            bias = jnp.sum(tc1_ref[...], axis=0, keepdims=True)
            for s in range(np_):
                sm[s, 0:6, 0:r] = gv_ref[0:6, s * r : (s + 1) * r]
                sm[s, 6:7, 0:nb] = bias[:, s * nb : (s + 1) * nb]
            wide = sm.shape[2]
            for k in range(0, np_, 2):
                for ref, flip in ((keep_ref, 0), (snd_ref, 1)):
                    s = me_ref[0] ^ (k + flip)
                    ref[k // 2, 0:r, :] = tq_ref[pl.ds(pl.multiple_of(s * r, 16), r), :].astype(ref.dtype)
                    ref[k // 2, r : r + EXTRA, 0:wide] = sm[s].astype(ref.dtype)
                    ref[k // 2, r : r + EXTRA, wide:] = jnp.zeros((EXTRA, W3 - wide), ref.dtype)


def back(me, a, xh, r, qkv, probs, do, dx1, w, vec, tc1, tv2, deps, SEQ, np_):
    N, SP, D = a.shape
    TP = do.shape[0]
    W3 = 3 * D
    FF = tc1.shape[1]
    R = PAIR * SP
    tok = lambda t: pl.BlockSpec((t, GROUP, D), lambda g, j, *_: (0, g, 0))
    img = lambda r, d: pl.BlockSpec((PAIR, r, d), lambda g, j, *_: (g * (GROUP // PAIR) + j, 0, 0))
    v = pltpu.VMEM
    s = jax.ShapeDtypeStruct
    prob = pl.BlockSpec((PAIR, D // HEAD_DIM, SP, SP), lambda g, j, *_: (g * (GROUP // PAIR) + j, 0, 0, 0))
    out_specs = [tok(SEQ)]
    out_shape = [s((SEQ, N, D), BF)]
    if np_:
        shape = (np_ // 2, D // np_ + EXTRA, W3)
        out_specs += [whole(*shape)] * 2
        out_shape += [s(shape, BF), s(shape, F32)]
        scratch = [v((D, W3), F32), v((np_, EXTRA, up(max(FF, D) // np_, 128)), F32), v((8, D), F32)]
    else:
        out_specs += [whole(D, W3), whole(8, D)]
        out_shape += [s((D, W3), F32), s((8, D), F32)]
        scratch = []
    scratch += [v((D // 128, TP * GROUP, 128), F32)] * 2
    scratch += [v((R, D), BF), v((D, R), BF), v((R, W3), BF), v((R, D), F32)]
    scratch += [v((16, D), F32)] + [v((SP, SP), F32)] * 2 + [v((SP, SP), BF)] * 2
    return pl.pallas_call(
        partial(back_body, SEQ, SP, TP, D, FF, np_, len(deps)),
        grid_spec=pltpu.PrefetchScalarGridSpec(
            num_scalar_prefetch=1,
            grid=(N // GROUP, GROUP // PAIR),
            in_specs=[img(SP, D), img(SP, D), img(SP, 128), img(SP, W3), prob, tok(TP), tok(TP)]
            + [full(w), full(vec), full(tc1), full(tv2)]
            + [pl.BlockSpec(memory_space=pl.ANY)] * len(deps),
            out_specs=out_specs,
            scratch_shapes=scratch,
        ),
        out_shape=out_shape,
        name="back",
        **params(40 * 10**9, 30 * 10**6),
    )(me, a, xh, r, qkv, probs, do, dx1, w, vec, tc1, tv2, *deps)


def adam_body(np_, count, slots, where, flag_ref, gid_ref, scale_ref, *refs):
    pieces, refs = refs[:np_], refs[np_:]
    weights, firsts, seconds, outs = refs[:count], refs[count : 2 * count], refs[2 * count : 3 * count], refs[3 * count :]
    for k, (p, row, col) in enumerate(where):
        r, c = weights[k].shape
        xs = [x[row : row + r, col : col + c].astype(F32) for x in pieces]
        grad = (xs[0] if len(xs) == 1 else (xs[0] + xs[1]) + (xs[2] + xs[3])) / slots
        flag = flag_ref[p].astype(F32)
        lr = scale_ref[gid_ref[p]]
        first = BETA_ONE * firsts[k][...] + (1.0 - BETA_ONE) * grad
        second = BETA_TWO * seconds[k][...] + (1.0 - BETA_TWO) * grad * grad
        direction = first / (1.0 - BETA_ONE**ADAM_STEPS) / (jnp.sqrt(second / (1.0 - BETA_TWO**ADAM_STEPS)) + ADAM_EPS)
        weight = weights[k][...]
        outs[k][...] = grad
        outs[count + k][...] = weight - LEARN_RATE * lr * (direction + DECAY_RATE * flag * weight)
        outs[2 * count + k][...] = first
        outs[3 * count + k][...] = second


def adam(flags, gids, scales, pieces, arrays, slots, where):
    smem = pl.BlockSpec(memory_space=pltpu.SMEM)
    vmem = pl.BlockSpec(memory_space=pltpu.VMEM)
    mine = [[xs[p] for p, _, _ in where] for xs in arrays]
    shapes = [jax.ShapeDtypeStruct(w.shape, F32) for w in mine[0]]
    return pl.pallas_call(
        partial(adam_body, len(pieces), len(where), slots, where),
        in_specs=[smem] * 3 + [vmem] * (len(pieces) + 3 * len(where)),
        out_specs=[vmem] * (4 * len(where)),
        out_shape=shapes * 4,
        name="adam",
        **params(10**9, 5 * 10**6),
    )(flags, gids, scales, *pieces, *mine[0], *mine[1], *mine[2])


def pairs(n, k):
    return [(i, i ^ k) for i in range(n)]


def touch_body(*refs):
    pass


def touch(dep, xs):
    spec = pl.BlockSpec(memory_space=pl.ANY)
    return pl.pallas_call(
        touch_body,
        in_specs=[spec] * (len(xs) + 1),
        out_specs=[spec] * len(xs),
        out_shape=[jax.ShapeDtypeStruct(x.shape, x.dtype) for x in xs],
        input_output_aliases={k: k for k in range(len(xs))},
        name="touch",
    )(*xs, dep)


def fetch(x, n):
    return [x] + [lax.ppermute(x, "fsdp", pairs(n, k)) for k in range(2, n, 2)]


def fetch_core(own, n):
    other = [lax.ppermute(x, "fsdp", pairs(n, 1)) for x in own]
    return [x for both in zip(own, other) for x in both]


def halve(snd, keep, n):
    h = keep + lax.ppermute(snd, "fsdp", pairs(n, 1)).astype(F32)
    return h[0], [h[k].astype(BF) for k in range(1, n // 2)]


def along_z(xs, n):
    return [lax.ppermute(x, "fsdp", pairs(n, 2 * k + 2)) for k, x in enumerate(xs)]


def finish(own, got, d):
    for piece in got:
        own = own + piece.astype(F32)
    b = own.astype(BF)
    return [b] + [lax.ppermute(b, "dp", pairs(d, k)) for k in range(1, d)]


def local(
    images, cotangent, counts,
    w_qkv, w_proj, w_fc1, w_fc2, b_fc1, vectors,
    m_qkv, m_proj, m_fc1, m_fc2, m_bias1, m_vectors,
    v_qkv, v_proj, v_fc1, v_fc2, v_bias1, v_vectors,
    decay_flags, group_ids, group_scales,
):
    n = lax.axis_size("fsdp")
    d = lax.axis_size("dp")
    N, SEQ, D = images.shape
    r = w_qkv.shape[0]
    FF = w_fc1.shape[1]
    T = 20
    TP = up(SEQ, T)
    direct = n in (2, 4, 8) and d == 4 and r % 16 == 0
    x = jnp.transpose(images, (1, 0, 2))
    cot = jnp.transpose(cotangent, (1, 0, 2))
    me = lax.axis_index("fsdp").astype(jnp.int32).reshape(1)
    rows = lambda b: b.reshape(1, -1)
    weights = [w_qkv, w_proj, w_fc1, w_fc2.T, rows(b_fc1), vectors]
    firsts = [m_qkv, m_proj, m_fc1, m_fc2.T, rows(m_bias1), m_vectors]
    seconds = [v_qkv, v_proj, v_fc1, v_fc2.T, rows(v_bias1), v_vectors]
    pack_a, pack_b = pack(weights[0], weights[5], weights[4], weights[2], weights[3], weights[1])
    xh, rf = norm(x)
    if direct:
        half_a = touch(rf, fetch(pack_a, n))
        pieces_a = fetch_core(half_a, n)
        half_b = fetch(touch(half_a[-1], [pack_b])[0], n)
        qkv, o, probs, a, wq, vec, c1 = attend(me, xh, pieces_a, None, None, FF, SEQ, TP)
        pieces_b = fetch_core(touch(vec, half_b), n)
        out, dx1, do, tc1, tv2, snd, keep = feed(me, counts, x, o, cot, c1, vec, pieces_b, (), T)
        own_b, sends = halve(snd, keep, n)
        got_b = along_z(sends, n)
        gi, snd, keep = back(me, a, xh, rf, qkv, probs, do, dx1, wq, vec, tc1, tv2, sends, SEQ, n)
        snd, *got_b = touch(vec, [snd, *got_b])
        own_a, sends = halve(snd, keep, n)
        got_a = along_z(sends, n)
        pb = finish(own_b, got_b, d)
        pa = finish(own_a, got_a, d)
    else:
        all_a = lax.all_gather(pack_a, "fsdp", axis=0, tiled=False)
        all_b = lax.all_gather(pack_b, "fsdp", axis=0, tiled=True)
        wq = all_a[:, :r].reshape(D, 3 * D)
        nb = FF // n
        vec = jnp.transpose(all_a[:, r : r + 8, :r], (1, 0, 2)).reshape(8, D).astype(F32)
        c1 = jnp.broadcast_to(all_a[:, r + 6, :nb].reshape(1, FF), (8, FF)).astype(F32)
        ws = (all_b[:, 2 * FF :], all_b[:, :FF], all_b[:, FF : 2 * FF])
        qkv, o, probs, a = attend(me, xh, (), wq, vec, FF, SEQ, TP)
        out, dx1, do, tc1, tv2, tp, t1, t2 = feed(me, counts, x, o, cot, c1, vec, (), ws, T)
        gi, tq, gv = back(me, a, xh, rf, qkv, probs, do, dx1, wq, vec, tc1, tv2, (), SEQ, 0)
        share = lambda g, axis: lax.psum(
            lax.psum_scatter(g, "fsdp", scatter_dimension=axis, tiled=True).astype(BF), "dp"
        ).astype(F32)
        pb = [share(jnp.concatenate([t1, t2, tp], axis=1), 0)]
        small = jnp.zeros((8, 3 * D), F32).at[:6, :r].set(share(gv[:6], 1))
        small = small.at[6, :nb].set(share(jnp.sum(tc1, axis=0), 0))
        pa = [jnp.concatenate([share(tq, 0), small], axis=0)]
    arrays = (weights, firsts, seconds)
    slots = float(N * n * d)
    where_a = ((0, 0, 0), (4, r + 6, 0), (5, r, 0))
    where_b = ((1, 0, 2 * FF), (2, 0, 0), (3, 0, FF))
    res = [None] * 24
    for pieces, where in ((pb, where_b), (pa, where_a)):
        got = adam(decay_flags, group_ids, group_scales, pieces, arrays, slots, where)
        for j in range(4):
            for k, (p, _, _) in enumerate(where):
                res[6 * j + p] = got[3 * j + k]
    for k in range(4):
        res[6 * k + 3] = res[6 * k + 3].T
        res[6 * k + 4] = res[6 * k + 4].reshape(-1)
    return (jnp.transpose(out, (1, 0, 2)), jnp.transpose(gi, (1, 0, 2)), *res)


def solution(mesh):
    P = PartitionSpec
    both = ("dp", "fsdp")
    six = (P("fsdp", None), P("fsdp", None), P("fsdp", None), P(None, "fsdp"), P("fsdp"), P(None, "fsdp"))
    data = (P(both, None, None), P(both, None, None))
    return jax.shard_map(
        local,
        mesh=mesh,
        in_specs=(*data, P(both), *six, *six, *six, P(), P(), P()),
        out_specs=(*data, *six, *six, *six, *six),
        check_vma=False,
    )
```

```python
import math
from functools import partial

import jax
import jax.numpy as jnp
from jax import lax
from jax.experimental import pallas as pl
from jax.experimental.pallas import tpu as pltpu
from jax.sharding import PartitionSpec

BF = jnp.bfloat16
F32 = jnp.float32
HEAD_DIM = 64
EPS_LN = 1e-06
LEARN_RATE = 0.2
BETA_ONE = 0.9
BETA_TWO = 0.999
ADAM_EPS = 1e-08
DECAY_RATE = 0.5
ADAM_STEPS = 10.0
GROUP = 8
PAIR = 4
EXTRA = 8
ROOT_HALF = math.sqrt(0.5)


def up(n, m):
    return (n + m - 1) // m * m


def dot(a, b, ca=1, cb=0):
    return lax.dot_general(a, b, (((ca,), (cb,)), ((), ())), preferred_element_type=F32)


def tiles(n, w):
    return [(a, min(w, n - a)) for a in range(0, n, w)]


def params(flops=0, nbytes=0):
    return dict(
        compiler_params=pltpu.CompilerParams(vmem_limit_bytes=58 << 20),
        cost_estimate=pl.CostEstimate(flops=flops, bytes_accessed=nbytes, transcendentals=0),
    )


def weave(ms, vs):
    k = 0
    for a, f in enumerate(ms):
        f()
        while k * len(ms) < len(vs) * (a + 1):
            vs[k]()
            k += 1
    for f in vs[k:]:
        f()


def norm_rows(x):
    c = x - jnp.mean(x, axis=-1, keepdims=True)
    r = lax.rsqrt(jnp.mean(c * c, axis=-1, keepdims=True) + EPS_LN)
    return c * r, r


def gelu_pair(u):
    phi = 0.5 + 0.5 * lax.erf(u * ROOT_HALF)
    e = jnp.exp2((-0.5 * math.log2(math.e)) * (u * u))
    return u * phi, phi + (u * (1.0 / math.sqrt(2.0 * math.pi))) * e


def full(a):
    return pl.BlockSpec(a.shape, lambda *_: (0,) * len(a.shape))


def whole(*shape):
    return pl.BlockSpec(shape, lambda *_: (0,) * len(shape))


def spread(src, dst, seq):
    for t, n in tiles(seq, 20):
        x = src[t : t + n].astype(F32).reshape(n * GROUP, src.shape[2])
        for c in range(dst.shape[0]):
            dst[c, t * GROUP : (t + n) * GROUP, :] = x[:, c * 128 : (c + 1) * 128]


def image(ref, i, t, n):
    return jnp.concatenate(
        [ref[c, pl.ds(t * GROUP + i, n, stride=GROUP), :] for c in range(ref.shape[0])], axis=1
    )


def token(ref, t, tp):
    return jnp.concatenate(
        [ref[c, pl.ds(t, GROUP, stride=tp), :] for c in range(ref.shape[0])], axis=1
    )


def tokens(ref, t, tp):
    return jnp.stack([token(ref, t, tp), token(ref, t + 1, tp)])


def pack_body(r, wq_ref, vec_ref, b_ref, w1_ref, w2_ref, wp_ref, a_ref, b_out, sm):
    FF = w1_ref.shape[1]
    a_ref[0:r, :] = wq_ref[...].astype(BF)
    sm[...] = jnp.zeros_like(sm)
    sm[0 : vec_ref.shape[0], 0 : vec_ref.shape[1]] = vec_ref[...]
    sm[6:7, 0 : b_ref.shape[1]] = b_ref[...]
    a_ref[r : r + EXTRA, :] = sm[...].astype(BF)
    b_out[:, 0:FF] = w1_ref[...].astype(BF)
    b_out[:, FF : 2 * FF] = w2_ref[...].astype(BF)
    b_out[:, 2 * FF :] = wp_ref[...].astype(BF)


def pack(wq, vec, b, w1, w2t, wp):
    r, W3 = wq.shape
    FF = w1.shape[1]
    C = 2 * FF + wp.shape[1]
    return pl.pallas_call(
        partial(pack_body, r),
        out_shape=[jax.ShapeDtypeStruct((r + EXTRA, W3), BF), jax.ShapeDtypeStruct((r, C), BF)],
        scratch_shapes=[pltpu.VMEM((EXTRA, W3), F32)],
        name="pack",
        **params(),
    )(wq, vec, b, w1, w2t, wp)


def norm_body(SEQ, D, x_ref, xh_ref, r_ref, xs):
    j = pl.program_id(1)

    @pl.when(j == 0)
    def _():
        spread(x_ref, xs, SEQ)

    for i in range(PAIR):
        for t, n in tiles(SEQ, 48):
            xh, r = norm_rows(image(xs, j * PAIR + i, t, n))
            xh_ref[i, t : t + n, :] = xh
            r_ref[i, t : t + n, :] = jnp.broadcast_to(r, (n, 128))


def norm(x):
    SEQ, N, D = x.shape
    SP = up(SEQ, 16)
    tok = pl.BlockSpec((SEQ, GROUP, D), lambda g, j: (0, g, 0))
    img = lambda d: pl.BlockSpec((PAIR, SP, d), lambda g, j: (g * (GROUP // PAIR) + j, 0, 0))
    return pl.pallas_call(
        partial(norm_body, SEQ, D),
        grid=(N // GROUP, GROUP // PAIR),
        in_specs=[tok],
        out_specs=[img(D), img(128)],
        out_shape=[jax.ShapeDtypeStruct((N, SP, d), F32) for d in (D, 128)],
        scratch_shapes=[pltpu.VMEM((D // 128, up(SEQ, 8) * GROUP, 128), F32)],
        name="norm",
        **params(8 * 10**9, 15 * 10**6),
    )(x)


def attend_body(SEQ, SP, TP, D, np_, me_ref, xh_ref, *refs):
    H = D // HEAD_DIM
    g = pl.program_id(0)
    j = pl.program_id(1)
    if np_:
        pieces, refs = refs[:np_], refs[np_:]
        qkv_ref, o_ref, p_ref, a_ref, w_ref, vec_ref, c1_ref, sm = refs[:8]
        refs = refs[8:]
    else:
        w_ref, vec_ref, qkv_ref, o_ref, p_ref, a_ref = refs[:6]
        refs = refs[6:]
    os_, a_scr, s0, s1 = refs

    @pl.when((g == 0) & (j == 0))
    def _():
        for ref in (a_scr, os_):
            ref[...] = jnp.zeros_like(ref)
        if np_:
            r = pieces[0].shape[0] - EXTRA
            for k in range(np_):
                s = me_ref[0] ^ k
                w_ref[pl.ds(pl.multiple_of(s * r, 16), r), :] = pieces[k][0:r, :]
                sm[s] = pieces[k][r : r + EXTRA, 0 : sm.shape[2]].astype(F32)
            nb = c1_ref.shape[1] // np_
            vec_ref[...] = jnp.concatenate([sm[s, :, 0:r] for s in range(np_)], axis=1)
            c1_ref[...] = jnp.broadcast_to(
                jnp.concatenate([sm[s, 6:7, 0:nb] for s in range(np_)], axis=1), c1_ref.shape
            )

    gain = vec_ref[0:1, :]
    shift = vec_ref[1:2, :]
    ss = (s0, s1)
    st = {}
    S8 = SEQ // 16 * 16

    def ln(i, t, n):
        y = (xh_ref[i, t : t + n, :] * gain + shift).astype(BF)
        a_scr[i * SP + t : i * SP + t + n, :] = y
        a_ref[i, t : t + n, :] = y

    def qkv(t, c, w):
        y = dot(a_scr[...], w_ref[:, t * D + c : t * D + c + w])
        if t == 0:
            y = y * (HEAD_DIM**-0.5)
        qkv_ref[:, :, t * D + c : t * D + c + w] = y.astype(BF).reshape(PAIR, SP, w)

    def score(u):
        i, h = divmod(u, H)
        lo = h * HEAD_DIM
        ss[u % 2][...] = dot(
            qkv_ref[i, :, D + lo : D + lo + HEAD_DIM], qkv_ref[i, :, lo : lo + HEAD_DIM], 1, 1
        )

    def tile(ref, t, n):
        x = ref[t : t + n, :]
        if t + n > SEQ:
            x = jnp.where(lax.broadcasted_iota(jnp.int32, (n, 1), 0) < SEQ - t, x, -1e30)
        return x

    def vmax(u, t, n):
        m = jnp.max(tile(ss[u % 2], t, n).reshape(n // 8, 8, SP), axis=0)
        st[u] = m if t == 0 else jnp.maximum(st[u], m)
        if t + n >= SEQ:
            st[u] = jnp.max(st[u], axis=0, keepdims=True)

    def vexp(u, t, n):
        p = jnp.exp(tile(ss[u % 2], t, n) - st[u])
        ss[u % 2][t : t + n, :] = p
        total = jnp.sum(p.reshape(n // 8, 8, SP), axis=0)
        k = ("l", u)
        st[k] = total if t == 0 else st[k] + total
        if t + n >= SEQ:
            total = jnp.sum(st[k], axis=0, keepdims=True)
            st[k] = 1.0 / total

    def vnorm(u, t, n):
        i, h = divmod(u, H)
        p_ref[i, h, t : t + n, :] = (ss[u % 2][t : t + n, :] * st[("l", u)]).astype(BF)

    def mix(u):
        i, h = divmod(u, H)
        lo = 2 * D + h * HEAD_DIM
        y = dot(p_ref[i, h], qkv_ref[i, :, lo : lo + HEAD_DIM], 0, 0)
        if h % 2 == 0:
            st["o"] = y
        else:
            y = jnp.concatenate([st["o"], y], axis=1)
            os_[h // 2, pl.ds(pl.multiple_of((j * PAIR + i) * TP, 8), SEQ), :] = y[:SEQ]

    for i in range(PAIR):
        for t, n in tiles(SEQ, 48):
            ln(i, t, n)
    c0 = min(256, D)
    hb = c0 // HEAD_DIM
    for t in range(3):
        qkv(t, 0, c0)
    rest = [partial(qkv, t, c, w) for c, w in tiles(D, 256)[1:] for t in range(3)]
    srows = tiles(S8, 64) + ([(S8, SP - S8)] if S8 < SEQ else [])
    order = [i * H + h for i in range(PAIR) for h in range(hb)]
    order += [i * H + h for i in range(PAIR) for h in range(hb, H)]
    nu = len(order)
    score(order[0])
    for k, u in enumerate(order):
        ms = rest[k : k + 1]
        if k >= 1:
            ms.append(partial(mix, order[k - 1]))
        if k + 1 < nu:
            ms.append(partial(score, order[k + 1]))
        vs = [partial(f, u, t, n) for f in (vmax, vexp, vnorm) for t, n in srows]
        weave(ms, vs)
    nu = order[-1] + 1
    mix(nu - 1)
    for i in range(PAIR):
        a_ref[i, SEQ:SP, :] = jnp.zeros((SP - SEQ, D), BF)

    @pl.when(j == pl.num_programs(1) - 1)
    def _():
        for t in range(0, TP, 2):
            o_ref[t : t + 2] = tokens(os_, t, TP).astype(BF)


def attend(me, xh, pieces, w, vec, FF, SEQ, TP):
    N, SP, D = xh.shape
    W3 = 3 * D
    np_ = len(pieces)
    tok = lambda t: pl.BlockSpec((t, GROUP, D), lambda g, j, *_: (0, g, 0))
    img = lambda r, d: pl.BlockSpec((PAIR, r, d), lambda g, j, *_: (g * (GROUP // PAIR) + j, 0, 0))
    probs = pl.BlockSpec((PAIR, D // HEAD_DIM, SP, SP), lambda g, j, *_: (g * (GROUP // PAIR) + j, 0, 0, 0))
    v = pltpu.VMEM
    s = jax.ShapeDtypeStruct
    ins = list(pieces) if np_ else [w, vec]
    out_specs = [img(SP, W3), tok(TP), probs, img(SP, D)]
    out_shape = [s((N, SP, W3), BF), s((TP, N, D), BF), s((N, D // HEAD_DIM, SP, SP), BF), s((N, SP, D), BF)]
    scratch = [v((D // 128, TP * GROUP, 128), F32), v((PAIR * SP, D), BF)]
    scratch += [v((SP, SP), F32)] * 2
    if np_:
        out_specs += [whole(D, W3), whole(8, D), whole(8, FF)]
        out_shape += [s((D, W3), BF), s((8, D), F32), s((8, FF), F32)]
        scratch = [v((np_, EXTRA, up(max(FF, D) // np_, 128)), F32)] + scratch
    return pl.pallas_call(
        partial(attend_body, SEQ, SP, TP, D, np_),
        grid_spec=pltpu.PrefetchScalarGridSpec(
            num_scalar_prefetch=1,
            grid=(N // GROUP, GROUP // PAIR),
            in_specs=[img(SP, D)] + [full(a) for a in ins],
            out_specs=out_specs,
            scratch_shapes=scratch,
        ),
        out_shape=out_shape,
        name="attend",
        **params(20 * 10**9, 25 * 10**6),
    )(me, xh, *ins)


def feed_body(SEQ, D, FF, T, N, np_, me_ref, cnt_ref, x_ref, o_ref, cot_ref, c1_ref, vec_ref, *refs):
    s = pl.program_id(0)
    R = T * N
    RT = 2 * N
    HR = R // 2
    if np_:
        pieces, refs = refs[:np_], refs[np_:]
        out_ref, dx1_ref, do_ref, tc1_ref, tv_ref, snd_ref, keep_ref = refs[:7]
        wp_ref, w1_ref, w2t_ref, tp_ref, t1_ref, t2_ref = refs[7:13]
        refs = refs[13:]
    else:
        wp_ref, w1_ref, w2t_ref, out_ref, dx1_ref, do_ref, tc1_ref, tv_ref, tp_ref, t1_ref, t2_ref = refs[:11]
        refs = refs[11:]
    b_scr, bt_scr, dy_scr, dyt_scr, xh_scr, r_scr, x1_scr, u0, u1, d0, d1, g_scr, du_scr, y_scr, db_scr, dx_scr = refs

    @pl.when(s == 0)
    def _():
        for ref in (tp_ref, t1_ref, t2_ref, tc1_ref, tv_ref, bt_scr, dyt_scr, g_scr, du_scr):
            ref[...] = jnp.zeros_like(ref)
        if np_:
            r = pieces[0].shape[0]
            for k in range(np_):
                at = pl.ds(pl.multiple_of((me_ref[0] ^ k) * r, 16), r)
                w1_ref[at, :] = pieces[k][:, 0:FF]
                w2t_ref[at, :] = pieces[k][:, FF : 2 * FF]
                wp_ref[at, :] = pieces[k][:, 2 * FF :]

    cp = vec_ref[2:3, :]
    g2 = vec_ref[3:4, :]
    e2 = vec_ref[4:5, :]
    c2 = vec_ref[5:6, :]
    io = lax.broadcasted_iota(jnp.int32, (RT, 1), 0)
    real = lax.rem(io, N) < cnt_ref[0]
    lim = SEQ * N - s * R
    acc = {}

    def rows(ref, r):
        return ref[r // N : r // N + 2].reshape(RT, D)

    def add(key, v):
        v = jnp.sum(v.reshape(v.shape[0] // 8, 8, v.shape[1]), axis=0)
        acc[key] = v if key not in acc else acc[key] + v

    def m_proj(h):
        x1_scr[h : h + HR, :] = dot(o_ref[h // N : (h + HR) // N].reshape(HR, D), wp_ref[...])

    def v_norm(r):
        inside = (io + r) < lim
        x = jnp.where(inside, rows(x_ref, r).astype(F32), 0.0)
        dy_scr[r : r + RT, :] = jnp.where(real & inside, rows(cot_ref, r), jnp.zeros((), BF))
        x1 = x + x1_scr[r : r + RT, :] + cp
        x1_scr[r : r + RT, :] = x1 + c2
        xh, rr = norm_rows(x1)
        xh_scr[r : r + RT, :] = xh
        r_scr[r : r + RT, :] = jnp.broadcast_to(rr, (RT, 128))
        b_scr[r : r + RT, :] = (xh * g2 + e2).astype(BF)

    cols = tiles(FF, 256)
    us = (u0, u1)
    ds = (d0, d1)

    def m_u(i, h, HR=HR):
        c, w = cols[i]
        us[i % 2][h : h + HR, :w] = dot(b_scr[h : h + HR, :], w1_ref[:, c : c + w]) + c1_ref[0:1, c : c + w]

    def m_d(i, h, HR=HR):
        c, w = cols[i]
        ds[i % 2][h : h + HR, :w] = dot(dy_scr[h : h + HR, :], w2t_ref[:, c : c + w])

    def v_gelu(i, r):
        c, w = cols[i]
        ga, dg = gelu_pair(us[i % 2][r : r + 16, :w])
        g_scr[r : r + 16, c : c + w] = ga.astype(BF)
        du = ds[i % 2][r : r + 16, :w] * dg
        du_scr[r : r + 16, c : c + w] = du.astype(BF)
        add(("c1", i), du)

    def m_t1(i):
        c, w = cols[i]
        t1_ref[:, c : c + w] += dot(bt_scr[...], du_scr[:, c : c + w])

    def m_t2(i):
        c, w = cols[i]
        t2_ref[:, c : c + w] += dot(dyt_scr[...], g_scr[:, c : c + w])

    def m_y(h, HR=HR):
        y_scr[h : h + HR, :] = dot(g_scr[h : h + HR, :], w2t_ref[...], 1, 1)

    def m_db(h, HR=HR):
        db_scr[h : h + HR, :] = dot(du_scr[h : h + HR, :], w1_ref[...], 1, 1)

    def v_out(r):
        y = x1_scr[r : r + RT, :] + y_scr[r : r + RT, :]
        out_ref[r // N : r // N + 2] = jnp.where(real, y, 0.0).astype(BF).reshape(2, N, D)

    def v_back(r):
        db = db_scr[r : r + RT, :]
        xh = xh_scr[r : r + RT, :]
        dyf = dy_scr[r : r + RT, :].astype(F32)
        dxh = db * g2
        mean1 = jnp.mean(dxh, axis=-1, keepdims=True)
        mean2 = jnp.mean(dxh * xh, axis=-1, keepdims=True)
        dx = dyf + r_scr[r : r + RT, 0:1] * (dxh - mean1 - xh * mean2)
        add("g2", db * xh)
        add("e2", db)
        add("c2", dyf)
        add("cp", dx)
        dx1_ref[r // N : r // N + 2] = dx.reshape(2, N, D)
        dx_scr[r : r + RT, :] = dx.astype(BF)

    def m_do(h):
        y = dot(dx_scr[h : h + HR, :], wp_ref[...], 1, 1)
        do_ref[h // N : (h + HR) // N] = y.astype(BF).reshape(HR // N, N, D)

    def m_tp():
        tp_ref[...] += dot(o_ref[...].reshape(R, D), dx_scr[...], 0, 0)

    first = list(range(0, HR, RT))
    second = list(range(HR, R, RT))
    last = len(cols) - 1
    def turn(dst, src):
        dst[...] = src[...].T

    m_proj(0)
    weave([partial(m_proj, HR), partial(m_t1, last)], [partial(v_norm, r) for r in first])
    weave([partial(m_t2, last), partial(m_u, 0, 0), partial(m_d, 0, 0)], [partial(v_norm, r) for r in second])
    weave([partial(m_u, 0, HR), partial(m_d, 0, HR)], [partial(turn, bt_scr, b_scr), partial(turn, dyt_scr, dy_scr)])
    for i in range(len(cols)):
        ms = []
        if i < last:
            ms += [partial(f, i + 1, 0, R) for f in (m_u, m_d)]
        if i >= 1:
            ms += [partial(m_t1, i - 1), partial(m_t2, i - 1)]
        weave(ms, [partial(v_gelu, i, r) for r in range(0, R, 16)])
        c, w = cols[i]
        tc1_ref[:, c : c + w] += acc[("c1", i)]
    m_db(0, R)
    weave([partial(m_y, 0, R)], [partial(v_back, r) for r in first + second])
    weave([partial(m_do, 0), partial(m_do, HR), m_tp], [partial(v_out, r) for r in first + second])
    for i, k in ((2, "cp"), (3, "g2"), (4, "e2"), (5, "c2")):
        tv_ref[i * 8 : i * 8 + 8, :] += acc[k]

    @pl.when(s == pl.num_programs(0) - 1)
    def _():
        m_t1(last)
        m_t2(last)
        if np_:
            r = D // np_
            for k in range(0, np_, 2):
                for ref, flip in ((keep_ref, 0), (snd_ref, 1)):
                    at = pl.ds(pl.multiple_of((me_ref[0] ^ (k + flip)) * r, 16), r)
                    ref[k // 2, :, 0:FF] = t1_ref[at, :].astype(ref.dtype)
                    ref[k // 2, :, FF : 2 * FF] = t2_ref[at, :].astype(ref.dtype)
                    ref[k // 2, :, 2 * FF :] = tp_ref[at, :].astype(ref.dtype)


def feed(me, cnt, x, o, cot, c1, vec, pieces, weights, T):
    SEQ, N, D = x.shape
    TP = o.shape[0]
    FF = c1.shape[1]
    np_ = len(pieces)
    R = T * N
    v = pltpu.VMEM
    s = jax.ShapeDtypeStruct
    blk = pl.BlockSpec((T, N, D), lambda i, *_: (i, 0, 0))
    ins = list(pieces) if np_ else list(weights)
    out_specs = [blk, blk, blk, whole(8, FF), whole(64, D)]
    out_shape = [s((SEQ, N, D), BF), s((TP, N, D), F32), s((TP, N, D), BF), s((8, FF), F32), s((64, D), F32)]
    scratch = []
    if np_:
        shape = (np_ // 2, D // np_, 2 * FF + D)
        out_specs += [whole(*shape)] * 2
        out_shape += [s(shape, BF)] * 2
        scratch += [v((D, D), BF), v((D, FF), BF), v((D, FF), BF), v((D, D), F32), v((D, FF), F32), v((D, FF), F32)]
    else:
        out_specs += [whole(D, D), whole(D, FF), whole(D, FF)]
        out_shape += [s((D, D), F32), s((D, FF), F32), s((D, FF), F32)]
    scratch += [v((R, D), BF), v((D, R), BF), v((R, D), BF), v((D, R), BF), v((R, D), F32), v((R, 128), F32), v((R, D), F32)]
    scratch += [v((R, 256), F32)] * 4 + [v((R, FF), BF)] * 2 + [v((R, D), F32)] * 2 + [v((R, D), BF)]
    return pl.pallas_call(
        partial(feed_body, SEQ, D, FF, T, N, np_),
        grid_spec=pltpu.PrefetchScalarGridSpec(
            num_scalar_prefetch=2,
            grid=(TP // T,),
            in_specs=[blk, blk, blk, full(c1), full(vec)] + [full(a) for a in ins],
            out_specs=out_specs,
            scratch_shapes=scratch,
        ),
        out_shape=out_shape,
        name="feed",
        **params(45 * 10**9, 30 * 10**6),
    )(me, cnt, x, o, cot, c1, vec, *ins)


def back_body(SEQ, SP, TP, D, FF, np_, DEPS, me_ref, a_ref, xh_ref, r_ref, qkv_ref, p_ref, do_ref, dx1_ref, w_ref, vec_ref, tc1_ref, tv2_ref, *refs):
    gi_ref, refs = refs[DEPS], refs[DEPS + 1 :]
    if np_:
        snd_ref, keep_ref, tq_ref, sm = refs[:4]
        gv_ref, refs = refs[4], refs[5:]
    else:
        tq_ref, gv_ref, refs = refs[0], refs[1], refs[2:]
    dos, gs, dob, at_scr, d_scr, da_scr, tv_ref, e0, e1, q0, q1 = refs
    H = D // HEAD_DIM
    W3 = 3 * D
    g = pl.program_id(0)
    j = pl.program_id(1)

    @pl.when((g == 0) & (j == 0))
    def _():
        for ref in (d_scr, dob, tq_ref, tv_ref):
            ref[...] = jnp.zeros_like(ref)

    @pl.when(j == 0)
    def _():
        spread(do_ref, dos, SEQ)

    gain = vec_ref[0:1, :]
    es = (e0, e1)
    qq = (q0, q1)
    st = {}
    S8 = SEQ // 16 * 16

    def load(i, t, n):
        dob[i * SP + t : i * SP + t + n, :] = image(dos, j * PAIR + i, t, n).astype(BF)

    def part(i, h, t):
        lo = t * D + h * HEAD_DIM
        return qkv_ref[i, :, lo : lo + HEAD_DIM]

    def dpart(i, h):
        return dob[i * SP : (i + 1) * SP, h * HEAD_DIM : (h + 1) * HEAD_DIM]

    def dprob(u):
        i, h = divmod(u, H)
        es[u % 2][...] = dot(part(i, h, 2), dpart(i, h), 1, 1)

    def v_inner(u, t, n):
        x = p_ref[divmod(u, H) + (slice(t, t + n),)].astype(F32) * es[u % 2][t : t + n, :]
        x = jnp.sum(x.reshape(n // 8, 8, SP), axis=0)
        st[u] = x if t == 0 else st[u] + x
        if t + n >= SEQ:
            st[u] = jnp.sum(st[u], axis=0, keepdims=True)

    def v_ds(u, t, n):
        p = p_ref[divmod(u, H) + (slice(t, t + n),)].astype(F32)
        qq[u % 2][t : t + n, :] = (p * (es[u % 2][t : t + n, :] - st[u])).astype(BF)

    def put(u, t, y):
        i, h = divmod(u, H)
        if h % 2 == 0:
            st[("d", t)] = y
        else:
            y = jnp.concatenate([st[("d", t)], y], axis=0).T if t == 0 else jnp.concatenate([st[("d", t)], y], axis=1)
            y = y.astype(BF)
            lo = t * D + (h - 1) * HEAD_DIM
            d_scr[i * SP : i * SP + SEQ, lo : lo + 2 * HEAD_DIM] = y[:SEQ]

    def m_dv(u):
        put(u, 2, dot(p_ref[divmod(u, H)], dpart(*divmod(u, H))))

    def m_dk(u):
        i, h = divmod(u, H)
        put(u, 1, dot(qq[u % 2][...], part(i, h, 0)))

    def m_dq(u):
        i, h = divmod(u, H)
        put(u, 0, dot(part(i, h, 1), qq[u % 2][...], 0, 0) * (HEAD_DIM**-0.5))

    rows = tiles(SEQ, 48)
    srows = tiles(S8, 64) + ([(S8, SP - S8)] if S8 < SEQ else [])
    for t, n in rows:
        load(0, t, n)
    at_scr[...] = a_ref[...].reshape(PAIR * SP, D).T
    pre = [partial(load, i, t, n) for i in range(1, PAIR) for t, n in rows]
    nu = PAIR * H
    dprob(0)
    for k in range(nu):
        ms = []
        if k + 1 < nu:
            ms.append(partial(dprob, k + 1))
        ms.append(partial(m_dv, k))
        if k >= 1:
            ms += [partial(m_dq, k - 1), partial(m_dk, k - 1)]
        vs = [partial(f, k, t, n) for f in (v_inner, v_ds) for t, n in srows]
        vs += pre[k : k + 1]
        weave(ms, vs)
    m_dk(nu - 1)
    m_dq(nu - 1)
    acc = {}

    def m_da():
        da_scr[...] = dot(d_scr[...], w_ref[...], 1, 1)

    def m_tq(c, w):
        tq_ref[:, c : c + w] += dot(at_scr[...], d_scr[:, c : c + w])

    def add(key, v):
        f = v.shape[0] // 8 * 8
        if f:
            x = jnp.sum(v[:f].reshape(f // 8, 8, D), axis=0)
            acc[key] = x if key not in acc else acc[key] + x
        if f < v.shape[0]:
            x = jnp.sum(v[f:], axis=0, keepdims=True)
            key = key + "tail"
            acc[key] = x if key not in acc else acc[key] + x

    def v_back(i, t, n):
        at = slice(i * SP + t, i * SP + t + n)
        d = da_scr[at, :]
        xh = xh_ref[i, t : t + n, :]
        dxh = d * gain
        mean1 = jnp.mean(dxh, axis=-1, keepdims=True)
        mean2 = jnp.mean(dxh * xh, axis=-1, keepdims=True)
        y = r_ref[i, t : t + n, 0:1] * (dxh - mean1 - xh * mean2)
        for c in range(gs.shape[0]):
            gs[c, pl.ds(pl.multiple_of((j * PAIR + i) * TP + t, 8), n), :] = y[:, c * 128 : (c + 1) * 128]
        add("g", d * xh)
        add("e", d)

    cols = tiles(W3, 256)
    m_da()
    weave([partial(m_tq, c, w) for c, w in cols], [partial(v_back, i, t, n) for i in range(PAIR) for t, n in rows])
    tv_ref[0:8, :] += acc["g"]
    tv_ref[8:16, :] += acc["e"]
    if "gtail" in acc:
        tv_ref[0:1, :] += acc["gtail"]
        tv_ref[8:9, :] += acc["etail"]

    @pl.when(j == pl.num_programs(1) - 1)
    def _():
        for t in range(0, SEQ - 1, 2):
            gi_ref[t : t + 2] = (tokens(gs, t, TP) + dx1_ref[t : t + 2]).astype(BF)
        if SEQ % 2:
            gi_ref[SEQ - 1] = (token(gs, SEQ - 1, TP) + dx1_ref[SEQ - 1]).astype(BF)

    @pl.when((j == pl.num_programs(1) - 1) & (g == pl.num_programs(0) - 1))
    def _():
        for i in range(2):
            gv_ref[i : i + 1, :] = jnp.sum(tv_ref[8 * i : 8 * i + 8, :], axis=0, keepdims=True)
        for i in range(2, 6):
            gv_ref[i : i + 1, :] = jnp.sum(tv2_ref[8 * i : 8 * i + 8, :], axis=0, keepdims=True)
        if np_:
            r = D // np_
            nb = FF // np_
            sm[...] = jnp.zeros_like(sm)
            bias = jnp.sum(tc1_ref[...], axis=0, keepdims=True)
            for s in range(np_):
                sm[s, 0:6, 0:r] = gv_ref[0:6, s * r : (s + 1) * r]
                sm[s, 6:7, 0:nb] = bias[:, s * nb : (s + 1) * nb]
            wide = sm.shape[2]
            for k in range(0, np_, 2):
                for ref, flip in ((keep_ref, 0), (snd_ref, 1)):
                    s = me_ref[0] ^ (k + flip)
                    ref[k // 2, 0:r, :] = tq_ref[pl.ds(pl.multiple_of(s * r, 16), r), :].astype(ref.dtype)
                    ref[k // 2, r : r + EXTRA, 0:wide] = sm[s].astype(ref.dtype)
                    ref[k // 2, r : r + EXTRA, wide:] = jnp.zeros((EXTRA, W3 - wide), ref.dtype)


def back(me, a, xh, r, qkv, probs, do, dx1, w, vec, tc1, tv2, deps, SEQ, np_):
    N, SP, D = a.shape
    TP = do.shape[0]
    W3 = 3 * D
    FF = tc1.shape[1]
    R = PAIR * SP
    tok = lambda t: pl.BlockSpec((t, GROUP, D), lambda g, j, *_: (0, g, 0))
    img = lambda r, d: pl.BlockSpec((PAIR, r, d), lambda g, j, *_: (g * (GROUP // PAIR) + j, 0, 0))
    v = pltpu.VMEM
    s = jax.ShapeDtypeStruct
    prob = pl.BlockSpec((PAIR, D // HEAD_DIM, SP, SP), lambda g, j, *_: (g * (GROUP // PAIR) + j, 0, 0, 0))
    out_specs = [tok(SEQ)]
    out_shape = [s((SEQ, N, D), BF)]
    if np_:
        shape = (np_ // 2, D // np_ + EXTRA, W3)
        out_specs += [whole(*shape)] * 2
        out_shape += [s(shape, BF)] * 2
        scratch = [v((D, W3), F32), v((np_, EXTRA, up(max(FF, D) // np_, 128)), F32), v((8, D), F32)]
    else:
        out_specs += [whole(D, W3), whole(8, D)]
        out_shape += [s((D, W3), F32), s((8, D), F32)]
        scratch = []
    scratch += [v((D // 128, TP * GROUP, 128), F32)] * 2
    scratch += [v((R, D), BF), v((D, R), BF), v((R, W3), BF), v((R, D), F32)]
    scratch += [v((16, D), F32)] + [v((SP, SP), F32)] * 2 + [v((SP, SP), BF)] * 2
    return pl.pallas_call(
        partial(back_body, SEQ, SP, TP, D, FF, np_, len(deps)),
        grid_spec=pltpu.PrefetchScalarGridSpec(
            num_scalar_prefetch=1,
            grid=(N // GROUP, GROUP // PAIR),
            in_specs=[img(SP, D), img(SP, D), img(SP, 128), img(SP, W3), prob, tok(TP), tok(TP)]
            + [full(w), full(vec), full(tc1), full(tv2)]
            + [pl.BlockSpec(memory_space=pl.ANY)] * len(deps),
            out_specs=out_specs,
            scratch_shapes=scratch,
        ),
        out_shape=out_shape,
        name="back",
        **params(40 * 10**9, 30 * 10**6),
    )(me, a, xh, r, qkv, probs, do, dx1, w, vec, tc1, tv2, *deps)


def adam_body(np_, count, slots, where, flag_ref, gid_ref, scale_ref, *refs):
    pieces, refs = refs[:np_], refs[np_:]
    weights, firsts, seconds, outs = refs[:count], refs[count : 2 * count], refs[2 * count : 3 * count], refs[3 * count :]
    for k, (p, row, col) in enumerate(where):
        r, c = weights[k].shape
        xs = [x[row : row + r, col : col + c].astype(F32) for x in pieces]
        grad = (xs[0] if len(xs) == 1 else (xs[0] + xs[1]) + (xs[2] + xs[3])) / slots
        flag = flag_ref[p].astype(F32)
        lr = scale_ref[gid_ref[p]]
        first = BETA_ONE * firsts[k][...] + (1.0 - BETA_ONE) * grad
        second = BETA_TWO * seconds[k][...] + (1.0 - BETA_TWO) * grad * grad
        direction = first / (1.0 - BETA_ONE**ADAM_STEPS) / (jnp.sqrt(second / (1.0 - BETA_TWO**ADAM_STEPS)) + ADAM_EPS)
        weight = weights[k][...]
        outs[k][...] = grad
        outs[count + k][...] = weight - LEARN_RATE * lr * (direction + DECAY_RATE * flag * weight)
        outs[2 * count + k][...] = first
        outs[3 * count + k][...] = second


def adam(flags, gids, scales, pieces, arrays, slots, where):
    smem = pl.BlockSpec(memory_space=pltpu.SMEM)
    vmem = pl.BlockSpec(memory_space=pltpu.VMEM)
    mine = [[xs[p] for p, _, _ in where] for xs in arrays]
    shapes = [jax.ShapeDtypeStruct(w.shape, F32) for w in mine[0]]
    return pl.pallas_call(
        partial(adam_body, len(pieces), len(where), slots, where),
        in_specs=[smem] * 3 + [vmem] * (len(pieces) + 3 * len(where)),
        out_specs=[vmem] * (4 * len(where)),
        out_shape=shapes * 4,
        name="adam",
        **params(10**9, 5 * 10**6),
    )(flags, gids, scales, *pieces, *mine[0], *mine[1], *mine[2])


def pairs(n, k):
    return [(i, i ^ k) for i in range(n)]


def touch_body(*refs):
    pass


def touch(dep, xs):
    spec = pl.BlockSpec(memory_space=pl.ANY)
    return pl.pallas_call(
        touch_body,
        in_specs=[spec] * (len(xs) + 1),
        out_specs=[spec] * len(xs),
        out_shape=[jax.ShapeDtypeStruct(x.shape, x.dtype) for x in xs],
        input_output_aliases={k: k for k in range(len(xs))},
        name="touch",
    )(*xs, dep)


def fetch(x, n):
    return [x] + [lax.ppermute(x, "fsdp", pairs(n, k)) for k in range(2, n, 2)]


def fetch_core(own, n):
    other = [lax.ppermute(x, "fsdp", pairs(n, 1)) for x in own]
    return [x for both in zip(own, other) for x in both]


def halve(snd, keep, n):
    h = keep.astype(F32) + lax.ppermute(snd, "fsdp", pairs(n, 1)).astype(F32)
    return h[0], [h[k].astype(BF) for k in range(1, n // 2)]


def along_z(xs, n):
    return [lax.ppermute(x, "fsdp", pairs(n, 2 * k + 2)) for k, x in enumerate(xs)]


def finish(own, got, d):
    for piece in got:
        own = own + piece.astype(F32)
    b = own.astype(BF)
    return [b] + [lax.ppermute(b, "dp", pairs(d, k)) for k in range(1, d)]


def local(
    images, cotangent, counts,
    w_qkv, w_proj, w_fc1, w_fc2, b_fc1, vectors,
    m_qkv, m_proj, m_fc1, m_fc2, m_bias1, m_vectors,
    v_qkv, v_proj, v_fc1, v_fc2, v_bias1, v_vectors,
    decay_flags, group_ids, group_scales,
):
    n = lax.axis_size("fsdp")
    d = lax.axis_size("dp")
    N, SEQ, D = images.shape
    r = w_qkv.shape[0]
    FF = w_fc1.shape[1]
    T = 20
    TP = up(SEQ, T)
    direct = n in (2, 4, 8) and d == 4 and r % 16 == 0
    x = jnp.transpose(images, (1, 0, 2))
    cot = jnp.transpose(cotangent, (1, 0, 2))
    me = lax.axis_index("fsdp").astype(jnp.int32).reshape(1)
    rows = lambda b: b.reshape(1, -1)
    weights = [w_qkv, w_proj, w_fc1, w_fc2.T, rows(b_fc1), vectors]
    firsts = [m_qkv, m_proj, m_fc1, m_fc2.T, rows(m_bias1), m_vectors]
    seconds = [v_qkv, v_proj, v_fc1, v_fc2.T, rows(v_bias1), v_vectors]
    pack_a, pack_b = pack(weights[0], weights[5], weights[4], weights[2], weights[3], weights[1])
    xh, rf = norm(x)
    if direct:
        half_a = touch(rf, fetch(pack_a, n))
        pieces_a = fetch_core(half_a, n)
        half_b = fetch(touch(half_a[-1], [pack_b])[0], n)
        qkv, o, probs, a, wq, vec, c1 = attend(me, xh, pieces_a, None, None, FF, SEQ, TP)
        pieces_b = fetch_core(touch(vec, half_b), n)
        out, dx1, do, tc1, tv2, snd, keep = feed(me, counts, x, o, cot, c1, vec, pieces_b, (), T)
        own_b, sends = halve(snd, keep, n)
        got_b = along_z(sends, n)
        gi, snd, keep = back(me, a, xh, rf, qkv, probs, do, dx1, wq, vec, tc1, tv2, sends, SEQ, n)
        snd, *got_b = touch(vec, [snd, *got_b])
        own_a, sends = halve(snd, keep, n)
        got_a = along_z(sends, n)
        pb = finish(own_b, got_b, d)
        pa = finish(own_a, got_a, d)
    else:
        all_a = lax.all_gather(pack_a, "fsdp", axis=0, tiled=False)
        all_b = lax.all_gather(pack_b, "fsdp", axis=0, tiled=True)
        wq = all_a[:, :r].reshape(D, 3 * D)
        nb = FF // n
        vec = jnp.transpose(all_a[:, r : r + 8, :r], (1, 0, 2)).reshape(8, D).astype(F32)
        c1 = jnp.broadcast_to(all_a[:, r + 6, :nb].reshape(1, FF), (8, FF)).astype(F32)
        ws = (all_b[:, 2 * FF :], all_b[:, :FF], all_b[:, FF : 2 * FF])
        qkv, o, probs, a = attend(me, xh, (), wq, vec, FF, SEQ, TP)
        out, dx1, do, tc1, tv2, tp, t1, t2 = feed(me, counts, x, o, cot, c1, vec, (), ws, T)
        gi, tq, gv = back(me, a, xh, rf, qkv, probs, do, dx1, wq, vec, tc1, tv2, (), SEQ, 0)
        share = lambda g, axis: lax.psum(
            lax.psum_scatter(g, "fsdp", scatter_dimension=axis, tiled=True).astype(BF), "dp"
        ).astype(F32)
        pb = [share(jnp.concatenate([t1, t2, tp], axis=1), 0)]
        small = jnp.zeros((8, 3 * D), F32).at[:6, :r].set(share(gv[:6], 1))
        small = small.at[6, :nb].set(share(jnp.sum(tc1, axis=0), 0))
        pa = [jnp.concatenate([share(tq, 0), small], axis=0)]
    arrays = (weights, firsts, seconds)
    slots = float(N * n * d)
    where_a = ((0, 0, 0), (4, r + 6, 0), (5, r, 0))
    where_b = ((1, 0, 2 * FF), (2, 0, 0), (3, 0, FF))
    res = [None] * 24
    for pieces, where in ((pb, where_b), (pa, where_a)):
        got = adam(decay_flags, group_ids, group_scales, pieces, arrays, slots, where)
        for j in range(4):
            for k, (p, _, _) in enumerate(where):
                res[6 * j + p] = got[3 * j + k]
    for k in range(4):
        res[6 * k + 3] = res[6 * k + 3].T
        res[6 * k + 4] = res[6 * k + 4].reshape(-1)
    return (jnp.transpose(out, (1, 0, 2)), jnp.transpose(gi, (1, 0, 2)), *res)


def solution(mesh):
    P = PartitionSpec
    both = ("dp", "fsdp")
    six = (P("fsdp", None), P("fsdp", None), P("fsdp", None), P(None, "fsdp"), P("fsdp"), P(None, "fsdp"))
    data = (P(both, None, None), P(both, None, None))
    return jax.shard_map(
        local,
        mesh=mesh,
        in_specs=(*data, P(both), *six, *six, *six, P(), P(), P()),
        out_specs=(*data, *six, *six, *six, *six),
        check_vma=False,
    )
```
